32 devices in a mesh: energy: 4 (over y, x), momentum: 2 (over core), phonon: 4 (over z).
Axes of the slice: x: 2, y: 2, z: 4, core: 2. Of those that a mesh axis runs over, the one named last changes fastest.
Arguments:
- g_less: bfloat16 [8, 2, 2, 144, 2176], P('energy', 'momentum', None, None, 'phonon'), may hold values from -6 to 6
- g_great: bfloat16 [8, 2, 2, 144, 2176], P('energy', 'momentum', None, None, 'phonon'), may hold values from -6 to 6
- d_less: float32 [64, 2, 9, 17, 128], P(('energy', 'momentum', 'phonon')), may hold values from -2 to 2
- d_ret: bfloat16 [64, 2, 384, 384], P(('energy', 'momentum', 'phonon')), may hold values from -0.21875 to 0.21875
- neighbours: int32 [17, 128], replicated, may hold values from 0 to 127
- bond_dirs: float32 [3, 17, 128], replicated, may hold values from -4 to 4
- energy_offset: int32 [64], replicated, may hold values from 1 to 4
- momentum_offset: int32 [64], replicated, may hold values from 0 to 1
- absorb: float32 [64], replicated, may hold values from 0.1 to 0.9
Outputs:
- self_energy: bfloat16 [8, 2, 2, 144, 2176], P('energy', 'momentum', None, None, 'phonon')
- d_next: bfloat16 [64, 2, 384, 384], P(('energy', 'momentum', 'phonon'))
The draws below stay inside these ranges and needn't reach their ends.
Inputs may be any that keep to these rules, and one draw needn't show every extreme that they name: `neighbours`: atoms of the window.
All inputs are finite; a program needn't handle non-finite values.
Results may differ from the reference program's by a relative error of at most 0.008.
Values may be sent and summed in bfloat16 or wider, within the bound.
No kernel may reach another device: no remote copies, remote signals or barrier semaphores. Data moves between devices by JAX's collectives and lax.ppermute only.
A program may use at most 128 MiB of HBM per device.

```python
import math
import jax
import jax.numpy as jnp
from jax import lax

A = 128
NB = 17
ORB = 12
REACH = 4
NE = 8
NK = 2
MODES = 64
ORDER = 384


def set_ends(result, stream_key, low, high):
    place = [jax.random.randint(jax.random.fold_in(stream_key, axis), (), 0, length) for axis, length in enumerate(result.shape)]
    widest = result.shape.index(max(result.shape))
    beside = place[:widest] + [(place[widest] + 1) % result.shape[widest]] + place[widest + 1:]
    return result.at[tuple(place)].set(low).at[tuple(beside)].set(high)


def shard_levels(rng, shape, cuts, low, largest):
    loudness = 1.0
    for dim, parts in cuts:
        steps = jax.random.uniform(jax.random.fold_in(jax.random.fold_in(rng, 6), dim), (parts,), jnp.float32, low / len(cuts), largest / len(cuts))
        loudness = loudness * jnp.repeat(jnp.exp(steps), shape[dim] // parts).reshape((-1,) + (1,) * (len(shape) - 1 - dim))
    return loudness


def gaussian(key, dims, deviation, most, cuts=(), held_as=jnp.bfloat16):
    loudness = shard_levels(key, dims, cuts, -0.22, 0.18) if cuts else 1.0
    values = jax.random.normal(key, dims, jnp.float32) * deviation * loudness
    return jnp.minimum(jnp.maximum(values, -most), most).astype(held_as)


def setup_inputs(seed: int = 0) -> dict:
    splits = jax.random.split(jax.random.key(seed), 10)
    return {
        "g_less": gaussian(splits[0], (NE, NK, 2, ORB * ORB, A * NB), 1.0, 6.0, ((0, 4), (1, 2), (4, 4))),
        "g_great": gaussian(splits[1], (NE, NK, 2, ORB * ORB, A * NB), 1.0, 6.0, ((0, 4), (1, 2), (4, 4))),
        "d_less": gaussian(splits[2], (MODES, 2, 9, NB, A), (MODES ** -0.5), 2.0, ((0, 32),), jnp.float32),
        "d_ret": gaussian(splits[3], (MODES, 2, ORDER, ORDER), (2 * ORDER) ** -0.5, 0.21875, ((0, 32),)),
        "neighbours": set_ends(jax.random.randint(splits[4], (NB, A), 0, A), jax.random.fold_in(splits[4], 1), 0, A - 1).astype(jnp.int32),
        "bond_dirs": gaussian(splits[5], (3, NB, A), 0.6, 4.0, (), jnp.float32),
        "energy_offset": set_ends(jax.random.randint(splits[6], (MODES,), 1, REACH + 1), jax.random.fold_in(splits[6], 1), 1, REACH).astype(jnp.int32),
        "momentum_offset": set_ends(jax.random.randint(splits[7], (MODES,), 0, NK), jax.random.fold_in(splits[7], 1), 0, NK - 1).astype(jnp.int32),
        "absorb": jnp.clip(jnp.exp(jax.random.uniform(splits[8], (MODES,), jnp.float32, math.log(0.1), math.log(0.9))), 0.1, 0.9),
    }


HIGH = lax.Precision.HIGHEST


def complex_scale(weight, block):
    real_w = weight[0]
    imag_w = weight[1]
    real_b = block[:, :, 0].astype(jnp.float32)
    imag_b = block[:, :, 1].astype(jnp.float32)
    return jnp.stack([real_w * real_b - imag_w * imag_b, real_w * imag_b + imag_w * real_b], axis=2)


def reference(g_less, g_great, d_less, d_ret, neighbours, bond_dirs, energy_offset, momentum_offset, absorb):
    classes = REACH * NK
    entries = ORB * ORB
    pair_cube = bond_dirs[:, None] * bond_dirs[None, :]
    pair = pair_cube.reshape(9, NB, A)
    coupling = jnp.sum(d_less * pair[None, None], axis=2)
    label = (energy_offset - 1) * NK + momentum_offset
    table = (label[:, None] == jnp.arange(classes, dtype=jnp.int32)[None, :]).astype(jnp.float32)
    flat = coupling.reshape(MODES, -1)
    emitted = jnp.dot(table.T, flat, precision=HIGH).reshape(classes, 2, NB, A).transpose(3, 0, 1, 2)
    absorbed = jnp.dot((table * absorb[:, None]).T, flat, precision=HIGH).reshape(classes, 2, NB, A).transpose(3, 0, 1, 2)
    lesser = g_less.reshape(NE, NK, 2, entries, A, NB).transpose(4, 0, 1, 2, 3, 5)
    greater = g_great.reshape(NE, NK, 2, entries, A, NB).transpose(4, 0, 1, 2, 3, 5)
    scale = float(NE * NK * ORB * ORB) ** -0.5
    zero_pad = ((0, 0), (0, 0), (0, 0), (0, 0))

    def per_atom(items):
        low_blocks, high_blocks, emit_atom, soak_atom = items
        low_padded = jnp.pad(low_blocks, ((REACH, REACH),) + zero_pad)
        high_padded = jnp.pad(high_blocks, ((REACH, 0),) + zero_pad)
        total = jnp.zeros(low_blocks.shape, jnp.float32)
        low_real = low_blocks[:, :, 0].astype(jnp.float32)
        low_imag = low_blocks[:, :, 1].astype(jnp.float32)
        polar_list = []
        for energy_step in range(1, REACH + 1):
            for moment_step in range(NK):
                index = (energy_step - 1) * NK + moment_step
                below = jnp.roll(low_padded[REACH - energy_step: REACH - energy_step + NE], moment_step, axis=1)
                above = jnp.roll(low_padded[REACH + energy_step: REACH + energy_step + NE], -moment_step, axis=1)
                total = total + complex_scale(emit_atom[index], below) + complex_scale(soak_atom[index], above)
                earlier = jnp.roll(high_padded[REACH - energy_step: REACH - energy_step + NE], moment_step, axis=1)
                high_real = earlier[:, :, 0].astype(jnp.float32)
                high_imag = earlier[:, :, 1].astype(jnp.float32)
                real_sum = jnp.sum(low_real * high_real + low_imag * high_imag, axis=(0, 1, 2))
                imag_sum = jnp.sum(low_imag * high_real - low_real * high_imag, axis=(0, 1, 2))
                polar_list.append(jnp.stack([real_sum, imag_sum], axis=1) * scale)
        return total.astype(jnp.bfloat16), jnp.stack(polar_list)

    sigma_atoms, polar_atoms = lax.map(per_atom, (lesser, greater, emitted, absorbed))
    self_energy = sigma_atoms.transpose(1, 2, 3, 4, 0, 5).reshape(NE, NK, 2, entries, A * NB)
    polar_modes = jnp.einsum('mc,acnz->manz', table, polar_atoms, precision=HIGH)
    link = (neighbours[:, :, None] == jnp.arange(A, dtype=jnp.int32)[None, None, :]).astype(jnp.float32)

    def per_mode(items):
        polar_one, ret_one = items
        dense_list = []
        for part in range(2):
            weighted = pair_cube * polar_one[:, :, part].T[None, None]
            dense = jnp.einsum('ijna,nab->iajb', weighted, link, precision=HIGH).reshape(ORDER, ORDER)
            dense_list.append(dense.astype(jnp.bfloat16))
        dense_re, dense_im = dense_list
        ret_re, ret_im = ret_one[0], ret_one[1]
        half_re = (jnp.dot(dense_re, ret_re.T, preferred_element_type=jnp.float32)
                   + jnp.dot(dense_im, ret_im.T, preferred_element_type=jnp.float32)).astype(jnp.bfloat16)
        half_im = (jnp.dot(dense_im, ret_re.T, preferred_element_type=jnp.float32)
                   - jnp.dot(dense_re, ret_im.T, preferred_element_type=jnp.float32)).astype(jnp.bfloat16)
        next_re = jnp.dot(ret_re, half_re, preferred_element_type=jnp.float32) - jnp.dot(ret_im, half_im, preferred_element_type=jnp.float32)
        next_im = jnp.dot(ret_re, half_im, preferred_element_type=jnp.float32) + jnp.dot(ret_im, half_re, preferred_element_type=jnp.float32)
        return jnp.stack([next_re, next_im]).astype(jnp.bfloat16)

    d_next = lax.map(per_mode, (polar_modes, d_ret))
    return self_energy, d_next
```

```python
import functools

import jax
import jax.numpy as jnp
import numpy as np
from jax import lax
from jax.experimental import pallas as pl
from jax.experimental.pallas import tpu as pltpu
from jax.sharding import PartitionSpec as P

ORB = 12
REACH = 4
LANES = 128


HIGH = lax.Precision.HIGHEST


def shifted_2(block, axis, distance):
    devices = range(lax.axis_size(axis))
    route = [(i - distance, i) for i in devices if i - distance in devices]
    return lax.ppermute(block, axis, route)


def scaled_blocks(weights, blocks):
    real_w = weights[None, :, :, 0, None, :]
    imag_w = weights[None, :, :, 1, None, :]
    real_b = blocks[:, None, :, 0].astype(jnp.float32)
    imag_b = blocks[:, None, :, 1].astype(jnp.float32)
    real_part = jnp.sum(real_w * real_b - imag_w * imag_b, axis=2)
    imag_part = jnp.sum(real_w * imag_b + imag_w * real_b, axis=2)
    return jnp.stack([real_part, imag_part], axis=2)


def inner_sums(local_blocks, shifted):
    local_real = local_blocks[:, :, 0].astype(jnp.float32)[:, :, None]
    local_imag = local_blocks[:, :, 1].astype(jnp.float32)[:, :, None]
    other_real = shifted[:, :, 0].astype(jnp.float32)[:, None]
    other_imag = shifted[:, :, 1].astype(jnp.float32)[:, None]
    real_sum = jnp.sum(local_real * other_real + local_imag * other_imag, axis=(0, 3))
    imag_sum = jnp.sum(local_imag * other_real - local_real * other_imag, axis=(0, 3))
    return jnp.stack([real_sum, imag_sum], axis=2)


def times_adjoint(left, right):
    return jnp.einsum("mab,mcb->mac", left, right, preferred_element_type=jnp.float32)


def times_plain(left, right):
    return jnp.einsum("mab,mbc->mac", left, right, preferred_element_type=jnp.float32)


def general(
    g_less, g_great, d_less, d_ret, neighbours, bond_dirs, energy_offset, momentum_offset, absorb
):
    energies = g_less.shape[0]
    momenta_here = g_less.shape[1]
    local_width = g_less.shape[4]
    bonds = d_less.shape[3]
    whole_atoms = d_less.shape[4]
    atom_share = local_width // bonds
    all_momenta = momenta_here * lax.axis_size("momentum")
    all_energies = energies * lax.axis_size("energy")
    modes_here = d_less.shape[0]
    order = d_ret.shape[2]
    classes = REACH * all_momenta
    energy_rank = lax.axis_index("energy")
    momentum_rank = lax.axis_index("momentum")
    phonon_rank = lax.axis_index("phonon")
    span = -(-REACH // energies)
    lower_steps = list(range(span, 0, -1))
    both_steps = lower_steps + list(range(-1, -span - 1, -1))
    label = (energy_offset - 1) * all_momenta + momentum_offset
    table = (label[:, None] == jnp.arange(classes, dtype=jnp.int32)[None, :]).astype(jnp.float32)
    soaked = table * absorb[:, None]
    pair_cube = bond_dirs[:, None] * bond_dirs[None, :]
    pair = pair_cube.reshape((9,) + bond_dirs.shape[1:])
    coupling = jnp.sum(d_less * pair[None, None], axis=2)
    first_mode = (
        (energy_rank * lax.axis_size("momentum") + momentum_rank) * lax.axis_size("phonon")
        + phonon_rank
    ) * modes_here
    own_table = lax.dynamic_slice_in_dim(table, first_mode, modes_here, 0)
    spread = lax.all_to_all(
        coupling.astype(jnp.bfloat16), "phonon", split_axis=3, concat_axis=0, tiled=True
    ).astype(coupling.dtype)
    blank = jnp.zeros((classes, 2 * bonds * atom_share), jnp.float32)
    piece = lax.all_gather(
        spread.astype(jnp.bfloat16), ("energy", "momentum"), axis=0, tiled=True
    ).astype(jnp.float32)
    rows = piece.shape[0]
    flat_piece = piece.reshape(rows, -1)
    emitted = blank + jnp.einsum("mc,mx->cx", table, flat_piece, precision=HIGH)
    absorbed = blank + jnp.einsum("mc,mx->cx", soaked, flat_piece, precision=HIGH)
    emitted = emitted.reshape(classes, 2, bonds, atom_share)
    absorbed = absorbed.reshape(classes, 2, bonds, atom_share)
    emit_table = emitted.transpose(0, 1, 3, 2).reshape(REACH, all_momenta, 2, local_width)
    soak_table = absorbed.transpose(0, 1, 3, 2).reshape(REACH, all_momenta, 2, local_width)
    moved = [shifted_2(g_less, "energy", step) for step in both_steps]
    lower = jnp.concatenate(moved[:span], axis=0)
    upper = jnp.concatenate(moved[span:], axis=0)
    lesser_rimmed = jnp.concatenate([lower, g_less, upper], axis=0)
    greater_moved = [shifted_2(g_great, "energy", step) for step in lower_steps]
    greater_rim = jnp.concatenate(greater_moved, axis=0)
    greater_rimmed = jnp.concatenate([greater_rim, g_great], axis=0)
    lesser_wide, greater_wide = (
        lax.all_gather(lesser_rimmed, "momentum", axis=1, tiled=True),
        lax.all_gather(greater_rimmed, "momentum", axis=1, tiled=True),
    )
    here_moment = momentum_rank * momenta_here + jnp.arange(momenta_here, dtype=jnp.int32)
    every_moment = jnp.arange(all_momenta, dtype=jnp.int32)
    behind = (here_moment[:, None] - every_moment[None, :]) % all_momenta
    ahead = (every_moment[None, :] - here_moment[:, None]) % all_momenta
    pick_behind = (behind[:, :, None] == every_moment[None, None, :]).astype(jnp.float32)
    pick_ahead = (ahead[:, :, None] == every_moment[None, None, :]).astype(jnp.float32)
    total = jnp.zeros(g_less.shape, jnp.float32)
    polar_parts = []
    for energy_step in range(1, REACH + 1):
        below = lesser_wide[REACH - energy_step : REACH - energy_step + energies]
        above = lesser_wide[REACH + energy_step : REACH + energy_step + energies]
        weight_below = jnp.einsum(
            "lkq,qzx->lkzx", pick_behind, emit_table[energy_step - 1], precision=HIGH
        )
        weight_above = jnp.einsum(
            "lkq,qzx->lkzx", pick_ahead, soak_table[energy_step - 1], precision=HIGH
        )
        total = total + scaled_blocks(weight_below, below) + scaled_blocks(weight_above, above)
        earlier = greater_wide[REACH - energy_step : REACH - energy_step + energies]
        pairs = inner_sums(g_less, earlier)
        polar_parts.append(jnp.einsum("lkq,lkzx->qzx", pick_behind, pairs, precision=HIGH))
    self_energy = total.astype(jnp.bfloat16)
    scale = float(all_energies * all_momenta * ORB * ORB) ** (-0.5)
    polar_local = jnp.stack(polar_parts).reshape(classes, 2, local_width) * scale
    polar_summed = lax.psum(polar_local, ("energy", "momentum"))
    polar_full = lax.all_gather(polar_summed, "phonon", axis=2, tiled=True)
    own_polar = jnp.einsum("mc,czx->mzx", own_table, polar_full, precision=HIGH)
    own_polar = own_polar.reshape(modes_here, 2, whole_atoms, bonds).transpose(0, 1, 3, 2)
    link = (
        neighbours[:, :, None] == jnp.arange(whole_atoms, dtype=jnp.int32)[None, None, :]
    ).astype(jnp.float32)
    weighted = pair_cube[None, None] * own_polar[:, :, None, None]
    dense = jnp.einsum("mzijna,nab->mziajb", weighted, link, precision=HIGH)
    dense = dense.reshape(modes_here, 2, order, order).astype(jnp.bfloat16)
    dense_re, dense_im = (dense[:, 0], dense[:, 1])
    ret_re, ret_im = (d_ret[:, 0], d_ret[:, 1])
    half_re = (times_adjoint(dense_re, ret_re) + times_adjoint(dense_im, ret_im)).astype(
        jnp.bfloat16
    )
    half_im = (times_adjoint(dense_im, ret_re) - times_adjoint(dense_re, ret_im)).astype(
        jnp.bfloat16
    )
    next_re = times_plain(ret_re, half_re) - times_plain(ret_im, half_im)
    next_im = times_plain(ret_re, half_im) + times_plain(ret_im, half_re)
    d_next = jnp.stack([next_re, next_im], axis=1).astype(jnp.bfloat16)
    return (self_energy, d_next)


GROUP = ("energy", "momentum")
EVERY = ("energy", "momentum", "phonon")
F32 = jnp.float32
BF16 = jnp.bfloat16


class Plan:
    def __init__(self, g_shape, d_shape, ret_shape, n_energy, n_momentum, n_phonon):
        self.energies, self.momenta, _, self.entries, self.width = g_shape
        self.modes, _, _, self.bonds, self.atoms = d_shape
        self.order = ret_shape[2]
        self.n_momentum = n_momentum
        self.n_phonon = n_phonon
        self.group = n_energy * n_momentum
        self.devices = self.group * n_phonon
        self.all_energies = self.energies * n_energy
        self.all_momenta = self.momenta * n_momentum
        self.classes = REACH * self.all_momenta
        self.slabs = 2 * self.energies
        self.tiles = self.width // LANES
        self.rest = self.width % LANES
        self.halves = self.group // max(self.tiles, 1)
        self.rows = self.entries // max(self.halves, 1)
        self.rest_rows = self.entries // self.group
        self.main_rows = self.slabs * self.rows
        self.rest_pad = -(-self.rest_rows // 8) * 8
        self.message = -(-(self.main_rows + self.rest_pad) // 16) * 16
        self.tail = self.message - self.main_rows
        self.held = self.rows + self.rest_pad
        self.columns = self.width * n_phonon

    def fits(self):
        return (
            self.momenta == 1
            and self.group & (self.group - 1) == 0
            and self.tiles > 0
            and self.halves * self.tiles == self.group
            and self.entries % (8 * self.halves) == 0
            and self.entries % 16 == 0
            and self.entries % self.group == 0
            and self.rest > 0
            and self.slabs * self.rest == LANES
            and self.tail >= self.rest_pad
            and self.modes * 4 <= 8
            and self.atoms == LANES
            and self.order == 3 * self.atoms
            and self.all_energies <= 8
            and self.all_momenta <= 2
        )


def call(kernel, out_shape, *operands, scratch=(), scalars=0, flops=0, moved=0):
    smem = pl.BlockSpec(memory_space=pltpu.SMEM)
    vmem = pl.BlockSpec(memory_space=pltpu.VMEM)
    specs = [smem] * scalars + [vmem] * (len(operands) - scalars)
    many = isinstance(out_shape, (list, tuple))
    return pl.pallas_call(
        kernel,
        out_shape=out_shape,
        in_specs=specs,
        out_specs=[vmem] * len(out_shape) if many else vmem,
        scratch_shapes=list(scratch),
        compiler_params=pltpu.CompilerParams(vmem_limit_bytes=48 * 2**20),
        cost_estimate=pl.CostEstimate(flops=flops, bytes_accessed=moved, transcendentals=0),
    )(*operands)


def deal_kernel(plan, rank_ref, less_ref, great_ref, *refs):
    outs, rest_ref = refs[: plan.group], refs[plan.group]
    rank = rank_ref[0]
    sources = (less_ref, great_ref)
    for which, source in enumerate(sources):
        pieces = [
            source[e, 0, z, :, plan.tiles * LANES :].astype(F32)
            for e in range(plan.energies)
            for z in range(2)
        ]
        rest_ref[which, : plan.entries] = jnp.concatenate(pieces, axis=1)
        rest_ref[which, plan.entries :] = jnp.zeros((plan.tail, LANES), F32)
    for k in range(plan.group):
        target = rank ^ k
        tile = target // plan.halves
        half = target % plan.halves
        lanes = pl.ds(pl.multiple_of(tile * LANES, LANES), LANES)
        for which, source in enumerate(sources):
            parts = []
            for e in range(plan.energies):
                for z in range(2):
                    whole = source[e, 0, z, :, lanes].astype(F32)
                    part = whole[: plan.rows]
                    for other in range(1, plan.halves):
                        piece = whole[other * plan.rows : (other + 1) * plan.rows]
                        part = jnp.where(half == other, piece, part)
                    parts.append(part)
            parts.append(rest_ref[which, pl.ds(target * plan.rest_rows, plan.tail), :])
            outs[k][which] = jnp.concatenate(parts, axis=0).astype(BF16)


def couple_kernel(plan, less_ref, dirs_ref, mod_ref, out_ref):
    bonds, width = plan.bonds, plan.width
    padded = -(-bonds // 8) * 8
    dirs = dirs_ref[...]
    rows = []
    for m in range(plan.modes):
        for z in range(2):
            total = jnp.zeros((bonds, plan.atoms), F32)
            for i in range(3):
                for j in range(3):
                    total = total + less_ref[m, z, 3 * i + j] * (dirs[i] * dirs[j])
            rows.append(jnp.pad(total, ((0, padded - bonds), (0, 0))))
    stacked = jnp.concatenate(rows, axis=0).astype(BF16)
    atom = lax.broadcasted_iota(jnp.int32, (plan.atoms, plan.columns), 0)
    column = lax.broadcasted_iota(jnp.int32, (plan.atoms, plan.columns), 1)
    inside = column - atom * bonds
    chosen = jnp.where((inside >= 0) & (inside < bonds), 1.0, 0.0).astype(BF16)
    spread = jnp.dot(stacked, chosen, preferred_element_type=F32)
    bond = lax.broadcasted_iota(jnp.int32, (padded, plan.columns), 0)
    keep = bond == mod_ref[...]
    lines = []
    for row in range(2 * plan.modes):
        piece = spread[row * padded : (row + 1) * padded]
        lines.append(jnp.sum(jnp.where(keep, piece, 0.0), axis=0, keepdims=True))
    while len(lines) < 4:
        lines.append(jnp.zeros((1, plan.columns), F32))
    flat = jnp.concatenate(lines, axis=0)
    for p in range(plan.n_phonon):
        start = p * width
        rest = flat[:, start + plan.tiles * LANES : start + width]
        rest = jnp.concatenate([rest, jnp.zeros((4, LANES - plan.rest), F32)], axis=1)
        for tile in range(plan.tiles):
            main = flat[:, start + tile * LANES : start + (tile + 1) * LANES]
            block = jnp.concatenate([main, rest], axis=0)
            for half in range(plan.halves):
                out_ref[(tile * plan.halves + half) * plan.n_phonon + p] = block


def place_of(plan, source, e, z):
    energy = plan.energies * (source // plan.n_momentum) + e
    return (energy * plan.all_momenta + source % plan.n_momentum) * 2 + z


def stage_blocks(plan, rank, which, messages, held_ref):
    row = lax.broadcasted_iota(jnp.int32, (plan.rest_pad, LANES), 0)
    for k, message in enumerate(messages):
        source = rank ^ k
        values = message[which].astype(F32)
        tail = values[plan.main_rows : plan.main_rows + plan.rest_pad]
        tail = jnp.where(row < plan.rest_rows, tail, 0.0)
        for e in range(plan.energies):
            for z in range(2):
                slab = 2 * e + z
                place = place_of(plan, source, e, z)
                held_ref[place, : plan.rows] = values[slab * plan.rows : (slab + 1) * plan.rows]
                turned = tail if slab == 0 else pltpu.roll(tail, LANES - slab * plan.rest, 1)
                held_ref[place, plan.rows :] = turned


def polar_kernel(plan, rank_ref, pick_ref, *refs):
    messages = refs[: plan.group]
    out_ref, low_ref, high_ref = refs[plan.group :]
    rank = rank_ref[0]
    stage_blocks(plan, rank, 0, messages, low_ref)
    stage_blocks(plan, rank, 1, messages, high_ref)
    count, momenta = plan.all_energies, plan.all_momenta

    def step(chunk, sums):
        rows = pl.ds(pl.multiple_of(chunk * 8, 8), 8)
        sums = list(sums)
        for energy_step in range(1, REACH + 1):
            for q in range(momenta):
                index = ((energy_step - 1) * momenta + q) * 2
                for energy in range(energy_step, count):
                    for k in range(momenta):
                        low = (energy * momenta + k) * 2
                        high = ((energy - energy_step) * momenta + (k - q) % momenta) * 2
                        low_re, low_im = low_ref[low, rows], low_ref[low + 1, rows]
                        high_re, high_im = high_ref[high, rows], high_ref[high + 1, rows]
                        sums[index] = sums[index] + (low_re * high_re + low_im * high_im)
                        sums[index + 1] = sums[index + 1] + (low_im * high_re - low_re * high_im)
        return tuple(sums)

    none = tuple(jnp.zeros((8, LANES), F32) for _ in range(2 * plan.classes))
    main = lax.fori_loop(0, plan.rows // 8, step, none)
    rest = lax.fori_loop(plan.rows // 8, plan.held // 8, step, none)
    scale = float(count * momenta * plan.entries) ** (-0.5)
    lines = [jnp.sum(part, axis=0, keepdims=True) * scale for part in main + rest]
    table = jnp.concatenate(lines, axis=0)
    picked = lax.dot_general(
        pick_ref[...], table, (((0,), (0,)), ((), ())), precision=HIGH, preferred_element_type=F32
    )
    out_ref[...] = picked.reshape(out_ref.shape)


def energy_kernel(plan, rank_ref, weigh_ref, coupling_ref, *refs):
    messages = refs[: plan.group]
    outs = refs[plan.group : 2 * plan.group]
    low_ref, sum_ref, weight_ref = refs[2 * plan.group :]
    rank = rank_ref[0]
    flat = coupling_ref[...].reshape(plan.devices * 8, LANES)
    weight_ref[...] = jnp.dot(weigh_ref[...], flat, precision=HIGH, preferred_element_type=F32)
    stage_blocks(plan, rank, 0, messages, low_ref)
    count, momenta = plan.all_energies, plan.all_momenta

    def run(base):
        def step(chunk, carry):
            rows = pl.ds(pl.multiple_of(chunk * 8, 8), 8)
            re = [None] * (count * momenta)
            im = [None] * (count * momenta)
            for energy_step in range(1, REACH + 1):
                for q in range(momenta):
                    index = base + ((energy_step - 1) * momenta + q) * 2
                    pairs = []
                    for part, sign in ((0, -1), (1, 1)):
                        at = index + part * 2 * plan.classes
                        w_re = jnp.broadcast_to(weight_ref[at : at + 1], (8, LANES))
                        w_im = jnp.broadcast_to(weight_ref[at + 1 : at + 2], (8, LANES))
                        pairs.append((sign, w_re, w_im))
                    for energy in range(count):
                        for k in range(momenta):
                            slot = energy * momenta + k
                            for sign, w_re, w_im in pairs:
                                other = energy + sign * energy_step
                                if other < 0 or other >= count:
                                    continue
                                at = (other * momenta + (k + sign * q) % momenta) * 2
                                b_re, b_im = low_ref[at, rows], low_ref[at + 1, rows]
                                t_re = w_re * b_re - w_im * b_im
                                t_im = w_re * b_im + w_im * b_re
                                re[slot] = t_re if re[slot] is None else re[slot] + t_re
                                im[slot] = t_im if im[slot] is None else im[slot] + t_im
            for slot in range(count * momenta):
                sum_ref[2 * slot, rows] = re[slot]
                sum_ref[2 * slot + 1, rows] = im[slot]
            return carry

        return step

    lax.fori_loop(0, plan.rows // 8, run(0), 0)
    lax.fori_loop(plan.rows // 8, plan.held // 8, run(4 * plan.classes), 0)
    lane = lax.broadcasted_iota(jnp.int32, (plan.rest_pad, LANES), 1)
    for k in range(plan.group):
        target = rank ^ k
        parts = []
        tail = jnp.zeros((plan.rest_pad, LANES), F32)
        for e in range(plan.energies):
            for z in range(2):
                slab = 2 * e + z
                place = place_of(plan, target, e, z)
                parts.append(sum_ref[place, : plan.rows])
                piece = sum_ref[place, plan.rows :]
                if slab:
                    piece = pltpu.roll(piece, slab * plan.rest, 1)
                mine = (lane >= slab * plan.rest) & (lane < (slab + 1) * plan.rest)
                tail = jnp.where(mine, piece, tail)
        parts.append(tail)
        if plan.tail > plan.rest_pad:
            parts.append(jnp.zeros((plan.tail - plan.rest_pad, LANES), F32))
        outs[k][...] = jnp.concatenate(parts, axis=0).astype(BF16)


def gather_kernel(plan, rank_ref, *refs):
    messages = refs[: plan.group]
    out_ref, wide_ref, rest_ref = refs[plan.group :]
    rank = rank_ref[0]
    for k, message in enumerate(messages):
        source = rank ^ k
        tile = source // plan.halves
        half = source % plan.halves
        values = message[...].astype(F32)
        lanes = pl.ds(pl.multiple_of(tile * LANES, LANES), LANES)
        rows = pl.ds(pl.multiple_of(half * plan.rows, 8), plan.rows)
        tail = values[plan.main_rows : plan.main_rows + plan.rest_pad]
        for slab in range(plan.slabs):
            wide_ref[slab, rows, lanes] = values[slab * plan.rows : (slab + 1) * plan.rows]
            turned = tail if slab == 0 else pltpu.roll(tail, LANES - slab * plan.rest, 1)
            rest_ref[slab, source] = turned
    for e in range(plan.energies):
        for z in range(2):
            slab = 2 * e + z
            parts = [rest_ref[slab, source, : plan.rest_rows] for source in range(plan.group)]
            rest = jnp.concatenate(parts, axis=0)[:, : plan.rest]
            whole = jnp.concatenate([wide_ref[slab], rest], axis=1)
            out_ref[e, 0, z] = whole.astype(BF16)


def next_kernel(plan, polar_ref, ret_ref, near_ref, dirs_ref, mod_ref, out_ref, v_ref, dense_ref):
    bonds, atoms, order = plan.bonds, plan.atoms, plan.order
    padded = -(-bonds // 8) * 8
    lines = []
    for p in range(plan.n_phonon):
        rest = jnp.zeros((4, LANES), F32)
        for tile in range(plan.tiles):
            main = jnp.zeros((4, LANES), F32)
            for half in range(plan.halves):
                block = polar_ref[(tile * plan.halves + half) * plan.n_phonon + p]
                main = main + block[:4]
                rest = rest + block[4:]
            lines.append(main)
        lines.append(rest[:, : plan.rest])
    flat = jnp.concatenate(lines, axis=1)
    bond = lax.broadcasted_iota(jnp.int32, (padded, plan.columns), 0)
    keep = bond == mod_ref[...]
    tall = jnp.concatenate(
        [jnp.where(keep, flat[row : row + 1], 0.0) for row in range(2 * plan.modes)], axis=0
    )
    upper = tall.astype(BF16)
    lower = (tall - upper.astype(F32)).astype(BF16)
    atom = lax.broadcasted_iota(jnp.int32, (atoms, plan.columns), 0)
    column = lax.broadcasted_iota(jnp.int32, (atoms, plan.columns), 1)
    inside = column - atom * bonds
    chosen = jnp.where((inside >= 0) & (inside < bonds), 1.0, 0.0).astype(BF16)
    contract = (((1,), (1,)), ((), ()))
    by_bond = lax.dot_general(upper, chosen, contract, preferred_element_type=F32)
    by_bond = by_bond + lax.dot_general(lower, chosen, contract, preferred_element_type=F32)
    ways = [(i, j) for i in range(3) for j in range(i, 3)]
    for way, (i, j) in enumerate(ways):
        pair = dirs_ref[i] * dirs_ref[j]
        for row in range(2 * plan.modes):
            values = by_bond[row * padded : row * padded + bonds]
            v_ref[row * len(ways) + way, :bonds] = values * pair

    def step(chunk, carry):
        first = pl.multiple_of(chunk * 16, 16)
        number = lax.broadcasted_iota(jnp.int32, (16, atoms), 0) + first
        for row in range(2 * plan.modes):
            sums = [jnp.zeros((16, atoms), F32) for _ in ways]
            for n in range(bonds):
                hit = number == near_ref[n : n + 1]
                for way in range(len(ways)):
                    value = v_ref[row * len(ways) + way, n : n + 1]
                    sums[way] = sums[way] + jnp.where(hit, value, 0.0)
            for way, (i, j) in enumerate(ways):
                block = sums[way].astype(BF16)
                dense_ref[
                    row, pl.ds(pl.multiple_of(j * atoms + first, 16), 16), i * atoms : (i + 1) * atoms
                ] = block
                if i != j:
                    dense_ref[
                        row,
                        pl.ds(pl.multiple_of(i * atoms + first, 16), 16),
                        j * atoms : (j + 1) * atoms,
                    ] = block
        return carry

    lax.fori_loop(0, atoms // 16, step, 0)
    plain = (((1,), (0,)), ((), ()))
    for m in range(plan.modes):
        ret_re, ret_im = ret_ref[m, 0], ret_ref[m, 1]
        dense_re, dense_im = dense_ref[2 * m], dense_ref[2 * m + 1]

        def times(left, right, how):
            return lax.dot_general(left, right, how, preferred_element_type=F32)

        half_re = (times(ret_re, dense_re, plain) + times(ret_im, dense_im, plain)).astype(BF16)
        half_im = (times(ret_re, dense_im, plain) - times(ret_im, dense_re, plain)).astype(BF16)
        next_re = times(ret_re, half_re, contract) - times(ret_im, half_im, contract)
        next_im = times(ret_re, half_im, contract) + times(ret_im, half_re, contract)
        out_ref[m, 0] = next_re.astype(BF16)
        out_ref[m, 1] = next_im.astype(BF16)


def mode_tables(plan, energy_offset, momentum_offset, absorb):
    label = (energy_offset - 1) * plan.all_momenta + momentum_offset
    line = jnp.arange(8, dtype=jnp.int32)
    shape = (2, 2, plan.classes, 2, plan.devices, 8)
    wanted = jnp.arange(plan.classes, dtype=jnp.int32)
    labels = label.reshape(plan.devices, plan.modes)
    weights = absorb.reshape(plan.devices, plan.modes)
    inner = line % 4 // 2
    by_line = sum(jnp.where(inner == i, labels[:, i : i + 1], 0) for i in range(plan.modes))
    scale = sum(jnp.where(inner == i, weights[:, i : i + 1], 0.0) for i in range(plan.modes))
    used = (inner < plan.modes)[None, :]
    same = (by_line[None] == wanted[:, None, None]) & used[None]
    part = (line % 2)[None, :] == jnp.arange(2, dtype=jnp.int32)[:, None]
    kind = (line // 4)[None, :] == jnp.arange(2, dtype=jnp.int32)[:, None]
    hit = (
        same[None, :, None] & part[None, None, :, None] & kind[:, None, None, None]
    ).astype(F32)
    table = jnp.stack([hit, hit * scale[None, None, None]], axis=1)
    return table.reshape(4 * 2 * plan.classes, plan.devices * 8)


def exchange(plan, blocks):
    routes = [[(i, i ^ k) for i in range(plan.group)] for k in range(plan.group)]
    moved = [lax.ppermute(blocks[k], GROUP, routes[k]) for k in range(1, plan.group)]
    return [blocks[0]] + moved


def dealt(
    plan, g_less, g_great, d_less, d_ret, neighbours, bond_dirs, energy_offset, momentum_offset, absorb
):
    rank = lax.axis_index(GROUP).astype(jnp.int32).reshape(1)
    group, held = plan.group, plan.held
    slots = plan.all_energies * plan.all_momenta * 2
    mod = np.arange(plan.columns, dtype=np.int32)[None] % plan.bonds
    table = mode_tables(plan, energy_offset, momentum_offset, absorb)
    lines = 2 * plan.classes
    picks = jnp.concatenate([table[:lines], table[2 * lines : 3 * lines]], axis=0)

    message = jax.ShapeDtypeStruct((2, plan.message, LANES), BF16)
    blocks = call(
        functools.partial(deal_kernel, plan), [message] * group, rank, g_less, g_great,
        scalars=1, scratch=[pltpu.VMEM((2, plan.entries + plan.tail, LANES), F32)],
        moved=4 * g_less.size * 2,
    )
    small = jax.ShapeDtypeStruct((plan.devices, 8, LANES), F32)
    coupling = call(functools.partial(couple_kernel, plan), small, d_less, bond_dirs, mod)
    blocks = exchange(plan, blocks)
    coupling = lax.all_to_all(coupling, EVERY, 0, 0, tiled=True)
    block_scratch = pltpu.VMEM((slots, held, LANES), F32)
    polar = call(
        functools.partial(polar_kernel, plan), small, rank, picks, *blocks,
        scalars=1, scratch=[block_scratch] * 2,
    )
    answer = jax.ShapeDtypeStruct((plan.message, LANES), BF16)
    sums = call(
        functools.partial(energy_kernel, plan), [answer] * group, rank, table, coupling, *blocks,
        scalars=1,
        scratch=[block_scratch, block_scratch, pltpu.VMEM((4 * lines, LANES), F32)],
    )
    polar = lax.all_to_all(polar, EVERY, 0, 0, tiled=True)
    sums = exchange(plan, sums)
    self_energy = call(
        functools.partial(gather_kernel, plan), jax.ShapeDtypeStruct(g_less.shape, BF16), rank, *sums,
        scalars=1,
        scratch=[
            pltpu.VMEM((plan.slabs, plan.entries, plan.tiles * LANES), F32),
            pltpu.VMEM((plan.slabs, group, plan.rest_pad, LANES), F32),
        ],
    )
    padded = -(-plan.bonds // 8) * 8
    d_next = call(
        functools.partial(next_kernel, plan), jax.ShapeDtypeStruct(d_ret.shape, BF16),
        polar, d_ret, neighbours, bond_dirs, mod,
        scratch=[
            pltpu.VMEM((12 * plan.modes, padded, plan.atoms), F32),
            pltpu.VMEM((2 * plan.modes, plan.order, plan.order), BF16),
        ],
    )
    return self_energy, d_next


def local(*arrays):
    plan = Plan(
        arrays[0].shape, arrays[2].shape, arrays[3].shape,
        lax.axis_size("energy"), lax.axis_size("momentum"), lax.axis_size("phonon"),
    )
    return dealt(plan, *arrays) if plan.fits() else general(*arrays)


def solution(mesh):
    in_specs = (
        P("energy", "momentum", None, None, "phonon"),
        P("energy", "momentum", None, None, "phonon"),
        P(("energy", "momentum", "phonon"), None, None, None, None),
        P(("energy", "momentum", "phonon"), None, None, None),
        P(),
        P(),
        P(),
        P(),
        P(),
    )
    out_specs = (
        P("energy", "momentum", None, None, "phonon"),
        P(("energy", "momentum", "phonon"), None, None, None),
    )
    return jax.shard_map(local, mesh=mesh, in_specs=in_specs, out_specs=out_specs, check_vma=False)
```

```python
import functools

import jax
import jax.numpy as jnp
from jax import lax
from jax.experimental import pallas as pl
from jax.experimental.pallas import tpu as pltpu
from jax.sharding import PartitionSpec as P

ORB = 12
REACH = 4
LANES = 128


HIGH = lax.Precision.HIGHEST


def shifted_2(block, axis, distance):
    devices = range(lax.axis_size(axis))
    route = [(i - distance, i) for i in devices if i - distance in devices]
    return lax.ppermute(block, axis, route)


def scaled_blocks(weights, blocks):
    real_w = weights[None, :, :, 0, None, :]
    imag_w = weights[None, :, :, 1, None, :]
    real_b = blocks[:, None, :, 0].astype(jnp.float32)
    imag_b = blocks[:, None, :, 1].astype(jnp.float32)
    real_part = jnp.sum(real_w * real_b - imag_w * imag_b, axis=2)
    imag_part = jnp.sum(real_w * imag_b + imag_w * real_b, axis=2)
    return jnp.stack([real_part, imag_part], axis=2)


def inner_sums(local_blocks, shifted):
    local_real = local_blocks[:, :, 0].astype(jnp.float32)[:, :, None]
    local_imag = local_blocks[:, :, 1].astype(jnp.float32)[:, :, None]
    other_real = shifted[:, :, 0].astype(jnp.float32)[:, None]
    other_imag = shifted[:, :, 1].astype(jnp.float32)[:, None]
    real_sum = jnp.sum(local_real * other_real + local_imag * other_imag, axis=(0, 3))
    imag_sum = jnp.sum(local_imag * other_real - local_real * other_imag, axis=(0, 3))
    return jnp.stack([real_sum, imag_sum], axis=2)


def times_adjoint(left, right):
    return jnp.einsum("mab,mcb->mac", left, right, preferred_element_type=jnp.float32)


def times_plain(left, right):
    return jnp.einsum("mab,mbc->mac", left, right, preferred_element_type=jnp.float32)


def general(
    g_less, g_great, d_less, d_ret, neighbours, bond_dirs, energy_offset, momentum_offset, absorb
):
    energies = g_less.shape[0]
    momenta_here = g_less.shape[1]
    local_width = g_less.shape[4]
    bonds = d_less.shape[3]
    whole_atoms = d_less.shape[4]
    atom_share = local_width // bonds
    all_momenta = momenta_here * lax.axis_size("momentum")
    all_energies = energies * lax.axis_size("energy")
    modes_here = d_less.shape[0]
    order = d_ret.shape[2]
    classes = REACH * all_momenta
    energy_rank = lax.axis_index("energy")
    momentum_rank = lax.axis_index("momentum")
    phonon_rank = lax.axis_index("phonon")
    span = -(-REACH // energies)
    lower_steps = list(range(span, 0, -1))
    both_steps = lower_steps + list(range(-1, -span - 1, -1))
    label = (energy_offset - 1) * all_momenta + momentum_offset
    table = (label[:, None] == jnp.arange(classes, dtype=jnp.int32)[None, :]).astype(jnp.float32)
    soaked = table * absorb[:, None]
    pair_cube = bond_dirs[:, None] * bond_dirs[None, :]
    pair = pair_cube.reshape((9,) + bond_dirs.shape[1:])
    coupling = jnp.sum(d_less * pair[None, None], axis=2)
    first_mode = (
        (energy_rank * lax.axis_size("momentum") + momentum_rank) * lax.axis_size("phonon")
        + phonon_rank
    ) * modes_here
    own_table = lax.dynamic_slice_in_dim(table, first_mode, modes_here, 0)
    spread = lax.all_to_all(
        coupling.astype(jnp.bfloat16), "phonon", split_axis=3, concat_axis=0, tiled=True
    ).astype(coupling.dtype)
    blank = jnp.zeros((classes, 2 * bonds * atom_share), jnp.float32)
    piece = lax.all_gather(
        spread.astype(jnp.bfloat16), ("energy", "momentum"), axis=0, tiled=True
    ).astype(jnp.float32)
    rows = piece.shape[0]
    flat_piece = piece.reshape(rows, -1)
    emitted = blank + jnp.einsum("mc,mx->cx", table, flat_piece, precision=HIGH)
    absorbed = blank + jnp.einsum("mc,mx->cx", soaked, flat_piece, precision=HIGH)
    emitted = emitted.reshape(classes, 2, bonds, atom_share)
    absorbed = absorbed.reshape(classes, 2, bonds, atom_share)
    emit_table = emitted.transpose(0, 1, 3, 2).reshape(REACH, all_momenta, 2, local_width)
    soak_table = absorbed.transpose(0, 1, 3, 2).reshape(REACH, all_momenta, 2, local_width)
    moved = [shifted_2(g_less, "energy", step) for step in both_steps]
    lower = jnp.concatenate(moved[:span], axis=0)
    upper = jnp.concatenate(moved[span:], axis=0)
    lesser_rimmed = jnp.concatenate([lower, g_less, upper], axis=0)
    greater_moved = [shifted_2(g_great, "energy", step) for step in lower_steps]
    greater_rim = jnp.concatenate(greater_moved, axis=0)
    greater_rimmed = jnp.concatenate([greater_rim, g_great], axis=0)
    lesser_wide, greater_wide = (
        lax.all_gather(lesser_rimmed, "momentum", axis=1, tiled=True),
        lax.all_gather(greater_rimmed, "momentum", axis=1, tiled=True),
    )
    here_moment = momentum_rank * momenta_here + jnp.arange(momenta_here, dtype=jnp.int32)
    every_moment = jnp.arange(all_momenta, dtype=jnp.int32)
    behind = (here_moment[:, None] - every_moment[None, :]) % all_momenta
    ahead = (every_moment[None, :] - here_moment[:, None]) % all_momenta
    pick_behind = (behind[:, :, None] == every_moment[None, None, :]).astype(jnp.float32)
    pick_ahead = (ahead[:, :, None] == every_moment[None, None, :]).astype(jnp.float32)
    total = jnp.zeros(g_less.shape, jnp.float32)
    polar_parts = []
    for energy_step in range(1, REACH + 1):
        below = lesser_wide[REACH - energy_step : REACH - energy_step + energies]
        above = lesser_wide[REACH + energy_step : REACH + energy_step + energies]
        weight_below = jnp.einsum(
            "lkq,qzx->lkzx", pick_behind, emit_table[energy_step - 1], precision=HIGH
        )
        weight_above = jnp.einsum(
            "lkq,qzx->lkzx", pick_ahead, soak_table[energy_step - 1], precision=HIGH
        )
        total = total + scaled_blocks(weight_below, below) + scaled_blocks(weight_above, above)
        earlier = greater_wide[REACH - energy_step : REACH - energy_step + energies]
        pairs = inner_sums(g_less, earlier)
        polar_parts.append(jnp.einsum("lkq,lkzx->qzx", pick_behind, pairs, precision=HIGH))
    self_energy = total.astype(jnp.bfloat16)
    scale = float(all_energies * all_momenta * ORB * ORB) ** (-0.5)
    polar_local = jnp.stack(polar_parts).reshape(classes, 2, local_width) * scale
    polar_summed = lax.psum(polar_local, ("energy", "momentum"))
    polar_full = lax.all_gather(polar_summed, "phonon", axis=2, tiled=True)
    own_polar = jnp.einsum("mc,czx->mzx", own_table, polar_full, precision=HIGH)
    own_polar = own_polar.reshape(modes_here, 2, whole_atoms, bonds).transpose(0, 1, 3, 2)
    link = (
        neighbours[:, :, None] == jnp.arange(whole_atoms, dtype=jnp.int32)[None, None, :]
    ).astype(jnp.float32)
    weighted = pair_cube[None, None] * own_polar[:, :, None, None]
    dense = jnp.einsum("mzijna,nab->mziajb", weighted, link, precision=HIGH)
    dense = dense.reshape(modes_here, 2, order, order).astype(jnp.bfloat16)
    dense_re, dense_im = (dense[:, 0], dense[:, 1])
    ret_re, ret_im = (d_ret[:, 0], d_ret[:, 1])
    half_re = (times_adjoint(dense_re, ret_re) + times_adjoint(dense_im, ret_im)).astype(
        jnp.bfloat16
    )
    half_im = (times_adjoint(dense_im, ret_re) - times_adjoint(dense_re, ret_im)).astype(
        jnp.bfloat16
    )
    next_re = times_plain(ret_re, half_re) - times_plain(ret_im, half_im)
    next_im = times_plain(ret_re, half_im) + times_plain(ret_im, half_re)
    d_next = jnp.stack([next_re, next_im], axis=1).astype(jnp.bfloat16)
    return (self_energy, d_next)


GROUP = ("energy", "momentum")
EVERY = ("energy", "momentum", "phonon")
F32 = jnp.float32
BF16 = jnp.bfloat16


class Plan:
    def __init__(self, g_shape, d_shape, ret_shape, n_energy, n_momentum, n_phonon):
        self.energies, self.momenta, _, self.entries, self.width = g_shape
        self.modes, _, _, self.bonds, self.atoms = d_shape
        self.order = ret_shape[2]
        self.n_momentum = n_momentum
        self.n_phonon = n_phonon
        self.group = n_energy * n_momentum
        self.devices = self.group * n_phonon
        self.all_energies = self.energies * n_energy
        self.all_momenta = self.momenta * n_momentum
        self.classes = REACH * self.all_momenta
        self.slabs = 2 * self.energies
        self.tiles = self.width // LANES
        self.rest = self.width % LANES
        self.halves = self.group // max(self.tiles, 1)
        self.rows = self.entries // max(self.halves, 1)
        self.rest_rows = self.entries // self.group
        self.main_rows = self.slabs * self.rows
        self.rest_pad = -(-self.rest_rows // 8) * 8
        self.message = -(-(self.main_rows + self.rest_pad) // 16) * 16
        self.tail = self.message - self.main_rows
        self.held = self.rows + self.rest_pad
        self.columns = self.width * n_phonon
        self.partners = sorted(
            range(self.group), key=lambda k: (k > 0, k < n_momentum, k % n_momentum, k)
        )

    def fits(self):
        return (
            self.momenta == 1
            and self.group & (self.group - 1) == 0
            and self.tiles > 0
            and self.halves * self.tiles == self.group
            and self.entries % (8 * self.halves) == 0
            and self.entries % 16 == 0
            and self.entries % self.group == 0
            and self.rest > 0
            and self.slabs * self.rest == LANES
            and self.tail >= self.rest_pad
            and self.modes * 4 <= 8
            and self.atoms == LANES
            and self.order == 3 * self.atoms
            and self.all_energies <= 8
            and self.all_momenta <= 2
        )


def call(kernel, out_shape, *operands, scratch=(), scalars=0, flops=0, moved=0):
    smem = pl.BlockSpec(memory_space=pltpu.SMEM)
    vmem = pl.BlockSpec(memory_space=pltpu.VMEM)
    specs = [smem] * scalars + [vmem] * (len(operands) - scalars)
    many = isinstance(out_shape, (list, tuple))
    return pl.pallas_call(
        kernel,
        out_shape=out_shape,
        in_specs=specs,
        out_specs=[vmem] * len(out_shape) if many else vmem,
        scratch_shapes=list(scratch),
        compiler_params=pltpu.CompilerParams(vmem_limit_bytes=48 * 2**20),
        cost_estimate=pl.CostEstimate(flops=flops, bytes_accessed=moved, transcendentals=0),
    )(*operands)


def deal_kernel(plan, rank_ref, less_ref, great_ref, *refs):
    outs, rest_ref = refs[: plan.group], refs[plan.group]
    rank = rank_ref[0]
    sources = (less_ref, great_ref)
    for which, source in enumerate(sources):
        pieces = [
            source[e, 0, z, :, plan.tiles * LANES :].astype(F32)
            for e in range(plan.energies)
            for z in range(2)
        ]
        rest_ref[which, : plan.entries] = jnp.concatenate(pieces, axis=1)
        rest_ref[which, plan.entries :] = jnp.zeros((plan.tail, LANES), F32)
    for k, partner in enumerate(plan.partners):
        target = rank ^ partner
        tile = target // plan.halves
        half = target % plan.halves
        lanes = pl.ds(pl.multiple_of(tile * LANES, LANES), LANES)
        for which, source in enumerate(sources):
            parts = []
            for e in range(plan.energies):
                for z in range(2):
                    whole = source[e, 0, z, :, lanes].astype(F32)
                    part = whole[: plan.rows]
                    for other in range(1, plan.halves):
                        piece = whole[other * plan.rows : (other + 1) * plan.rows]
                        part = jnp.where(half == other, piece, part)
                    parts.append(part)
            parts.append(rest_ref[which, pl.ds(target * plan.rest_rows, plan.tail), :])
            outs[k][which] = jnp.concatenate(parts, axis=0).astype(BF16)


def bond_of(plan, shape):
    column = lax.broadcasted_iota(jnp.int32, shape, len(shape) - 1)
    atom = jnp.floor((column.astype(F32) + 0.5) * (1.0 / plan.bonds)).astype(jnp.int32)
    return column - atom * plan.bonds


def atom_table(plan):
    atom = lax.broadcasted_iota(jnp.int32, (plan.atoms, plan.columns), 0)
    column = lax.broadcasted_iota(jnp.int32, (plan.atoms, plan.columns), 1)
    inside = column - atom * plan.bonds
    return jnp.where((inside >= 0) & (inside < plan.bonds), 1.0, 0.0).astype(BF16)


def mode_table(plan, energy_ref, momentum_ref, absorb_ref):
    width = plan.devices * 8
    modes = plan.devices * plan.modes
    label = (energy_ref[...] - 1) * plan.all_momenta + momentum_ref[...]
    stacked = jnp.concatenate(
        [label.astype(F32), absorb_ref[...], jnp.zeros((6, modes), F32)], axis=0
    )
    mode = lax.broadcasted_iota(jnp.int32, (modes, width), 0)
    column = lax.broadcasted_iota(jnp.int32, (modes, width), 1)
    inner = (column & 3) >> 1
    chosen = (mode == (column >> 3) * plan.modes + inner) & (inner < plan.modes)
    spread = jnp.dot(
        stacked, jnp.where(chosen, 1.0, 0.0), precision=HIGH, preferred_element_type=F32
    )
    label = (spread[:1] + 0.5).astype(jnp.int32)
    column = lax.broadcasted_iota(jnp.int32, (2 * plan.classes, width), 1)
    row = lax.broadcasted_iota(jnp.int32, (2 * plan.classes, width), 0)
    hit = (label == (row >> 1)) & ((column & 1) == (row & 1))
    hit = hit & (((column & 3) >> 1) < plan.modes)
    blocks = []
    for kind in range(2):
        here = hit & (((column >> 2) & 1) == kind)
        blocks.append(jnp.where(here, 1.0, 0.0))
        blocks.append(jnp.where(here, spread[1:2], 0.0))
    return jnp.concatenate(blocks, axis=0)


def couple_kernel(
    plan, less_ref, dirs_ref, energy_ref, momentum_ref, absorb_ref, out_ref, table_ref, pair_ref, held_ref
):
    bonds, width = plan.bonds, plan.width
    held_ref[...] = jnp.zeros(held_ref.shape, F32)
    for n in range(bonds):
        pairs = [dirs_ref[n, i : i + 1] * dirs_ref[n, j : j + 1] for i in range(3) for j in range(3)]
        for way, (i, j) in enumerate((i, j) for i in range(3) for j in range(i, 3)):
            pair_ref[way, n : n + 1] = pairs[3 * i + j]
        for m in range(plan.modes):
            total = less_ref[m, 0, n] * pairs[0]
            for t in range(1, 9):
                total = total + less_ref[m, t, n] * pairs[t]
            row = (m * bonds + n) * 2
            held_ref[row : row + 2] = total
    rows = held_ref.shape[0]
    spread = jnp.dot(held_ref[...].astype(BF16), atom_table(plan), preferred_element_type=F32)
    row = lax.broadcasted_iota(jnp.int32, (rows, 1), 0)
    bond = (row >> 1) - jnp.where(row >= 2 * bonds, bonds, 0)
    keep = bond == bond_of(plan, (1, plan.columns))
    kept = jnp.where(keep, spread, 0.0).astype(BF16)
    line = lax.broadcasted_iota(jnp.int32, (8, rows), 0)
    row = lax.broadcasted_iota(jnp.int32, (8, rows), 1)
    owner = jnp.where(row >= 2 * bonds, 2, 0) + (row & 1)
    gather = jnp.where((line == owner) & (row < 2 * bonds * plan.modes), 1.0, 0.0).astype(BF16)
    flat = jnp.dot(gather, kept, preferred_element_type=F32)[:4]
    for p in range(plan.n_phonon):
        start = p * width
        rest = flat[:, start + plan.tiles * LANES : start + width]
        rest = jnp.concatenate([rest, jnp.zeros((4, LANES - plan.rest), F32)], axis=1)
        for tile in range(plan.tiles):
            main = flat[:, start + tile * LANES : start + (tile + 1) * LANES]
            block = jnp.concatenate([main, rest], axis=0)
            for half in range(plan.halves):
                out_ref[(tile * plan.halves + half) * plan.n_phonon + p] = block
    table_ref[...] = mode_table(plan, energy_ref, momentum_ref, absorb_ref)


def place_of(plan, source, e, z):
    energy = plan.energies * (source // plan.n_momentum) + e
    return (energy * plan.all_momenta + source % plan.n_momentum) * 2 + z


def stage_blocks(plan, rank, which, messages, held_ref):
    row = lax.broadcasted_iota(jnp.int32, (plan.rest_pad, LANES), 0)
    for partner, message in zip(plan.partners, messages):
        source = rank ^ partner
        values = message[which].astype(F32)
        tail = values[plan.main_rows : plan.main_rows + plan.rest_pad]
        tail = jnp.where(row < plan.rest_rows, tail, 0.0)
        for e in range(plan.energies):
            for z in range(2):
                slab = 2 * e + z
                place = place_of(plan, source, e, z)
                held_ref[place, : plan.rows] = values[slab * plan.rows : (slab + 1) * plan.rows]
                turned = tail if slab == 0 else pltpu.roll(tail, LANES - slab * plan.rest, 1)
                held_ref[place, plan.rows :] = turned


def polar_kernel(plan, rank_ref, table_ref, *refs):
    messages = refs[: plan.group]
    out_ref, low_ref, high_ref = refs[plan.group :]
    rank = rank_ref[0]
    stage_blocks(plan, rank, 0, messages, low_ref)
    stage_blocks(plan, rank, 1, messages, high_ref)
    count, momenta = plan.all_energies, plan.all_momenta

    def step(chunk, sums):
        rows = pl.ds(pl.multiple_of(chunk * 8, 8), 8)
        sums = list(sums)
        for energy_step in range(1, REACH + 1):
            for q in range(momenta):
                index = ((energy_step - 1) * momenta + q) * 2
                for energy in range(energy_step, count):
                    for k in range(momenta):
                        low = (energy * momenta + k) * 2
                        high = ((energy - energy_step) * momenta + (k - q) % momenta) * 2
                        low_re, low_im = low_ref[low, rows], low_ref[low + 1, rows]
                        high_re, high_im = high_ref[high, rows], high_ref[high + 1, rows]
                        sums[index] = sums[index] + (low_re * high_re + low_im * high_im)
                        sums[index + 1] = sums[index + 1] + (low_im * high_re - low_re * high_im)
        return tuple(sums)

    none = tuple(jnp.zeros((8, LANES), F32) for _ in range(2 * plan.classes))
    main = lax.fori_loop(0, plan.rows // 8, step, none)
    rest = lax.fori_loop(plan.rows // 8, plan.held // 8, step, none)
    scale = float(count * momenta * plan.entries) ** (-0.5)
    lines = [jnp.sum(part, axis=0, keepdims=True) * scale for part in main + rest]
    table = jnp.concatenate(lines, axis=0)
    lines = 2 * plan.classes
    picks = jnp.concatenate([table_ref[:lines], table_ref[2 * lines : 3 * lines]], axis=0)
    picked = lax.dot_general(
        picks, table, (((0,), (0,)), ((), ())), precision=HIGH, preferred_element_type=F32
    )
    out_ref[...] = picked.reshape(out_ref.shape)


def energy_kernel(plan, rank_ref, weigh_ref, coupling_ref, *refs):
    messages = refs[: plan.group]
    outs = refs[plan.group : 2 * plan.group]
    low_ref, sum_ref, weight_ref = refs[2 * plan.group :]
    rank = rank_ref[0]
    flat = coupling_ref[...].reshape(plan.devices * 8, LANES)
    weight_ref[...] = jnp.dot(weigh_ref[...], flat, precision=HIGH, preferred_element_type=F32)
    stage_blocks(plan, rank, 0, messages, low_ref)
    count, momenta = plan.all_energies, plan.all_momenta

    def run(base):
        def step(chunk, carry):
            rows = pl.ds(pl.multiple_of(chunk * 8, 8), 8)
            re = [None] * (count * momenta)
            im = [None] * (count * momenta)
            for energy_step in range(1, REACH + 1):
                for q in range(momenta):
                    index = base + ((energy_step - 1) * momenta + q) * 2
                    pairs = []
                    for part, sign in ((0, -1), (1, 1)):
                        at = index + part * 2 * plan.classes
                        w_re = jnp.broadcast_to(weight_ref[at : at + 1], (8, LANES))
                        w_im = jnp.broadcast_to(weight_ref[at + 1 : at + 2], (8, LANES))
                        pairs.append((sign, w_re, w_im))
                    for energy in range(count):
                        for k in range(momenta):
                            slot = energy * momenta + k
                            for sign, w_re, w_im in pairs:
                                other = energy + sign * energy_step
                                if other < 0 or other >= count:
                                    continue
                                at = (other * momenta + (k + sign * q) % momenta) * 2
                                b_re, b_im = low_ref[at, rows], low_ref[at + 1, rows]
                                t_re = w_re * b_re - w_im * b_im
                                t_im = w_re * b_im + w_im * b_re
                                re[slot] = t_re if re[slot] is None else re[slot] + t_re
                                im[slot] = t_im if im[slot] is None else im[slot] + t_im
            for slot in range(count * momenta):
                sum_ref[2 * slot, rows] = re[slot]
                sum_ref[2 * slot + 1, rows] = im[slot]
            return carry

        return step

    lax.fori_loop(0, plan.rows // 8, run(0), 0)
    lax.fori_loop(plan.rows // 8, plan.held // 8, run(4 * plan.classes), 0)
    lane = lax.broadcasted_iota(jnp.int32, (plan.rest_pad, LANES), 1)
    for k, partner in enumerate(plan.partners):
        target = rank ^ partner
        parts = []
        tail = jnp.zeros((plan.rest_pad, LANES), F32)
        for e in range(plan.energies):
            for z in range(2):
                slab = 2 * e + z
                place = place_of(plan, target, e, z)
                parts.append(sum_ref[place, : plan.rows])
                piece = sum_ref[place, plan.rows :]
                if slab:
                    piece = pltpu.roll(piece, slab * plan.rest, 1)
                mine = (lane >= slab * plan.rest) & (lane < (slab + 1) * plan.rest)
                tail = jnp.where(mine, piece, tail)
        parts.append(tail)
        if plan.tail > plan.rest_pad:
            parts.append(jnp.zeros((plan.tail - plan.rest_pad, LANES), F32))
        outs[k][...] = jnp.concatenate(parts, axis=0).astype(BF16)


def gather_kernel(plan, rank_ref, *refs):
    messages = refs[: plan.group]
    out_ref, wide_ref, rest_ref = refs[plan.group :]
    rank = rank_ref[0]
    for partner, message in zip(plan.partners, messages):
        source = rank ^ partner
        tile = source // plan.halves
        half = source % plan.halves
        values = message[...].astype(F32)
        lanes = pl.ds(pl.multiple_of(tile * LANES, LANES), LANES)
        rows = pl.ds(pl.multiple_of(half * plan.rows, 8), plan.rows)
        tail = values[plan.main_rows : plan.main_rows + plan.rest_pad]
        for slab in range(plan.slabs):
            wide_ref[slab, rows, lanes] = values[slab * plan.rows : (slab + 1) * plan.rows]
            turned = tail if slab == 0 else pltpu.roll(tail, LANES - slab * plan.rest, 1)
            rest_ref[slab, source] = turned
    for e in range(plan.energies):
        for z in range(2):
            slab = 2 * e + z
            parts = [rest_ref[slab, source, : plan.rest_rows] for source in range(plan.group)]
            rest = jnp.concatenate(parts, axis=0)[:, : plan.rest]
            whole = jnp.concatenate([wide_ref[slab], rest], axis=1)
            out_ref[e, 0, z] = whole.astype(BF16)


def next_kernel(plan, polar_ref, ret_ref, near_ref, pair_ref, out_ref, v_ref, dense_ref):
    bonds, atoms, order = plan.bonds, plan.atoms, plan.order
    padded = -(-bonds // 8) * 8
    lines = []
    for p in range(plan.n_phonon):
        rest = jnp.zeros((4, LANES), F32)
        for tile in range(plan.tiles):
            main = jnp.zeros((4, LANES), F32)
            for half in range(plan.halves):
                block = polar_ref[(tile * plan.halves + half) * plan.n_phonon + p]
                main = main + block[:4]
                rest = rest + block[4:]
            lines.append(main)
        lines.append(rest[:, : plan.rest])
    flat = jnp.concatenate(lines, axis=1)
    bond = lax.broadcasted_iota(jnp.int32, (padded, 1), 0)
    keep = bond == bond_of(plan, (1, plan.columns))
    tall = jnp.concatenate(
        [jnp.where(keep, flat[row : row + 1], 0.0) for row in range(2 * plan.modes)], axis=0
    )
    upper = tall.astype(BF16)
    lower = (tall - upper.astype(F32)).astype(BF16)
    contract = (((1,), (1,)), ((), ()))
    both = lax.dot_general(
        jnp.concatenate([upper, lower], axis=0), atom_table(plan), contract, preferred_element_type=F32
    )
    by_bond = both[: tall.shape[0]] + both[tall.shape[0] :]
    ways = [(i, j) for i in range(3) for j in range(i, 3)]
    for way in range(len(ways)):
        for row in range(2 * plan.modes):
            values = by_bond[row * padded : row * padded + bonds]
            v_ref[row * len(ways) + way, :bonds] = values * pair_ref[way]

    def step(chunk, carry):
        first = pl.multiple_of(chunk * 16, 16)
        number = lax.broadcasted_iota(jnp.int32, (16, atoms), 0) + first
        for row in range(2 * plan.modes):
            sums = [jnp.zeros((16, atoms), F32) for _ in ways]
            for n in range(bonds):
                hit = number == near_ref[n : n + 1]
                for way in range(len(ways)):
                    value = v_ref[row * len(ways) + way, n : n + 1]
                    sums[way] = sums[way] + jnp.where(hit, value, 0.0)
            for way, (i, j) in enumerate(ways):
                block = sums[way].astype(BF16)
                dense_ref[
                    row, pl.ds(pl.multiple_of(j * atoms + first, 16), 16), i * atoms : (i + 1) * atoms
                ] = block
                if i != j:
                    dense_ref[
                        row,
                        pl.ds(pl.multiple_of(i * atoms + first, 16), 16),
                        j * atoms : (j + 1) * atoms,
                    ] = block
        return carry

    lax.fori_loop(0, atoms // 16, step, 0)
    plain = (((1,), (0,)), ((), ()))
    for m in range(plan.modes):
        ret_re, ret_im = ret_ref[m, 0], ret_ref[m, 1]
        dense_re, dense_im = dense_ref[2 * m], dense_ref[2 * m + 1]

        def times(left, right, how):
            return lax.dot_general(left, right, how, preferred_element_type=F32)

        half_re = (times(ret_re, dense_re, plain) + times(ret_im, dense_im, plain)).astype(BF16)
        half_im = (times(ret_re, dense_im, plain) - times(ret_im, dense_re, plain)).astype(BF16)
        next_re = times(ret_re, half_re, contract) - times(ret_im, half_im, contract)
        next_im = times(ret_re, half_im, contract) + times(ret_im, half_re, contract)
        out_ref[m, 0] = next_re.astype(BF16)
        out_ref[m, 1] = next_im.astype(BF16)


def exchange(plan, blocks):
    moved = [blocks[0]]
    for partner, block in zip(plan.partners[1:], blocks[1:]):
        moved.append(lax.ppermute(block, GROUP, [(i, i ^ partner) for i in range(plan.group)]))
    return moved


def dealt(
    plan, g_less, g_great, d_less, d_ret, neighbours, bond_dirs, energy_offset, momentum_offset, absorb
):
    rank = lax.axis_index(GROUP).astype(jnp.int32).reshape(1)
    group, held = plan.group, plan.held
    slots = plan.all_energies * plan.all_momenta * 2
    lines = 2 * plan.classes
    modes = plan.devices * plan.modes

    message = jax.ShapeDtypeStruct((2, plan.message, LANES), BF16)
    blocks = call(
        functools.partial(deal_kernel, plan), [message] * group, rank, g_less, g_great,
        scalars=1, scratch=[pltpu.VMEM((2, plan.entries + plan.tail, LANES), F32)],
        moved=4 * g_less.size * 2,
    )
    own, d_less, bond_dirs = lax.optimization_barrier((blocks[0], d_less, bond_dirs))
    blocks = exchange(plan, [own] + list(blocks[1:]))
    small = jax.ShapeDtypeStruct((plan.devices, 8, LANES), F32)
    coupling, table, pairs = call(
        functools.partial(couple_kernel, plan),
        [
            small,
            jax.ShapeDtypeStruct((4 * lines, plan.devices * 8), F32),
            jax.ShapeDtypeStruct((6, plan.bonds, plan.atoms), F32),
        ],
        d_less.transpose(0, 2, 3, 1, 4), bond_dirs.transpose(1, 0, 2),
        energy_offset.reshape(1, modes), momentum_offset.reshape(1, modes), absorb.reshape(1, modes),
        scratch=[pltpu.VMEM((-(-2 * plan.bonds * plan.modes // 16) * 16, plan.atoms), F32)],
        moved=4 * d_less.size,
    )
    coupling = lax.all_to_all(coupling, EVERY, 0, 0, tiled=True)
    block_scratch = pltpu.VMEM((slots, held, LANES), F32)
    polar = call(
        functools.partial(polar_kernel, plan), small, rank, table, *blocks,
        scalars=1, scratch=[block_scratch] * 2, moved=8 * 2**20,
    )
    polar = lax.all_to_all(polar, EVERY, 0, 0, tiled=True)
    answer = jax.ShapeDtypeStruct((plan.message, LANES), BF16)
    sums = call(
        functools.partial(energy_kernel, plan), [answer] * group, rank, table, coupling, *blocks,
        scalars=1,
        scratch=[block_scratch, block_scratch, pltpu.VMEM((4 * lines, LANES), F32)],
        moved=8 * 2**20,
    )
    sums = exchange(plan, sums)
    padded = -(-plan.bonds // 8) * 8
    d_next = call(
        functools.partial(next_kernel, plan), jax.ShapeDtypeStruct(d_ret.shape, BF16),
        polar, d_ret, neighbours, pairs,
        scratch=[
            pltpu.VMEM((12 * plan.modes, padded, plan.atoms), F32),
            pltpu.VMEM((2 * plan.modes, plan.order, plan.order), BF16),
        ],
        moved=20 * 2**20,
    )
    d_next, own = lax.optimization_barrier((d_next, sums[0]))
    self_energy = call(
        functools.partial(gather_kernel, plan), jax.ShapeDtypeStruct(g_less.shape, BF16), rank,
        own, *sums[1:],
        scalars=1,
        scratch=[
            pltpu.VMEM((plan.slabs, plan.entries, plan.tiles * LANES), F32),
            pltpu.VMEM((plan.slabs, group, plan.rest_pad, LANES), F32),
        ],
        moved=4 * 2**20,
    )
    return self_energy, d_next


def local(*arrays):
    plan = Plan(
        arrays[0].shape, arrays[2].shape, arrays[3].shape,
        lax.axis_size("energy"), lax.axis_size("momentum"), lax.axis_size("phonon"),
    )
    return dealt(plan, *arrays) if plan.fits() else general(*arrays)


def solution(mesh):
    in_specs = (
        P("energy", "momentum", None, None, "phonon"),
        P("energy", "momentum", None, None, "phonon"),
        P(("energy", "momentum", "phonon"), None, None, None, None),
        P(("energy", "momentum", "phonon"), None, None, None),
        P(),
        P(),
        P(),
        P(),
        P(),
    )
    out_specs = (
        P("energy", "momentum", None, None, "phonon"),
        P(("energy", "momentum", "phonon"), None, None, None),
    )
    return jax.shard_map(local, mesh=mesh, in_specs=in_specs, out_specs=out_specs, check_vma=False)
```

```python
import functools

import jax
import jax.numpy as jnp
from jax import lax
from jax.experimental import pallas as pl
from jax.experimental.pallas import tpu as pltpu
from jax.sharding import PartitionSpec as P

ORB = 12
REACH = 4
LANES = 128


HIGH = lax.Precision.HIGHEST


def shifted_2(block, axis, distance):
    devices = range(lax.axis_size(axis))
    route = [(i - distance, i) for i in devices if i - distance in devices]
    return lax.ppermute(block, axis, route)


def scaled_blocks(weights, blocks):
    real_w = weights[None, :, :, 0, None, :]
    imag_w = weights[None, :, :, 1, None, :]
    real_b = blocks[:, None, :, 0].astype(jnp.float32)
    imag_b = blocks[:, None, :, 1].astype(jnp.float32)
    real_part = jnp.sum(real_w * real_b - imag_w * imag_b, axis=2)
    imag_part = jnp.sum(real_w * imag_b + imag_w * real_b, axis=2)
    return jnp.stack([real_part, imag_part], axis=2)


def inner_sums(local_blocks, shifted):
    local_real = local_blocks[:, :, 0].astype(jnp.float32)[:, :, None]
    local_imag = local_blocks[:, :, 1].astype(jnp.float32)[:, :, None]
    other_real = shifted[:, :, 0].astype(jnp.float32)[:, None]
    other_imag = shifted[:, :, 1].astype(jnp.float32)[:, None]
    real_sum = jnp.sum(local_real * other_real + local_imag * other_imag, axis=(0, 3))
    imag_sum = jnp.sum(local_imag * other_real - local_real * other_imag, axis=(0, 3))
    return jnp.stack([real_sum, imag_sum], axis=2)


def times_adjoint(left, right):
    return jnp.einsum("mab,mcb->mac", left, right, preferred_element_type=jnp.float32)


def times_plain(left, right):
    return jnp.einsum("mab,mbc->mac", left, right, preferred_element_type=jnp.float32)


def general(
    g_less, g_great, d_less, d_ret, neighbours, bond_dirs, energy_offset, momentum_offset, absorb
):
    energies = g_less.shape[0]
    momenta_here = g_less.shape[1]
    local_width = g_less.shape[4]
    bonds = d_less.shape[3]
    whole_atoms = d_less.shape[4]
    atom_share = local_width // bonds
    all_momenta = momenta_here * lax.axis_size("momentum")
    all_energies = energies * lax.axis_size("energy")
    modes_here = d_less.shape[0]
    order = d_ret.shape[2]
    classes = REACH * all_momenta
    energy_rank = lax.axis_index("energy")
    momentum_rank = lax.axis_index("momentum")
    phonon_rank = lax.axis_index("phonon")
    span = -(-REACH // energies)
    lower_steps = list(range(span, 0, -1))
    both_steps = lower_steps + list(range(-1, -span - 1, -1))
    label = (energy_offset - 1) * all_momenta + momentum_offset
    table = (label[:, None] == jnp.arange(classes, dtype=jnp.int32)[None, :]).astype(jnp.float32)
    soaked = table * absorb[:, None]
    pair_cube = bond_dirs[:, None] * bond_dirs[None, :]
    pair = pair_cube.reshape((9,) + bond_dirs.shape[1:])
    coupling = jnp.sum(d_less * pair[None, None], axis=2)
    first_mode = (
        (energy_rank * lax.axis_size("momentum") + momentum_rank) * lax.axis_size("phonon")
        + phonon_rank
    ) * modes_here
    own_table = lax.dynamic_slice_in_dim(table, first_mode, modes_here, 0)
    spread = lax.all_to_all(
        coupling.astype(jnp.bfloat16), "phonon", split_axis=3, concat_axis=0, tiled=True
    ).astype(coupling.dtype)
    blank = jnp.zeros((classes, 2 * bonds * atom_share), jnp.float32)
    piece = lax.all_gather(
        spread.astype(jnp.bfloat16), ("energy", "momentum"), axis=0, tiled=True
    ).astype(jnp.float32)
    rows = piece.shape[0]
    flat_piece = piece.reshape(rows, -1)
    emitted = blank + jnp.einsum("mc,mx->cx", table, flat_piece, precision=HIGH)
    absorbed = blank + jnp.einsum("mc,mx->cx", soaked, flat_piece, precision=HIGH)
    emitted = emitted.reshape(classes, 2, bonds, atom_share)
    absorbed = absorbed.reshape(classes, 2, bonds, atom_share)
    emit_table = emitted.transpose(0, 1, 3, 2).reshape(REACH, all_momenta, 2, local_width)
    soak_table = absorbed.transpose(0, 1, 3, 2).reshape(REACH, all_momenta, 2, local_width)
    moved = [shifted_2(g_less, "energy", step) for step in both_steps]
    lower = jnp.concatenate(moved[:span], axis=0)
    upper = jnp.concatenate(moved[span:], axis=0)
    lesser_rimmed = jnp.concatenate([lower, g_less, upper], axis=0)
    greater_moved = [shifted_2(g_great, "energy", step) for step in lower_steps]
    greater_rim = jnp.concatenate(greater_moved, axis=0)
    greater_rimmed = jnp.concatenate([greater_rim, g_great], axis=0)
    lesser_wide, greater_wide = (
        lax.all_gather(lesser_rimmed, "momentum", axis=1, tiled=True),
        lax.all_gather(greater_rimmed, "momentum", axis=1, tiled=True),
    )
    here_moment = momentum_rank * momenta_here + jnp.arange(momenta_here, dtype=jnp.int32)
    every_moment = jnp.arange(all_momenta, dtype=jnp.int32)
    behind = (here_moment[:, None] - every_moment[None, :]) % all_momenta
    ahead = (every_moment[None, :] - here_moment[:, None]) % all_momenta
    pick_behind = (behind[:, :, None] == every_moment[None, None, :]).astype(jnp.float32)
    pick_ahead = (ahead[:, :, None] == every_moment[None, None, :]).astype(jnp.float32)
    total = jnp.zeros(g_less.shape, jnp.float32)
    polar_parts = []
    for energy_step in range(1, REACH + 1):
        below = lesser_wide[REACH - energy_step : REACH - energy_step + energies]
        above = lesser_wide[REACH + energy_step : REACH + energy_step + energies]
        weight_below = jnp.einsum(
            "lkq,qzx->lkzx", pick_behind, emit_table[energy_step - 1], precision=HIGH
        )
        weight_above = jnp.einsum(
            "lkq,qzx->lkzx", pick_ahead, soak_table[energy_step - 1], precision=HIGH
        )
        total = total + scaled_blocks(weight_below, below) + scaled_blocks(weight_above, above)
        earlier = greater_wide[REACH - energy_step : REACH - energy_step + energies]
        pairs = inner_sums(g_less, earlier)
        polar_parts.append(jnp.einsum("lkq,lkzx->qzx", pick_behind, pairs, precision=HIGH))
    self_energy = total.astype(jnp.bfloat16)
    scale = float(all_energies * all_momenta * ORB * ORB) ** (-0.5)
    polar_local = jnp.stack(polar_parts).reshape(classes, 2, local_width) * scale
    polar_summed = lax.psum(polar_local, ("energy", "momentum"))
    polar_full = lax.all_gather(polar_summed, "phonon", axis=2, tiled=True)
    own_polar = jnp.einsum("mc,czx->mzx", own_table, polar_full, precision=HIGH)
    own_polar = own_polar.reshape(modes_here, 2, whole_atoms, bonds).transpose(0, 1, 3, 2)
    link = (
        neighbours[:, :, None] == jnp.arange(whole_atoms, dtype=jnp.int32)[None, None, :]
    ).astype(jnp.float32)
    weighted = pair_cube[None, None] * own_polar[:, :, None, None]
    dense = jnp.einsum("mzijna,nab->mziajb", weighted, link, precision=HIGH)
    dense = dense.reshape(modes_here, 2, order, order).astype(jnp.bfloat16)
    dense_re, dense_im = (dense[:, 0], dense[:, 1])
    ret_re, ret_im = (d_ret[:, 0], d_ret[:, 1])
    half_re = (times_adjoint(dense_re, ret_re) + times_adjoint(dense_im, ret_im)).astype(
        jnp.bfloat16
    )
    half_im = (times_adjoint(dense_im, ret_re) - times_adjoint(dense_re, ret_im)).astype(
        jnp.bfloat16
    )
    next_re = times_plain(ret_re, half_re) - times_plain(ret_im, half_im)
    next_im = times_plain(ret_re, half_im) + times_plain(ret_im, half_re)
    d_next = jnp.stack([next_re, next_im], axis=1).astype(jnp.bfloat16)
    return (self_energy, d_next)


EVERY = ("energy", "momentum", "phonon")
F32 = jnp.float32
BF16 = jnp.bfloat16


class Plan:
    def __init__(self, g_shape, d_shape, ret_shape, n_energy, n_momentum, n_phonon):
        self.energies, self.momenta, _, self.entries, self.width = g_shape
        self.modes, _, _, self.bonds, self.atoms = d_shape
        self.order = ret_shape[2]
        self.n_energy = n_energy
        self.n_momentum = n_momentum
        self.n_phonon = n_phonon
        self.devices = n_energy * n_momentum * n_phonon
        self.all_energies = self.energies * n_energy
        self.all_momenta = self.momenta * n_momentum
        self.classes = REACH * self.all_momenta
        self.slabs = 2 * self.energies
        self.tiles = self.width // LANES
        self.rest = self.width % LANES
        self.rest_rows = self.entries // n_energy
        self.main_rows = self.slabs * self.entries
        self.rest_pad = -(-self.rest_rows // 8) * 8
        self.message = -(-(self.main_rows + self.rest_pad) // 16) * 16
        self.tail = self.message - self.main_rows
        self.held = self.entries + self.rest_pad
        self.columns = self.width * n_phonon

    def fits(self):
        return (
            self.momenta == 1
            and self.all_momenta == 2
            and self.n_energy == self.tiles
            and self.n_energy & (self.n_energy - 1) == 0
            and self.entries % 16 == 0
            and self.entries % self.n_energy == 0
            and self.rest > 0
            and self.slabs * self.rest == LANES
            and self.modes <= 2
            and self.atoms == LANES
            and self.order == 3 * self.atoms
            and self.all_energies <= 8
        )


def call(kernel, out_shape, *operands, scratch=(), scalars=0, flops=0, moved=0):
    smem = pl.BlockSpec(memory_space=pltpu.SMEM)
    vmem = pl.BlockSpec(memory_space=pltpu.VMEM)
    specs = [smem] * scalars + [vmem] * (len(operands) - scalars)
    many = isinstance(out_shape, (list, tuple))
    return pl.pallas_call(
        kernel,
        out_shape=out_shape,
        in_specs=specs,
        out_specs=[vmem] * len(out_shape) if many else vmem,
        scratch_shapes=list(scratch),
        compiler_params=pltpu.CompilerParams(vmem_limit_bytes=48 * 2**20),
        cost_estimate=pl.CostEstimate(flops=flops, bytes_accessed=moved, transcendentals=0),
    )(*operands)


def deal_kernel(plan, rank_ref, source_ref, *refs):
    outs, rest_ref = refs[: plan.n_energy], refs[plan.n_energy]
    rank = rank_ref[0]
    slabs = [(e, z) for e in range(plan.energies) for z in range(2)]
    pieces = [source_ref[e, 0, z, :, plan.tiles * LANES :].astype(F32) for e, z in slabs]
    rest_ref[: plan.entries] = jnp.concatenate(pieces, axis=1)
    rest_ref[plan.entries :] = jnp.zeros((plan.tail, LANES), F32)
    for partner in range(plan.n_energy):
        target = rank ^ partner
        lanes = pl.ds(pl.multiple_of(target * LANES, LANES), LANES)
        for slab, (e, z) in enumerate(slabs):
            rows = slice(slab * plan.entries, (slab + 1) * plan.entries)
            outs[partner][rows] = source_ref[e, 0, z, :, lanes]
        rest = rest_ref[pl.ds(target * plan.rest_rows, plan.tail), :]
        outs[partner][plan.main_rows :] = rest.astype(BF16)


def bond_of(plan, shape):
    column = lax.broadcasted_iota(jnp.int32, shape, len(shape) - 1)
    atom = jnp.floor((column.astype(F32) + 0.5) * (1.0 / plan.bonds)).astype(jnp.int32)
    return column - atom * plan.bonds


def atom_table(plan):
    atom = lax.broadcasted_iota(jnp.int32, (plan.atoms, plan.columns), 0)
    column = lax.broadcasted_iota(jnp.int32, (plan.atoms, plan.columns), 1)
    inside = column - atom * plan.bonds
    return jnp.where((inside >= 0) & (inside < plan.bonds), 1.0, 0.0).astype(BF16)


def mode_table(plan, energy_ref, momentum_ref, absorb_ref):
    width = plan.devices * 8
    modes = plan.devices * plan.modes
    label = (energy_ref[...] - 1) * plan.all_momenta + momentum_ref[...]
    stacked = jnp.concatenate(
        [label.astype(F32), absorb_ref[...], jnp.zeros((6, modes), F32)], axis=0
    )
    mode = lax.broadcasted_iota(jnp.int32, (modes, width), 0)
    column = lax.broadcasted_iota(jnp.int32, (modes, width), 1)
    inner = (column & 3) >> 1
    chosen = (mode == (column >> 3) * plan.modes + inner) & (inner < plan.modes)
    spread = jnp.dot(
        stacked, jnp.where(chosen, 1.0, 0.0), precision=HIGH, preferred_element_type=F32
    )
    label = (spread[:1] + 0.5).astype(jnp.int32)
    column = lax.broadcasted_iota(jnp.int32, (2 * plan.classes, width), 1)
    row = lax.broadcasted_iota(jnp.int32, (2 * plan.classes, width), 0)
    hit = (label == (row >> 1)) & ((column & 1) == (row & 1))
    hit = hit & (((column & 3) >> 1) < plan.modes)
    blocks = []
    for kind in range(2):
        here = hit & (((column >> 2) & 1) == kind)
        blocks.append(jnp.where(here, 1.0, 0.0))
        blocks.append(jnp.where(here, spread[1:2], 0.0))
    return jnp.concatenate(blocks, axis=0)


def couple_kernel(
    plan, less_ref, dirs_ref, energy_ref, momentum_ref, absorb_ref, out_ref, table_ref, pair_ref, held_ref
):
    bonds, width = plan.bonds, plan.width
    held_ref[...] = jnp.zeros(held_ref.shape, F32)
    for n in range(bonds):
        pairs = [dirs_ref[n, i : i + 1] * dirs_ref[n, j : j + 1] for i in range(3) for j in range(3)]
        for way, (i, j) in enumerate((i, j) for i in range(3) for j in range(i, 3)):
            pair_ref[way, n : n + 1] = pairs[3 * i + j]
        for m in range(plan.modes):
            total = less_ref[m, 0, n] * pairs[0]
            for t in range(1, 9):
                total = total + less_ref[m, t, n] * pairs[t]
            row = (m * bonds + n) * 2
            held_ref[row : row + 2] = total
    rows = held_ref.shape[0]
    spread = jnp.dot(held_ref[...].astype(BF16), atom_table(plan), preferred_element_type=F32)
    row = lax.broadcasted_iota(jnp.int32, (rows, 1), 0)
    bond = (row >> 1) - jnp.where(row >= 2 * bonds, bonds, 0)
    keep = bond == bond_of(plan, (1, plan.columns))
    kept = jnp.where(keep, spread, 0.0).astype(BF16)
    line = lax.broadcasted_iota(jnp.int32, (8, rows), 0)
    row = lax.broadcasted_iota(jnp.int32, (8, rows), 1)
    owner = jnp.where(row >= 2 * bonds, 2, 0) + (row & 1)
    gather = jnp.where((line == owner) & (row < 2 * bonds * plan.modes), 1.0, 0.0).astype(BF16)
    flat = jnp.dot(gather, kept, preferred_element_type=F32)[:4]
    for p in range(plan.n_phonon):
        start = p * width
        rest = flat[:, start + plan.tiles * LANES : start + width]
        rest = jnp.concatenate([rest, jnp.zeros((4, LANES - plan.rest), F32)], axis=1)
        for tile in range(plan.tiles):
            main = flat[:, start + tile * LANES : start + (tile + 1) * LANES]
            block = jnp.concatenate([main, rest], axis=0)
            for half in range(plan.n_momentum):
                out_ref[(tile * plan.n_momentum + half) * plan.n_phonon + p] = block
    table_ref[...] = mode_table(plan, energy_ref, momentum_ref, absorb_ref)


def stage_blocks(plan, rank, messages, held_ref, stride, offset):
    row = lax.broadcasted_iota(jnp.int32, (plan.rest_pad, LANES), 0)
    for partner, message in enumerate(messages):
        first = plan.energies * (rank ^ partner)
        tail = message[plan.main_rows :].astype(F32)[: plan.rest_pad]
        tail = jnp.where(row < plan.rest_rows, tail, 0.0)
        for e in range(plan.energies):
            for z in range(2):
                slab = 2 * e + z
                place = ((first + e) * stride + offset) * 2 + z
                rows = slice(slab * plan.entries, (slab + 1) * plan.entries)
                held_ref[place, : plan.entries] = message[rows].astype(F32)
                turned = tail if slab == 0 else pltpu.roll(tail, LANES - slab * plan.rest, 1)
                held_ref[place, plan.entries :] = turned


def polar_kernel(plan, rank_ref, table_ref, *refs):
    chips = plan.n_energy
    out_ref, low_ref, high_ref = refs[3 * chips :]
    rank = rank_ref[0]
    stage_blocks(plan, rank, refs[:chips], low_ref, 2, 0)
    stage_blocks(plan, rank, refs[chips : 2 * chips], low_ref, 2, 1)
    stage_blocks(plan, rank, refs[2 * chips : 3 * chips], high_ref, 1, 0)
    count = plan.all_energies

    def step(chunk, sums):
        rows = pl.ds(pl.multiple_of(chunk * 8, 8), 8)
        sums = list(sums)
        for energy in range(count):
            high_re, high_im = high_ref[2 * energy, rows], high_ref[2 * energy + 1, rows]
            for energy_step in range(1, REACH + 1):
                if energy + energy_step >= count:
                    continue
                for q in range(2):
                    index = ((energy_step - 1) * 2 + q) * 2
                    low = ((energy + energy_step) * 2 + q) * 2
                    low_re, low_im = low_ref[low, rows], low_ref[low + 1, rows]
                    sums[index] = sums[index] + (low_re * high_re + low_im * high_im)
                    sums[index + 1] = sums[index + 1] + (low_im * high_re - low_re * high_im)
        return tuple(sums)

    none = tuple(jnp.zeros((8, LANES), F32) for _ in range(2 * plan.classes))
    main = lax.fori_loop(0, plan.entries // 8, step, none)
    rest = lax.fori_loop(plan.entries // 8, plan.held // 8, step, none)
    scale = float(count * 2 * plan.entries) ** (-0.5)
    lines = [jnp.sum(part, axis=0, keepdims=True) * scale for part in main + rest]
    sums = jnp.concatenate(lines, axis=0)
    lines = 2 * plan.classes
    picks = jnp.concatenate([table_ref[:lines], table_ref[2 * lines : 3 * lines]], axis=0)
    picked = lax.dot_general(
        picks, sums, (((0,), (0,)), ((), ())), precision=HIGH, preferred_element_type=F32
    )
    out_ref[...] = picked.reshape(out_ref.shape)


def energy_kernel(plan, rank_ref, table_ref, coupling_ref, *refs):
    chips = plan.n_energy
    outs = refs[2 * chips : 3 * chips]
    low_ref, sum_ref, weight_ref = refs[3 * chips :]
    rank = rank_ref[0]
    flat = coupling_ref[...].reshape(plan.devices * 8, LANES)
    weight_ref[...] = jnp.dot(table_ref[...], flat, precision=HIGH, preferred_element_type=F32)
    stage_blocks(plan, rank, refs[:chips], low_ref, 2, 0)
    stage_blocks(plan, rank, refs[chips : 2 * chips], low_ref, 2, 1)
    count = plan.all_energies

    def run(base):
        def step(chunk, carry):
            rows = pl.ds(pl.multiple_of(chunk * 8, 8), 8)
            re = [None] * count
            im = [None] * count
            for energy_step in range(1, REACH + 1):
                for q in range(2):
                    index = base + ((energy_step - 1) * 2 + q) * 2
                    for part, sign in ((0, -1), (1, 1)):
                        at = index + part * 2 * plan.classes
                        w_re = jnp.broadcast_to(weight_ref[at : at + 1], (8, LANES))
                        w_im = jnp.broadcast_to(weight_ref[at + 1 : at + 2], (8, LANES))
                        for energy in range(count):
                            other = energy + sign * energy_step
                            if other < 0 or other >= count:
                                continue
                            at = (other * 2 + q) * 2
                            b_re, b_im = low_ref[at, rows], low_ref[at + 1, rows]
                            t_re = w_re * b_re - w_im * b_im
                            t_im = w_re * b_im + w_im * b_re
                            re[energy] = t_re if re[energy] is None else re[energy] + t_re
                            im[energy] = t_im if im[energy] is None else im[energy] + t_im
            for energy in range(count):
                sum_ref[2 * energy, rows] = re[energy]
                sum_ref[2 * energy + 1, rows] = im[energy]
            return carry

        return step

    lax.fori_loop(0, plan.entries // 8, run(0), 0)
    lax.fori_loop(plan.entries // 8, plan.held // 8, run(4 * plan.classes), 0)
    lane = lax.broadcasted_iota(jnp.int32, (plan.rest_pad, LANES), 1)
    for partner in range(chips):
        first = plan.energies * (rank ^ partner)
        tail = jnp.zeros((plan.rest_pad, LANES), F32)
        for slab in range(plan.slabs):
            place = 2 * first + slab
            rows = slice(slab * plan.entries, (slab + 1) * plan.entries)
            outs[partner][rows] = sum_ref[place, : plan.entries].astype(BF16)
            piece = sum_ref[place, plan.entries :]
            if slab:
                piece = pltpu.roll(piece, slab * plan.rest, 1)
            mine = (lane >= slab * plan.rest) & (lane < (slab + 1) * plan.rest)
            tail = jnp.where(mine, piece, tail)
        if plan.tail > plan.rest_pad:
            blank = jnp.zeros((plan.tail - plan.rest_pad, LANES), F32)
            tail = jnp.concatenate([tail, blank], axis=0)
        outs[partner][plan.main_rows :] = tail.astype(BF16)


def gather_kernel(plan, rank_ref, *refs):
    chips = plan.n_energy
    out_ref, rest_ref = refs[chips:]
    rank = rank_ref[0]
    for partner, message in enumerate(refs[:chips]):
        source = rank ^ partner
        lanes = pl.ds(pl.multiple_of(source * LANES, LANES), LANES)
        tail = message[plan.main_rows :].astype(F32)[: plan.rest_pad]
        for slab in range(plan.slabs):
            rows = slice(slab * plan.entries, (slab + 1) * plan.entries)
            out_ref[slab // 2, 0, slab % 2, :, lanes] = message[rows]
            turned = tail if slab == 0 else pltpu.roll(tail, LANES - slab * plan.rest, 1)
            rest_ref[slab, source] = turned
    for slab in range(plan.slabs):
        parts = [rest_ref[slab, source, : plan.rest_rows] for source in range(chips)]
        rest = jnp.concatenate(parts, axis=0)[:, : plan.rest]
        out_ref[slab // 2, 0, slab % 2, :, plan.tiles * LANES :] = rest.astype(BF16)


def next_kernel(plan, polar_ref, ret_ref, near_ref, pair_ref, out_ref, v_ref, dense_ref):
    bonds, atoms, order = plan.bonds, plan.atoms, plan.order
    padded = -(-bonds // 8) * 8
    lines = []
    for p in range(plan.n_phonon):
        rest = jnp.zeros((4, LANES), F32)
        for tile in range(plan.tiles):
            main = jnp.zeros((4, LANES), F32)
            for half in range(plan.n_momentum):
                block = polar_ref[(tile * plan.n_momentum + half) * plan.n_phonon + p]
                main = main + block[:4]
                rest = rest + block[4:]
            lines.append(main)
        lines.append(rest[:, : plan.rest])
    flat = jnp.concatenate(lines, axis=1)
    bond = lax.broadcasted_iota(jnp.int32, (padded, 1), 0)
    keep = bond == bond_of(plan, (1, plan.columns))
    tall = jnp.concatenate(
        [jnp.where(keep, flat[row : row + 1], 0.0) for row in range(2 * plan.modes)], axis=0
    )
    upper = tall.astype(BF16)
    lower = (tall - upper.astype(F32)).astype(BF16)
    contract = (((1,), (1,)), ((), ()))
    both = lax.dot_general(
        jnp.concatenate([upper, lower], axis=0), atom_table(plan), contract, preferred_element_type=F32
    )
    by_bond = both[: tall.shape[0]] + both[tall.shape[0] :]
    ways = [(i, j) for i in range(3) for j in range(i, 3)]
    for way in range(len(ways)):
        for row in range(2 * plan.modes):
            values = by_bond[row * padded : row * padded + bonds]
            v_ref[row * len(ways) + way, :bonds] = values * pair_ref[way]

    def step(chunk, carry):
        first = pl.multiple_of(chunk * 16, 16)
        number = lax.broadcasted_iota(jnp.int32, (16, atoms), 0) + first
        for row in range(2 * plan.modes):
            sums = [jnp.zeros((16, atoms), F32) for _ in ways]
            for n in range(bonds):
                hit = number == near_ref[n : n + 1]
                for way in range(len(ways)):
                    value = v_ref[row * len(ways) + way, n : n + 1]
                    sums[way] = sums[way] + jnp.where(hit, value, 0.0)
            m, z = row // 2, row % 2
            for way, (i, j) in enumerate(ways):
                block = sums[way].astype(BF16)
                other = block if z else (-sums[way]).astype(BF16)
                for up, left in {(j, i), (i, j)}:
                    place = pl.multiple_of(up * atoms + first, 16)
                    columns = left * atoms
                    dense_ref[m, pl.ds(place, 16), pl.ds(z * order + columns, atoms)] = block
                    place = pl.multiple_of(order + up * atoms + first, 16)
                    dense_ref[m, pl.ds(place, 16), pl.ds((1 - z) * order + columns, atoms)] = other
        return carry

    lax.fori_loop(0, atoms // 16, step, 0)
    for m in range(plan.modes):
        ret = jnp.concatenate([ret_ref[m, 0], ret_ref[m, 1]], axis=1)
        half = jnp.dot(ret, dense_ref[m], preferred_element_type=F32).astype(BF16)
        half_re, half_im = half[:, :order], half[:, order:]
        right = jnp.concatenate(
            [
                jnp.concatenate([half_re, -half_im], axis=1),
                jnp.concatenate([half_im, half_re], axis=1),
            ],
            axis=0,
        )
        after = lax.dot_general(ret, right, contract, preferred_element_type=F32)
        out_ref[m, 0] = after[:, :order].astype(BF16)
        out_ref[m, 1] = after[:, order:].astype(BF16)


def swap(block, axis, distance):
    return lax.ppermute(block, axis, [(i, i ^ distance) for i in range(lax.axis_size(axis))])


def to_chips(plan, blocks):
    return [blocks[0]] + [swap(blocks[k], "energy", k) for k in range(1, plan.n_energy)]


def dealt(
    plan, g_less, g_great, d_less, d_ret, neighbours, bond_dirs, energy_offset, momentum_offset, absorb
):
    rank = lax.axis_index("energy").astype(jnp.int32).reshape(1)
    chips, held, count = plan.n_energy, plan.held, plan.all_energies
    lines = 2 * plan.classes
    modes = plan.devices * plan.modes
    message = jax.ShapeDtypeStruct((plan.message, LANES), BF16)

    def deal(blocks):
        return call(
            functools.partial(deal_kernel, plan), [message] * chips, rank, blocks,
            scalars=1, scratch=[pltpu.VMEM((plan.entries + plan.tail, LANES), F32)],
            moved=4 * blocks.size,
        )

    low_blocks = deal(g_less)
    own, g_great = lax.optimization_barrier((low_blocks[0], g_great))
    low_blocks = [own] + list(low_blocks[1:])
    low = to_chips(plan, low_blocks)
    high_blocks = deal(g_great)
    own, d_less, bond_dirs = lax.optimization_barrier((high_blocks[0], d_less, bond_dirs))
    high = to_chips(plan, [own] + list(high_blocks[1:]))
    low_beside = [swap(block, "momentum", 1) for block in low]
    small = jax.ShapeDtypeStruct((plan.devices, 8, LANES), F32)
    coupling, table, pairs = call(
        functools.partial(couple_kernel, plan),
        [
            small,
            jax.ShapeDtypeStruct((4 * lines, plan.devices * 8), F32),
            jax.ShapeDtypeStruct((6, plan.bonds, plan.atoms), F32),
        ],
        d_less.transpose(0, 2, 3, 1, 4), bond_dirs.transpose(1, 0, 2),
        energy_offset.reshape(1, modes), momentum_offset.reshape(1, modes), absorb.reshape(1, modes),
        scratch=[pltpu.VMEM((-(-2 * plan.bonds * plan.modes // 16) * 16, plan.atoms), F32)],
        moved=4 * d_less.size,
    )
    coupling = lax.all_to_all(coupling, EVERY, 0, 0, tiled=True)
    low_scratch = pltpu.VMEM((4 * count, held, LANES), F32)
    half_scratch = pltpu.VMEM((2 * count, held, LANES), F32)
    polar = call(
        functools.partial(polar_kernel, plan), small, rank, table, *low, *low_beside, *high,
        scalars=1, scratch=[low_scratch, half_scratch], moved=8 * 2**20,
    )
    polar = lax.all_to_all(polar, EVERY, 0, 0, tiled=True)
    sums = call(
        functools.partial(energy_kernel, plan), [message] * chips,
        rank, table, coupling, *low, *low_beside,
        scalars=1, scratch=[low_scratch, half_scratch, pltpu.VMEM((4 * lines, LANES), F32)],
        moved=8 * 2**20,
    )
    sums = to_chips(plan, sums)
    padded = -(-plan.bonds // 8) * 8
    d_next = call(
        functools.partial(next_kernel, plan), jax.ShapeDtypeStruct(d_ret.shape, BF16),
        polar, d_ret, neighbours, pairs,
        scratch=[
            pltpu.VMEM((12 * plan.modes, padded, plan.atoms), F32),
            pltpu.VMEM((plan.modes, 2 * plan.order, 2 * plan.order), BF16),
        ],
        moved=20 * 2**20,
    )
    d_next, own = lax.optimization_barrier((d_next, sums[0]))
    self_energy = call(
        functools.partial(gather_kernel, plan), jax.ShapeDtypeStruct(g_less.shape, BF16), rank,
        own, *sums[1:],
        scalars=1, scratch=[pltpu.VMEM((plan.slabs, chips, plan.rest_pad, LANES), F32)],
        moved=4 * 2**20,
    )
    return self_energy, d_next


def local(*arrays):
    plan = Plan(
        arrays[0].shape, arrays[2].shape, arrays[3].shape,
        lax.axis_size("energy"), lax.axis_size("momentum"), lax.axis_size("phonon"),
    )
    return dealt(plan, *arrays) if plan.fits() else general(*arrays)


def solution(mesh):
    in_specs = (
        P("energy", "momentum", None, None, "phonon"),
        P("energy", "momentum", None, None, "phonon"),
        P(("energy", "momentum", "phonon"), None, None, None, None),
        P(("energy", "momentum", "phonon"), None, None, None),
        P(),
        P(),
        P(),
        P(),
        P(),
    )
    out_specs = (
        P("energy", "momentum", None, None, "phonon"),
        P(("energy", "momentum", "phonon"), None, None, None),
    )
    return jax.shard_map(local, mesh=mesh, in_specs=in_specs, out_specs=out_specs, check_vma=False)
```

```python
import functools

import jax
import jax.numpy as jnp
from jax import lax
from jax.experimental import pallas as pl
from jax.experimental.pallas import tpu as pltpu
from jax.sharding import PartitionSpec as P

ORB = 12
REACH = 4
LANES = 128


HIGH = lax.Precision.HIGHEST


def shifted_2(block, axis, distance):
    devices = range(lax.axis_size(axis))
    route = [(i - distance, i) for i in devices if i - distance in devices]
    return lax.ppermute(block, axis, route)


def scaled_blocks(weights, blocks):
    real_w = weights[None, :, :, 0, None, :]
    imag_w = weights[None, :, :, 1, None, :]
    real_b = blocks[:, None, :, 0].astype(jnp.float32)
    imag_b = blocks[:, None, :, 1].astype(jnp.float32)
    real_part = jnp.sum(real_w * real_b - imag_w * imag_b, axis=2)
    imag_part = jnp.sum(real_w * imag_b + imag_w * real_b, axis=2)
    return jnp.stack([real_part, imag_part], axis=2)


def inner_sums(local_blocks, shifted):
    local_real = local_blocks[:, :, 0].astype(jnp.float32)[:, :, None]
    local_imag = local_blocks[:, :, 1].astype(jnp.float32)[:, :, None]
    other_real = shifted[:, :, 0].astype(jnp.float32)[:, None]
    other_imag = shifted[:, :, 1].astype(jnp.float32)[:, None]
    real_sum = jnp.sum(local_real * other_real + local_imag * other_imag, axis=(0, 3))
    imag_sum = jnp.sum(local_imag * other_real - local_real * other_imag, axis=(0, 3))
    return jnp.stack([real_sum, imag_sum], axis=2)


def times_adjoint(left, right):
    return jnp.einsum("mab,mcb->mac", left, right, preferred_element_type=jnp.float32)


def times_plain(left, right):
    return jnp.einsum("mab,mbc->mac", left, right, preferred_element_type=jnp.float32)


def general(
    g_less, g_great, d_less, d_ret, neighbours, bond_dirs, energy_offset, momentum_offset, absorb
):
    energies = g_less.shape[0]
    momenta_here = g_less.shape[1]
    local_width = g_less.shape[4]
    bonds = d_less.shape[3]
    whole_atoms = d_less.shape[4]
    atom_share = local_width // bonds
    all_momenta = momenta_here * lax.axis_size("momentum")
    all_energies = energies * lax.axis_size("energy")
    modes_here = d_less.shape[0]
    order = d_ret.shape[2]
    classes = REACH * all_momenta
    energy_rank = lax.axis_index("energy")
    momentum_rank = lax.axis_index("momentum")
    phonon_rank = lax.axis_index("phonon")
    span = -(-REACH // energies)
    lower_steps = list(range(span, 0, -1))
    both_steps = lower_steps + list(range(-1, -span - 1, -1))
    label = (energy_offset - 1) * all_momenta + momentum_offset
    table = (label[:, None] == jnp.arange(classes, dtype=jnp.int32)[None, :]).astype(jnp.float32)
    soaked = table * absorb[:, None]
    pair_cube = bond_dirs[:, None] * bond_dirs[None, :]
    pair = pair_cube.reshape((9,) + bond_dirs.shape[1:])
    coupling = jnp.sum(d_less * pair[None, None], axis=2)
    first_mode = (
        (energy_rank * lax.axis_size("momentum") + momentum_rank) * lax.axis_size("phonon")
        + phonon_rank
    ) * modes_here
    own_table = lax.dynamic_slice_in_dim(table, first_mode, modes_here, 0)
    spread = lax.all_to_all(
        coupling.astype(jnp.bfloat16), "phonon", split_axis=3, concat_axis=0, tiled=True
    ).astype(coupling.dtype)
    blank = jnp.zeros((classes, 2 * bonds * atom_share), jnp.float32)
    piece = lax.all_gather(
        spread.astype(jnp.bfloat16), ("energy", "momentum"), axis=0, tiled=True
    ).astype(jnp.float32)
    rows = piece.shape[0]
    flat_piece = piece.reshape(rows, -1)
    emitted = blank + jnp.einsum("mc,mx->cx", table, flat_piece, precision=HIGH)
    absorbed = blank + jnp.einsum("mc,mx->cx", soaked, flat_piece, precision=HIGH)
    emitted = emitted.reshape(classes, 2, bonds, atom_share)
    absorbed = absorbed.reshape(classes, 2, bonds, atom_share)
    emit_table = emitted.transpose(0, 1, 3, 2).reshape(REACH, all_momenta, 2, local_width)
    soak_table = absorbed.transpose(0, 1, 3, 2).reshape(REACH, all_momenta, 2, local_width)
    moved = [shifted_2(g_less, "energy", step) for step in both_steps]
    lower = jnp.concatenate(moved[:span], axis=0)
    upper = jnp.concatenate(moved[span:], axis=0)
    lesser_rimmed = jnp.concatenate([lower, g_less, upper], axis=0)
    greater_moved = [shifted_2(g_great, "energy", step) for step in lower_steps]
    greater_rim = jnp.concatenate(greater_moved, axis=0)
    greater_rimmed = jnp.concatenate([greater_rim, g_great], axis=0)
    lesser_wide, greater_wide = (
        lax.all_gather(lesser_rimmed, "momentum", axis=1, tiled=True),
        lax.all_gather(greater_rimmed, "momentum", axis=1, tiled=True),
    )
    here_moment = momentum_rank * momenta_here + jnp.arange(momenta_here, dtype=jnp.int32)
    every_moment = jnp.arange(all_momenta, dtype=jnp.int32)
    behind = (here_moment[:, None] - every_moment[None, :]) % all_momenta
    ahead = (every_moment[None, :] - here_moment[:, None]) % all_momenta
    pick_behind = (behind[:, :, None] == every_moment[None, None, :]).astype(jnp.float32)
    pick_ahead = (ahead[:, :, None] == every_moment[None, None, :]).astype(jnp.float32)
    total = jnp.zeros(g_less.shape, jnp.float32)
    polar_parts = []
    for energy_step in range(1, REACH + 1):
        below = lesser_wide[REACH - energy_step : REACH - energy_step + energies]
        above = lesser_wide[REACH + energy_step : REACH + energy_step + energies]
        weight_below = jnp.einsum(
            "lkq,qzx->lkzx", pick_behind, emit_table[energy_step - 1], precision=HIGH
        )
        weight_above = jnp.einsum(
            "lkq,qzx->lkzx", pick_ahead, soak_table[energy_step - 1], precision=HIGH
        )
        total = total + scaled_blocks(weight_below, below) + scaled_blocks(weight_above, above)
        earlier = greater_wide[REACH - energy_step : REACH - energy_step + energies]
        pairs = inner_sums(g_less, earlier)
        polar_parts.append(jnp.einsum("lkq,lkzx->qzx", pick_behind, pairs, precision=HIGH))
    self_energy = total.astype(jnp.bfloat16)
    scale = float(all_energies * all_momenta * ORB * ORB) ** (-0.5)
    polar_local = jnp.stack(polar_parts).reshape(classes, 2, local_width) * scale
    polar_summed = lax.psum(polar_local, ("energy", "momentum"))
    polar_full = lax.all_gather(polar_summed, "phonon", axis=2, tiled=True)
    own_polar = jnp.einsum("mc,czx->mzx", own_table, polar_full, precision=HIGH)
    own_polar = own_polar.reshape(modes_here, 2, whole_atoms, bonds).transpose(0, 1, 3, 2)
    link = (
        neighbours[:, :, None] == jnp.arange(whole_atoms, dtype=jnp.int32)[None, None, :]
    ).astype(jnp.float32)
    weighted = pair_cube[None, None] * own_polar[:, :, None, None]
    dense = jnp.einsum("mzijna,nab->mziajb", weighted, link, precision=HIGH)
    dense = dense.reshape(modes_here, 2, order, order).astype(jnp.bfloat16)
    dense_re, dense_im = (dense[:, 0], dense[:, 1])
    ret_re, ret_im = (d_ret[:, 0], d_ret[:, 1])
    half_re = (times_adjoint(dense_re, ret_re) + times_adjoint(dense_im, ret_im)).astype(
        jnp.bfloat16
    )
    half_im = (times_adjoint(dense_im, ret_re) - times_adjoint(dense_re, ret_im)).astype(
        jnp.bfloat16
    )
    next_re = times_plain(ret_re, half_re) - times_plain(ret_im, half_im)
    next_im = times_plain(ret_re, half_im) + times_plain(ret_im, half_re)
    d_next = jnp.stack([next_re, next_im], axis=1).astype(jnp.bfloat16)
    return (self_energy, d_next)


EVERY = ("energy", "momentum", "phonon")
F32 = jnp.float32
BF16 = jnp.bfloat16


class Plan:
    def __init__(self, g_shape, d_shape, ret_shape, n_energy, n_momentum, n_phonon):
        self.energies, self.momenta, _, self.entries, self.width = g_shape
        self.modes, _, _, self.bonds, self.atoms = d_shape
        self.order = ret_shape[2]
        self.n_energy = n_energy
        self.n_momentum = n_momentum
        self.n_phonon = n_phonon
        self.devices = n_energy * n_momentum * n_phonon
        self.all_energies = self.energies * n_energy
        self.all_momenta = self.momenta * n_momentum
        self.classes = REACH * self.all_momenta
        self.slabs = 2 * self.energies
        self.tiles = self.width // LANES
        self.rest = self.width % LANES
        self.rest_rows = self.entries // n_energy
        self.main_rows = self.slabs * self.entries
        self.rest_pad = -(-self.rest_rows // 8) * 8
        self.message = -(-(self.main_rows + self.rest_pad) // 16) * 16
        self.tail = self.message - self.main_rows
        self.held = self.entries + self.rest_pad
        self.columns = self.width * n_phonon

    def fits(self):
        return (
            self.momenta == 1
            and self.all_momenta == 2
            and self.n_energy == self.tiles
            and self.n_energy & (self.n_energy - 1) == 0
            and self.entries % 16 == 0
            and self.entries % self.n_energy == 0
            and self.rest > 0
            and self.slabs * self.rest == LANES
            and self.modes <= 2
            and self.atoms == LANES
            and self.order == 3 * self.atoms
            and self.all_energies <= 8
        )


def call(kernel, out_shape, *operands, scratch=(), scalars=0, flops=0, moved=0):
    smem = pl.BlockSpec(memory_space=pltpu.SMEM)
    vmem = pl.BlockSpec(memory_space=pltpu.VMEM)
    specs = [smem] * scalars + [vmem] * (len(operands) - scalars)
    many = isinstance(out_shape, (list, tuple))
    return pl.pallas_call(
        kernel,
        out_shape=out_shape,
        in_specs=specs,
        out_specs=[vmem] * len(out_shape) if many else vmem,
        scratch_shapes=list(scratch),
        compiler_params=pltpu.CompilerParams(vmem_limit_bytes=48 * 2**20),
        cost_estimate=pl.CostEstimate(flops=flops, bytes_accessed=moved, transcendentals=0),
    )(*operands)


def deal_kernel(plan, rank_ref, source_ref, *refs):
    outs, rest_ref = refs[: plan.n_energy], refs[plan.n_energy]
    rank = rank_ref[0]
    slabs = [(e, z) for e in range(plan.energies) for z in range(2)]
    pieces = [source_ref[e, 0, z, :, plan.tiles * LANES :].astype(F32) for e, z in slabs]
    rest_ref[: plan.entries] = jnp.concatenate(pieces, axis=1)
    rest_ref[plan.entries :] = jnp.zeros((plan.tail, LANES), F32)
    for partner in range(plan.n_energy):
        target = rank ^ partner
        lanes = pl.ds(pl.multiple_of(target * LANES, LANES), LANES)
        for slab, (e, z) in enumerate(slabs):
            rows = slice(slab * plan.entries, (slab + 1) * plan.entries)
            outs[partner][rows] = source_ref[e, 0, z, :, lanes]
        rest = rest_ref[pl.ds(target * plan.rest_rows, plan.tail), :]
        outs[partner][plan.main_rows :] = rest.astype(BF16)


def bond_of(plan, shape):
    column = lax.broadcasted_iota(jnp.int32, shape, len(shape) - 1)
    atom = jnp.floor((column.astype(F32) + 0.5) * (1.0 / plan.bonds)).astype(jnp.int32)
    return column - atom * plan.bonds


def atom_table(plan):
    atom = lax.broadcasted_iota(jnp.int32, (plan.atoms, plan.columns), 0)
    column = lax.broadcasted_iota(jnp.int32, (plan.atoms, plan.columns), 1)
    inside = column - atom * plan.bonds
    return jnp.where((inside >= 0) & (inside < plan.bonds), 1.0, 0.0).astype(BF16)


def mode_table(plan, energy_ref, momentum_ref, absorb_ref):
    width = plan.devices * 8
    modes = plan.devices * plan.modes
    label = (energy_ref[...] - 1) * plan.all_momenta + momentum_ref[...]
    stacked = jnp.concatenate(
        [label.astype(F32), absorb_ref[...], jnp.zeros((6, modes), F32)], axis=0
    )
    mode = lax.broadcasted_iota(jnp.int32, (modes, width), 0)
    column = lax.broadcasted_iota(jnp.int32, (modes, width), 1)
    inner = (column & 3) >> 1
    chosen = (mode == (column >> 3) * plan.modes + inner) & (inner < plan.modes)
    spread = jnp.dot(
        stacked, jnp.where(chosen, 1.0, 0.0), precision=HIGH, preferred_element_type=F32
    )
    label = (spread[:1] + 0.5).astype(jnp.int32)
    column = lax.broadcasted_iota(jnp.int32, (2 * plan.classes, width), 1)
    row = lax.broadcasted_iota(jnp.int32, (2 * plan.classes, width), 0)
    hit = (label == (row >> 1)) & ((column & 1) == (row & 1))
    hit = hit & (((column & 3) >> 1) < plan.modes)
    blocks = []
    for kind in range(2):
        here = hit & (((column >> 2) & 1) == kind)
        blocks.append(jnp.where(here, 1.0, 0.0))
        blocks.append(jnp.where(here, spread[1:2], 0.0))
    return jnp.concatenate(blocks, axis=0)


def couple_kernel(
    plan, less_ref, dirs_ref, energy_ref, momentum_ref, absorb_ref, out_ref, table_ref, pair_ref, held_ref
):
    bonds, width = plan.bonds, plan.width
    held_ref[...] = jnp.zeros(held_ref.shape, F32)
    for n in range(bonds):
        pairs = [dirs_ref[n, i : i + 1] * dirs_ref[n, j : j + 1] for i in range(3) for j in range(3)]
        for way, (i, j) in enumerate((i, j) for i in range(3) for j in range(i, 3)):
            pair_ref[way, n : n + 1] = pairs[3 * i + j]
        for m in range(plan.modes):
            total = less_ref[m, 0, n] * pairs[0]
            for t in range(1, 9):
                total = total + less_ref[m, t, n] * pairs[t]
            row = (m * bonds + n) * 2
            held_ref[row : row + 2] = total
    rows = held_ref.shape[0]
    spread = jnp.dot(held_ref[...].astype(BF16), atom_table(plan), preferred_element_type=F32)
    row = lax.broadcasted_iota(jnp.int32, (rows, 1), 0)
    bond = (row >> 1) - jnp.where(row >= 2 * bonds, bonds, 0)
    keep = bond == bond_of(plan, (1, plan.columns))
    kept = jnp.where(keep, spread, 0.0).astype(BF16)
    line = lax.broadcasted_iota(jnp.int32, (8, rows), 0)
    row = lax.broadcasted_iota(jnp.int32, (8, rows), 1)
    owner = jnp.where(row >= 2 * bonds, 2, 0) + (row & 1)
    gather = jnp.where((line == owner) & (row < 2 * bonds * plan.modes), 1.0, 0.0).astype(BF16)
    flat = jnp.dot(gather, kept, preferred_element_type=F32)[:4]
    for p in range(plan.n_phonon):
        start = p * width
        rest = flat[:, start + plan.tiles * LANES : start + width]
        rest = jnp.concatenate([rest, jnp.zeros((4, LANES - plan.rest), F32)], axis=1)
        for tile in range(plan.tiles):
            main = flat[:, start + tile * LANES : start + (tile + 1) * LANES]
            block = jnp.concatenate([main, rest], axis=0)
            for half in range(plan.n_momentum):
                out_ref[(tile * plan.n_momentum + half) * plan.n_phonon + p] = block
    table_ref[...] = mode_table(plan, energy_ref, momentum_ref, absorb_ref)


def stage_blocks(plan, rank, messages, held_ref, stride, offset):
    row = lax.broadcasted_iota(jnp.int32, (plan.rest_pad, LANES), 0)
    for partner, message in enumerate(messages):
        first = plan.energies * (rank ^ partner)
        tail = message[plan.main_rows :].astype(F32)[: plan.rest_pad]
        tail = jnp.where(row < plan.rest_rows, tail, 0.0)
        for e in range(plan.energies):
            for z in range(2):
                slab = 2 * e + z
                place = ((first + e) * stride + offset) * 2 + z
                rows = slice(slab * plan.entries, (slab + 1) * plan.entries)
                held_ref[place, : plan.entries] = message[rows].astype(F32)
                turned = tail if slab == 0 else pltpu.roll(tail, LANES - slab * plan.rest, 1)
                held_ref[place, plan.entries :] = turned


def polar_kernel(plan, rank_ref, table_ref, *refs):
    chips = plan.n_energy
    out_ref, low_ref, high_ref = refs[3 * chips :]
    rank = rank_ref[0]
    stage_blocks(plan, rank, refs[:chips], low_ref, 2, 0)
    stage_blocks(plan, rank, refs[chips : 2 * chips], low_ref, 2, 1)
    stage_blocks(plan, rank, refs[2 * chips : 3 * chips], high_ref, 1, 0)
    count = plan.all_energies

    def step(chunk, sums):
        rows = pl.ds(pl.multiple_of(chunk * 8, 8), 8)
        sums = list(sums)
        for energy in range(count):
            high_re, high_im = high_ref[2 * energy, rows], high_ref[2 * energy + 1, rows]
            for energy_step in range(1, REACH + 1):
                if energy + energy_step >= count:
                    continue
                for q in range(2):
                    index = ((energy_step - 1) * 2 + q) * 2
                    low = ((energy + energy_step) * 2 + q) * 2
                    low_re, low_im = low_ref[low, rows], low_ref[low + 1, rows]
                    sums[index] = sums[index] + (low_re * high_re + low_im * high_im)
                    sums[index + 1] = sums[index + 1] + (low_im * high_re - low_re * high_im)
        return tuple(sums)

    none = tuple(jnp.zeros((8, LANES), F32) for _ in range(2 * plan.classes))
    main = lax.fori_loop(0, plan.entries // 8, step, none)
    rest = lax.fori_loop(plan.entries // 8, plan.held // 8, step, none)
    scale = float(count * 2 * plan.entries) ** (-0.5)
    lines = [jnp.sum(part, axis=0, keepdims=True) * scale for part in main + rest]
    sums = jnp.concatenate(lines, axis=0)
    lines = 2 * plan.classes
    picks = jnp.concatenate([table_ref[:lines], table_ref[2 * lines : 3 * lines]], axis=0)
    picked = lax.dot_general(
        picks, sums, (((0,), (0,)), ((), ())), precision=HIGH, preferred_element_type=F32
    )
    out_ref[...] = picked.reshape(out_ref.shape)


def energy_kernel(plan, rank_ref, table_ref, coupling_ref, *refs):
    chips = plan.n_energy
    outs = refs[2 * chips : 3 * chips]
    low_ref, sum_ref, weight_ref = refs[3 * chips :]
    rank = rank_ref[0]
    flat = coupling_ref[...].reshape(plan.devices * 8, LANES)
    weight_ref[...] = jnp.dot(table_ref[...], flat, precision=HIGH, preferred_element_type=F32)
    stage_blocks(plan, rank, refs[:chips], low_ref, 2, 0)
    stage_blocks(plan, rank, refs[chips : 2 * chips], low_ref, 2, 1)
    count = plan.all_energies

    def run(base):
        def step(chunk, carry):
            rows = pl.ds(pl.multiple_of(chunk * 8, 8), 8)
            re = [None] * count
            im = [None] * count
            for energy_step in range(1, REACH + 1):
                for q in range(2):
                    index = base + ((energy_step - 1) * 2 + q) * 2
                    for part, sign in ((0, -1), (1, 1)):
                        at = index + part * 2 * plan.classes
                        w_re = jnp.broadcast_to(weight_ref[at : at + 1], (8, LANES))
                        w_im = jnp.broadcast_to(weight_ref[at + 1 : at + 2], (8, LANES))
                        for energy in range(count):
                            other = energy + sign * energy_step
                            if other < 0 or other >= count:
                                continue
                            at = (other * 2 + q) * 2
                            b_re, b_im = low_ref[at, rows], low_ref[at + 1, rows]
                            t_re = w_re * b_re - w_im * b_im
                            t_im = w_re * b_im + w_im * b_re
                            re[energy] = t_re if re[energy] is None else re[energy] + t_re
                            im[energy] = t_im if im[energy] is None else im[energy] + t_im
            for energy in range(count):
                sum_ref[2 * energy, rows] = re[energy]
                sum_ref[2 * energy + 1, rows] = im[energy]
            return carry

        return step

    lax.fori_loop(0, plan.entries // 8, run(0), 0)
    lax.fori_loop(plan.entries // 8, plan.held // 8, run(4 * plan.classes), 0)
    lane = lax.broadcasted_iota(jnp.int32, (plan.rest_pad, LANES), 1)
    for partner in range(chips):
        first = plan.energies * (rank ^ partner)
        tail = jnp.zeros((plan.rest_pad, LANES), F32)
        for slab in range(plan.slabs):
            place = 2 * first + slab
            rows = slice(slab * plan.entries, (slab + 1) * plan.entries)
            outs[partner][rows] = sum_ref[place, : plan.entries].astype(BF16)
            piece = sum_ref[place, plan.entries :]
            if slab:
                piece = pltpu.roll(piece, slab * plan.rest, 1)
            mine = (lane >= slab * plan.rest) & (lane < (slab + 1) * plan.rest)
            tail = jnp.where(mine, piece, tail)
        if plan.tail > plan.rest_pad:
            blank = jnp.zeros((plan.tail - plan.rest_pad, LANES), F32)
            tail = jnp.concatenate([tail, blank], axis=0)
        outs[partner][plan.main_rows :] = tail.astype(BF16)


def gather_kernel(plan, rank_ref, *refs):
    chips = plan.n_energy
    out_ref, rest_ref = refs[chips:]
    rank = rank_ref[0]
    for partner, message in enumerate(refs[:chips]):
        source = rank ^ partner
        lanes = pl.ds(pl.multiple_of(source * LANES, LANES), LANES)
        tail = message[plan.main_rows :].astype(F32)[: plan.rest_pad]
        for slab in range(plan.slabs):
            rows = slice(slab * plan.entries, (slab + 1) * plan.entries)
            out_ref[slab // 2, 0, slab % 2, :, lanes] = message[rows]
            turned = tail if slab == 0 else pltpu.roll(tail, LANES - slab * plan.rest, 1)
            rest_ref[slab, source] = turned
    for slab in range(plan.slabs):
        parts = [rest_ref[slab, source, : plan.rest_rows] for source in range(chips)]
        rest = jnp.concatenate(parts, axis=0)[:, : plan.rest]
        out_ref[slab // 2, 0, slab % 2, :, plan.tiles * LANES :] = rest.astype(BF16)


def next_kernel(plan, polar_ref, ret_ref, near_ref, pair_ref, out_ref, v_ref, dense_ref):
    bonds, atoms, order = plan.bonds, plan.atoms, plan.order
    padded = -(-bonds // 8) * 8
    lines = []
    for p in range(plan.n_phonon):
        rest = jnp.zeros((4, LANES), F32)
        for tile in range(plan.tiles):
            main = jnp.zeros((4, LANES), F32)
            for half in range(plan.n_momentum):
                block = polar_ref[(tile * plan.n_momentum + half) * plan.n_phonon + p]
                main = main + block[:4]
                rest = rest + block[4:]
            lines.append(main)
        lines.append(rest[:, : plan.rest])
    flat = jnp.concatenate(lines, axis=1)
    bond = lax.broadcasted_iota(jnp.int32, (padded, 1), 0)
    keep = bond == bond_of(plan, (1, plan.columns))
    tall = jnp.concatenate(
        [jnp.where(keep, flat[row : row + 1], 0.0) for row in range(2 * plan.modes)], axis=0
    )
    upper = tall.astype(BF16)
    lower = (tall - upper.astype(F32)).astype(BF16)
    contract = (((1,), (1,)), ((), ()))
    both = lax.dot_general(
        jnp.concatenate([upper, lower], axis=0), atom_table(plan), contract, preferred_element_type=F32
    )
    by_bond = both[: tall.shape[0]] + both[tall.shape[0] :]
    ways = [(i, j) for i in range(3) for j in range(i, 3)]
    for way in range(len(ways)):
        for row in range(2 * plan.modes):
            values = by_bond[row * padded : row * padded + bonds]
            v_ref[row * len(ways) + way, :bonds] = values * pair_ref[way]

    def step(chunk, carry):
        first = pl.multiple_of(chunk * 16, 16)
        number = lax.broadcasted_iota(jnp.int32, (16, atoms), 0) + first
        for row in range(2 * plan.modes):
            sums = [jnp.zeros((16, atoms), F32) for _ in ways]
            for n in range(bonds):
                hit = number == near_ref[n : n + 1]
                for way in range(len(ways)):
                    value = v_ref[row * len(ways) + way, n : n + 1]
                    sums[way] = sums[way] + jnp.where(hit, value, 0.0)
            m, z = row // 2, row % 2
            for way, (i, j) in enumerate(ways):
                block = sums[way].astype(BF16)
                other = block if z else (-sums[way]).astype(BF16)
                for up, left in {(j, i), (i, j)}:
                    place = pl.multiple_of(up * atoms + first, 16)
                    columns = left * atoms
                    dense_ref[m, pl.ds(place, 16), pl.ds(z * order + columns, atoms)] = block
                    place = pl.multiple_of(order + up * atoms + first, 16)
                    dense_ref[m, pl.ds(place, 16), pl.ds((1 - z) * order + columns, atoms)] = other
        return carry

    lax.fori_loop(0, atoms // 16, step, 0)
    for m in range(plan.modes):
        ret = jnp.concatenate([ret_ref[m, 0], ret_ref[m, 1]], axis=1)
        half = jnp.dot(ret, dense_ref[m], preferred_element_type=F32).astype(BF16)
        half_re, half_im = half[:, :order], half[:, order:]
        right = jnp.concatenate(
            [
                jnp.concatenate([half_re, -half_im], axis=1),
                jnp.concatenate([half_im, half_re], axis=1),
            ],
            axis=0,
        )
        after = lax.dot_general(ret, right, contract, preferred_element_type=F32)
        out_ref[m, 0] = after[:, :order].astype(BF16)
        out_ref[m, 1] = after[:, order:].astype(BF16)


def swap(block, axis, distance):
    return lax.ppermute(block, axis, [(i, i ^ distance) for i in range(lax.axis_size(axis))])


def to_chips(plan, blocks):
    return [blocks[0]] + [swap(blocks[k], "energy", k) for k in range(1, plan.n_energy)]


def dealt(
    plan, g_less, g_great, d_less, d_ret, neighbours, bond_dirs, energy_offset, momentum_offset, absorb
):
    rank = lax.axis_index("energy").astype(jnp.int32).reshape(1)
    chips, held, count = plan.n_energy, plan.held, plan.all_energies
    lines = 2 * plan.classes
    modes = plan.devices * plan.modes
    message = jax.ShapeDtypeStruct((plan.message, LANES), BF16)

    def deal(blocks):
        return call(
            functools.partial(deal_kernel, plan), [message] * chips, rank, blocks,
            scalars=1, scratch=[pltpu.VMEM((plan.entries + plan.tail, LANES), F32)],
            moved=4 * blocks.size,
        )

    low_blocks = deal(g_less)
    own, g_great = lax.optimization_barrier((low_blocks[0], g_great))
    low_blocks = [own] + list(low_blocks[1:])
    low = to_chips(plan, low_blocks)
    high_blocks = deal(g_great)
    own, d_less, bond_dirs = lax.optimization_barrier((high_blocks[0], d_less, bond_dirs))
    high = to_chips(plan, [own] + list(high_blocks[1:]))
    low[0], low[1] = lax.optimization_barrier((low[0], low[1]))
    low_beside = [swap(block, "momentum", 1) for block in low]
    small = jax.ShapeDtypeStruct((plan.devices, 8, LANES), F32)
    coupling, table, pairs = call(
        functools.partial(couple_kernel, plan),
        [
            small,
            jax.ShapeDtypeStruct((4 * lines, plan.devices * 8), F32),
            jax.ShapeDtypeStruct((6, plan.bonds, plan.atoms), F32),
        ],
        d_less.transpose(0, 2, 3, 1, 4), bond_dirs.transpose(1, 0, 2),
        energy_offset.reshape(1, modes), momentum_offset.reshape(1, modes), absorb.reshape(1, modes),
        scratch=[pltpu.VMEM((-(-2 * plan.bonds * plan.modes // 16) * 16, plan.atoms), F32)],
        moved=4 * d_less.size,
    )
    coupling = lax.all_to_all(coupling, EVERY, 0, 0, tiled=True)
    low_scratch = pltpu.VMEM((4 * count, held, LANES), F32)
    half_scratch = pltpu.VMEM((2 * count, held, LANES), F32)
    polar = call(
        functools.partial(polar_kernel, plan), small, rank, table, *low, *low_beside, *high,
        scalars=1, scratch=[low_scratch, half_scratch], moved=8 * 2**20,
    )
    polar = lax.all_to_all(polar, EVERY, 0, 0, tiled=True)
    sums = call(
        functools.partial(energy_kernel, plan), [message] * chips,
        rank, table, coupling, *low, *low_beside,
        scalars=1, scratch=[low_scratch, half_scratch, pltpu.VMEM((4 * lines, LANES), F32)],
        moved=8 * 2**20,
    )
    sums = to_chips(plan, sums)
    padded = -(-plan.bonds // 8) * 8
    d_next = call(
        functools.partial(next_kernel, plan), jax.ShapeDtypeStruct(d_ret.shape, BF16),
        polar, d_ret, neighbours, pairs,
        scratch=[
            pltpu.VMEM((12 * plan.modes, padded, plan.atoms), F32),
            pltpu.VMEM((plan.modes, 2 * plan.order, 2 * plan.order), BF16),
        ],
        moved=20 * 2**20,
    )
    d_next, own = lax.optimization_barrier((d_next, sums[0]))
    self_energy = call(
        functools.partial(gather_kernel, plan), jax.ShapeDtypeStruct(g_less.shape, BF16), rank,
        own, *sums[1:],
        scalars=1, scratch=[pltpu.VMEM((plan.slabs, chips, plan.rest_pad, LANES), F32)],
        moved=4 * 2**20,
    )
    return self_energy, d_next


def local(*arrays):
    plan = Plan(
        arrays[0].shape, arrays[2].shape, arrays[3].shape,
        lax.axis_size("energy"), lax.axis_size("momentum"), lax.axis_size("phonon"),
    )
    return dealt(plan, *arrays) if plan.fits() else general(*arrays)


def solution(mesh):
    in_specs = (
        P("energy", "momentum", None, None, "phonon"),
        P("energy", "momentum", None, None, "phonon"),
        P(("energy", "momentum", "phonon"), None, None, None, None),
        P(("energy", "momentum", "phonon"), None, None, None),
        P(),
        P(),
        P(),
        P(),
        P(),
    )
    out_specs = (
        P("energy", "momentum", None, None, "phonon"),
        P(("energy", "momentum", "phonon"), None, None, None),
    )
    return jax.shard_map(local, mesh=mesh, in_specs=in_specs, out_specs=out_specs, check_vma=False)
```

```python
import functools

import jax
import jax.numpy as jnp
from jax import lax
from jax.experimental import pallas as pl
from jax.experimental.pallas import tpu as pltpu
from jax.sharding import PartitionSpec as P

ORB = 12
REACH = 4
LANES = 128


HIGH = lax.Precision.HIGHEST


def shifted_2(block, axis, distance):
    devices = range(lax.axis_size(axis))
    route = [(i - distance, i) for i in devices if i - distance in devices]
    return lax.ppermute(block, axis, route)


def scaled_blocks(weights, blocks):
    real_w = weights[None, :, :, 0, None, :]
    imag_w = weights[None, :, :, 1, None, :]
    real_b = blocks[:, None, :, 0].astype(jnp.float32)
    imag_b = blocks[:, None, :, 1].astype(jnp.float32)
    real_part = jnp.sum(real_w * real_b - imag_w * imag_b, axis=2)
    imag_part = jnp.sum(real_w * imag_b + imag_w * real_b, axis=2)
    return jnp.stack([real_part, imag_part], axis=2)


def inner_sums(local_blocks, shifted):
    local_real = local_blocks[:, :, 0].astype(jnp.float32)[:, :, None]
    local_imag = local_blocks[:, :, 1].astype(jnp.float32)[:, :, None]
    other_real = shifted[:, :, 0].astype(jnp.float32)[:, None]
    other_imag = shifted[:, :, 1].astype(jnp.float32)[:, None]
    real_sum = jnp.sum(local_real * other_real + local_imag * other_imag, axis=(0, 3))
    imag_sum = jnp.sum(local_imag * other_real - local_real * other_imag, axis=(0, 3))
    return jnp.stack([real_sum, imag_sum], axis=2)


def times_adjoint(left, right):
    return jnp.einsum("mab,mcb->mac", left, right, preferred_element_type=jnp.float32)


def times_plain(left, right):
    return jnp.einsum("mab,mbc->mac", left, right, preferred_element_type=jnp.float32)


def general(
    g_less, g_great, d_less, d_ret, neighbours, bond_dirs, energy_offset, momentum_offset, absorb
):
    energies = g_less.shape[0]
    momenta_here = g_less.shape[1]
    local_width = g_less.shape[4]
    bonds = d_less.shape[3]
    whole_atoms = d_less.shape[4]
    atom_share = local_width // bonds
    all_momenta = momenta_here * lax.axis_size("momentum")
    all_energies = energies * lax.axis_size("energy")
    modes_here = d_less.shape[0]
    order = d_ret.shape[2]
    classes = REACH * all_momenta
    energy_rank = lax.axis_index("energy")
    momentum_rank = lax.axis_index("momentum")
    phonon_rank = lax.axis_index("phonon")
    span = -(-REACH // energies)
    lower_steps = list(range(span, 0, -1))
    both_steps = lower_steps + list(range(-1, -span - 1, -1))
    label = (energy_offset - 1) * all_momenta + momentum_offset
    table = (label[:, None] == jnp.arange(classes, dtype=jnp.int32)[None, :]).astype(jnp.float32)
    soaked = table * absorb[:, None]
    pair_cube = bond_dirs[:, None] * bond_dirs[None, :]
    pair = pair_cube.reshape((9,) + bond_dirs.shape[1:])
    coupling = jnp.sum(d_less * pair[None, None], axis=2)
    first_mode = (
        (energy_rank * lax.axis_size("momentum") + momentum_rank) * lax.axis_size("phonon")
        + phonon_rank
    ) * modes_here
    own_table = lax.dynamic_slice_in_dim(table, first_mode, modes_here, 0)
    spread = lax.all_to_all(
        coupling.astype(jnp.bfloat16), "phonon", split_axis=3, concat_axis=0, tiled=True
    ).astype(coupling.dtype)
    blank = jnp.zeros((classes, 2 * bonds * atom_share), jnp.float32)
    piece = lax.all_gather(
        spread.astype(jnp.bfloat16), ("energy", "momentum"), axis=0, tiled=True
    ).astype(jnp.float32)
    rows = piece.shape[0]
    flat_piece = piece.reshape(rows, -1)
    emitted = blank + jnp.einsum("mc,mx->cx", table, flat_piece, precision=HIGH)
    absorbed = blank + jnp.einsum("mc,mx->cx", soaked, flat_piece, precision=HIGH)
    emitted = emitted.reshape(classes, 2, bonds, atom_share)
    absorbed = absorbed.reshape(classes, 2, bonds, atom_share)
    emit_table = emitted.transpose(0, 1, 3, 2).reshape(REACH, all_momenta, 2, local_width)
    soak_table = absorbed.transpose(0, 1, 3, 2).reshape(REACH, all_momenta, 2, local_width)
    moved = [shifted_2(g_less, "energy", step) for step in both_steps]
    lower = jnp.concatenate(moved[:span], axis=0)
    upper = jnp.concatenate(moved[span:], axis=0)
    lesser_rimmed = jnp.concatenate([lower, g_less, upper], axis=0)
    greater_moved = [shifted_2(g_great, "energy", step) for step in lower_steps]
    greater_rim = jnp.concatenate(greater_moved, axis=0)
    greater_rimmed = jnp.concatenate([greater_rim, g_great], axis=0)
    lesser_wide, greater_wide = (
        lax.all_gather(lesser_rimmed, "momentum", axis=1, tiled=True),
        lax.all_gather(greater_rimmed, "momentum", axis=1, tiled=True),
    )
    here_moment = momentum_rank * momenta_here + jnp.arange(momenta_here, dtype=jnp.int32)
    every_moment = jnp.arange(all_momenta, dtype=jnp.int32)
    behind = (here_moment[:, None] - every_moment[None, :]) % all_momenta
    ahead = (every_moment[None, :] - here_moment[:, None]) % all_momenta
    pick_behind = (behind[:, :, None] == every_moment[None, None, :]).astype(jnp.float32)
    pick_ahead = (ahead[:, :, None] == every_moment[None, None, :]).astype(jnp.float32)
    total = jnp.zeros(g_less.shape, jnp.float32)
    polar_parts = []
    for energy_step in range(1, REACH + 1):
        below = lesser_wide[REACH - energy_step : REACH - energy_step + energies]
        above = lesser_wide[REACH + energy_step : REACH + energy_step + energies]
        weight_below = jnp.einsum(
            "lkq,qzx->lkzx", pick_behind, emit_table[energy_step - 1], precision=HIGH
        )
        weight_above = jnp.einsum(
            "lkq,qzx->lkzx", pick_ahead, soak_table[energy_step - 1], precision=HIGH
        )
        total = total + scaled_blocks(weight_below, below) + scaled_blocks(weight_above, above)
        earlier = greater_wide[REACH - energy_step : REACH - energy_step + energies]
        pairs = inner_sums(g_less, earlier)
        polar_parts.append(jnp.einsum("lkq,lkzx->qzx", pick_behind, pairs, precision=HIGH))
    self_energy = total.astype(jnp.bfloat16)
    scale = float(all_energies * all_momenta * ORB * ORB) ** (-0.5)
    polar_local = jnp.stack(polar_parts).reshape(classes, 2, local_width) * scale
    polar_summed = lax.psum(polar_local, ("energy", "momentum"))
    polar_full = lax.all_gather(polar_summed, "phonon", axis=2, tiled=True)
    own_polar = jnp.einsum("mc,czx->mzx", own_table, polar_full, precision=HIGH)
    own_polar = own_polar.reshape(modes_here, 2, whole_atoms, bonds).transpose(0, 1, 3, 2)
    link = (
        neighbours[:, :, None] == jnp.arange(whole_atoms, dtype=jnp.int32)[None, None, :]
    ).astype(jnp.float32)
    weighted = pair_cube[None, None] * own_polar[:, :, None, None]
    dense = jnp.einsum("mzijna,nab->mziajb", weighted, link, precision=HIGH)
    dense = dense.reshape(modes_here, 2, order, order).astype(jnp.bfloat16)
    dense_re, dense_im = (dense[:, 0], dense[:, 1])
    ret_re, ret_im = (d_ret[:, 0], d_ret[:, 1])
    half_re = (times_adjoint(dense_re, ret_re) + times_adjoint(dense_im, ret_im)).astype(
        jnp.bfloat16
    )
    half_im = (times_adjoint(dense_im, ret_re) - times_adjoint(dense_re, ret_im)).astype(
        jnp.bfloat16
    )
    next_re = times_plain(ret_re, half_re) - times_plain(ret_im, half_im)
    next_im = times_plain(ret_re, half_im) + times_plain(ret_im, half_re)
    d_next = jnp.stack([next_re, next_im], axis=1).astype(jnp.bfloat16)
    return (self_energy, d_next)


EVERY = ("energy", "momentum", "phonon")
F32 = jnp.float32
BF16 = jnp.bfloat16


class Plan:
    def __init__(self, g_shape, d_shape, ret_shape, n_energy, n_momentum, n_phonon):
        self.energies, self.momenta, _, self.entries, self.width = g_shape
        self.modes, _, _, self.bonds, self.atoms = d_shape
        self.order = ret_shape[2]
        self.n_energy = n_energy
        self.n_momentum = n_momentum
        self.n_phonon = n_phonon
        self.devices = n_energy * n_momentum * n_phonon
        self.all_energies = self.energies * n_energy
        self.all_momenta = self.momenta * n_momentum
        self.classes = REACH * self.all_momenta
        self.slabs = 2 * self.energies
        self.tiles = self.width // LANES
        self.rest = self.width % LANES
        self.rest_rows = self.entries // n_energy
        self.main_rows = self.slabs * self.entries
        self.rest_pad = -(-self.rest_rows // 8) * 8
        self.message = -(-(self.main_rows + self.rest_pad) // 16) * 16
        self.tail = self.message - self.main_rows
        self.held = self.entries + self.rest_pad
        self.columns = self.width * n_phonon

    def fits(self):
        return (
            self.momenta == 1
            and self.all_momenta == 2
            and self.n_energy == self.tiles
            and self.n_energy & (self.n_energy - 1) == 0
            and self.entries % 16 == 0
            and self.entries % self.n_energy == 0
            and self.rest > 0
            and self.slabs * self.rest == LANES
            and self.modes <= 2
            and self.atoms == LANES
            and self.order == 3 * self.atoms
            and self.all_energies <= 8
        )


def call(kernel, out_shape, *operands, scratch=(), scalars=0, flops=0, moved=0, out_space=pltpu.VMEM):
    smem = pl.BlockSpec(memory_space=pltpu.SMEM)
    vmem = pl.BlockSpec(memory_space=pltpu.VMEM)
    specs = [smem] * scalars + [vmem] * (len(operands) - scalars)
    many = isinstance(out_shape, (list, tuple))
    return pl.pallas_call(
        kernel,
        out_shape=out_shape,
        in_specs=specs,
        out_specs=[vmem] * len(out_shape) if many else pl.BlockSpec(memory_space=out_space),
        scratch_shapes=list(scratch),
        compiler_params=pltpu.CompilerParams(vmem_limit_bytes=48 * 2**20),
        cost_estimate=pl.CostEstimate(flops=flops, bytes_accessed=moved, transcendentals=0),
    )(*operands)


def deal_kernel(plan, rank_ref, source_ref, *refs):
    outs, rest_ref = refs[: plan.n_energy], refs[plan.n_energy]
    rank = rank_ref[0]
    slabs = [(e, z) for e in range(plan.energies) for z in range(2)]
    pieces = [source_ref[e, 0, z, :, plan.tiles * LANES :].astype(F32) for e, z in slabs]
    rest_ref[: plan.entries] = jnp.concatenate(pieces, axis=1)
    rest_ref[plan.entries :] = jnp.zeros((plan.tail, LANES), F32)
    for partner in range(plan.n_energy):
        target = rank ^ partner
        lanes = pl.ds(pl.multiple_of(target * LANES, LANES), LANES)
        for slab, (e, z) in enumerate(slabs):
            rows = slice(slab * plan.entries, (slab + 1) * plan.entries)
            outs[partner][rows] = source_ref[e, 0, z, :, lanes]
        rest = rest_ref[pl.ds(target * plan.rest_rows, plan.tail), :]
        outs[partner][plan.main_rows :] = rest.astype(BF16)


def bond_of(plan, shape):
    column = lax.broadcasted_iota(jnp.int32, shape, len(shape) - 1)
    atom = jnp.floor((column.astype(F32) + 0.5) * (1.0 / plan.bonds)).astype(jnp.int32)
    return column - atom * plan.bonds


def atom_table(plan):
    atom = lax.broadcasted_iota(jnp.int32, (plan.atoms, plan.columns), 0)
    column = lax.broadcasted_iota(jnp.int32, (plan.atoms, plan.columns), 1)
    inside = column - atom * plan.bonds
    return jnp.where((inside >= 0) & (inside < plan.bonds), 1.0, 0.0).astype(BF16)


def mode_table(plan, energy_ref, momentum_ref, absorb_ref):
    width = plan.devices * 8
    modes = plan.devices * plan.modes
    label = (energy_ref[...] - 1) * plan.all_momenta + momentum_ref[...]
    stacked = jnp.concatenate(
        [label.astype(F32), absorb_ref[...], jnp.zeros((6, modes), F32)], axis=0
    )
    mode = lax.broadcasted_iota(jnp.int32, (modes, width), 0)
    column = lax.broadcasted_iota(jnp.int32, (modes, width), 1)
    inner = (column & 3) >> 1
    chosen = (mode == (column >> 3) * plan.modes + inner) & (inner < plan.modes)
    spread = jnp.dot(
        stacked, jnp.where(chosen, 1.0, 0.0), precision=HIGH, preferred_element_type=F32
    )
    label = (spread[:1] + 0.5).astype(jnp.int32)
    column = lax.broadcasted_iota(jnp.int32, (2 * plan.classes, width), 1)
    row = lax.broadcasted_iota(jnp.int32, (2 * plan.classes, width), 0)
    hit = (label == (row >> 1)) & ((column & 1) == (row & 1))
    hit = hit & (((column & 3) >> 1) < plan.modes)
    blocks = []
    for kind in range(2):
        here = hit & (((column >> 2) & 1) == kind)
        blocks.append(jnp.where(here, 1.0, 0.0))
        blocks.append(jnp.where(here, spread[1:2], 0.0))
    return jnp.concatenate(blocks, axis=0)


def couple_kernel(
    plan, less_ref, dirs_ref, energy_ref, momentum_ref, absorb_ref,
    out_ref, table_ref, pair_ref, held_ref,
):
    bonds, width = plan.bonds, plan.width
    held_ref[...] = jnp.zeros(held_ref.shape, F32)
    for n in range(bonds):
        pairs = [dirs_ref[n, i : i + 1] * dirs_ref[n, j : j + 1] for i in range(3) for j in range(3)]
        for way, (i, j) in enumerate((i, j) for i in range(3) for j in range(i, 3)):
            pair_ref[way, n : n + 1] = pairs[3 * i + j]
        for m in range(plan.modes):
            total = less_ref[m, 0, n] * pairs[0]
            for t in range(1, 9):
                total = total + less_ref[m, t, n] * pairs[t]
            row = (m * bonds + n) * 2
            held_ref[row : row + 2] = total
    rows = held_ref.shape[0]
    spread = jnp.dot(held_ref[...].astype(BF16), atom_table(plan), preferred_element_type=F32)
    row = lax.broadcasted_iota(jnp.int32, (rows, 1), 0)
    bond = (row >> 1) - jnp.where(row >= 2 * bonds, bonds, 0)
    keep = bond == bond_of(plan, (1, plan.columns))
    kept = jnp.where(keep, spread, 0.0).astype(BF16)
    line = lax.broadcasted_iota(jnp.int32, (8, rows), 0)
    row = lax.broadcasted_iota(jnp.int32, (8, rows), 1)
    owner = jnp.where(row >= 2 * bonds, 2, 0) + (row & 1)
    gather = jnp.where((line == owner) & (row < 2 * bonds * plan.modes), 1.0, 0.0).astype(BF16)
    flat = jnp.dot(gather, kept, preferred_element_type=F32)[:4]
    for p in range(plan.n_phonon):
        start = p * width
        rest = flat[:, start + plan.tiles * LANES : start + width]
        rest = jnp.concatenate([rest, jnp.zeros((4, LANES - plan.rest), F32)], axis=1)
        for tile in range(plan.tiles):
            main = flat[:, start + tile * LANES : start + (tile + 1) * LANES]
            block = jnp.concatenate([main, rest], axis=0)
            for half in range(plan.n_momentum):
                out_ref[(tile * plan.n_momentum + half) * plan.n_phonon + p] = block
    table_ref[...] = mode_table(plan, energy_ref, momentum_ref, absorb_ref)


def stage_blocks(plan, rank, messages, held_ref, stride, offset):
    row = lax.broadcasted_iota(jnp.int32, (plan.rest_pad, LANES), 0)
    for partner, message in enumerate(messages):
        first = plan.energies * (rank ^ partner)
        tail = message[plan.main_rows :].astype(F32)[: plan.rest_pad]
        tail = jnp.where(row < plan.rest_rows, tail, 0.0)
        for e in range(plan.energies):
            for z in range(2):
                slab = 2 * e + z
                place = ((first + e) * stride + offset) * 2 + z
                rows = slice(slab * plan.entries, (slab + 1) * plan.entries)
                held_ref[place, : plan.entries] = message[rows].astype(F32)
                turned = tail if slab == 0 else pltpu.roll(tail, LANES - slab * plan.rest, 1)
                held_ref[place, plan.entries :] = turned


def polar_kernel(plan, rank_ref, table_ref, *refs):
    chips = plan.n_energy
    out_ref, low_ref, high_ref = refs[3 * chips :]
    rank = rank_ref[0]
    stage_blocks(plan, rank, refs[:chips], low_ref, 2, 0)
    stage_blocks(plan, rank, refs[chips : 2 * chips], low_ref, 2, 1)
    stage_blocks(plan, rank, refs[2 * chips : 3 * chips], high_ref, 1, 0)
    count = plan.all_energies

    def step(chunk, sums):
        rows = pl.ds(pl.multiple_of(chunk * 8, 8), 8)
        sums = list(sums)
        for energy in range(count):
            high_re, high_im = high_ref[2 * energy, rows], high_ref[2 * energy + 1, rows]
            for energy_step in range(1, REACH + 1):
                if energy + energy_step >= count:
                    continue
                for q in range(2):
                    index = ((energy_step - 1) * 2 + q) * 2
                    low = ((energy + energy_step) * 2 + q) * 2
                    low_re, low_im = low_ref[low, rows], low_ref[low + 1, rows]
                    sums[index] = sums[index] + (low_re * high_re + low_im * high_im)
                    sums[index + 1] = sums[index + 1] + (low_im * high_re - low_re * high_im)
        return tuple(sums)

    none = tuple(jnp.zeros((8, LANES), F32) for _ in range(2 * plan.classes))
    main = lax.fori_loop(0, plan.entries // 8, step, none, unroll=3)
    rest = lax.fori_loop(plan.entries // 8, plan.held // 8, step, none, unroll=5)
    scale = float(count * 2 * plan.entries) ** (-0.5)
    lines = [jnp.sum(part, axis=0, keepdims=True) * scale for part in main + rest]
    sums = jnp.concatenate(lines, axis=0)
    lines = 2 * plan.classes
    picks = jnp.concatenate([table_ref[:lines], table_ref[2 * lines : 3 * lines]], axis=0)
    picked = lax.dot_general(
        picks, sums, (((0,), (0,)), ((), ())), precision=HIGH, preferred_element_type=F32
    )
    out_ref[...] = picked.reshape(out_ref.shape)


def energy_kernel(plan, rank_ref, table_ref, coupling_ref, *refs):
    chips = plan.n_energy
    outs = refs[2 * chips : 3 * chips]
    low_ref, sum_ref, weight_ref = refs[3 * chips :]
    rank = rank_ref[0]
    flat = coupling_ref[...].reshape(plan.devices * 8, LANES)
    weight_ref[...] = jnp.dot(table_ref[...], flat, precision=HIGH, preferred_element_type=F32)
    stage_blocks(plan, rank, refs[:chips], low_ref, 2, 0)
    stage_blocks(plan, rank, refs[chips : 2 * chips], low_ref, 2, 1)
    count = plan.all_energies

    def run(base):
        def step(chunk, carry):
            rows = pl.ds(pl.multiple_of(chunk * 8, 8), 8)
            re = [None] * count
            im = [None] * count
            for energy_step in range(1, REACH + 1):
                for q in range(2):
                    index = base + ((energy_step - 1) * 2 + q) * 2
                    for part, sign in ((0, -1), (1, 1)):
                        at = index + part * 2 * plan.classes
                        w_re = jnp.broadcast_to(weight_ref[at : at + 1], (8, LANES))
                        w_im = jnp.broadcast_to(weight_ref[at + 1 : at + 2], (8, LANES))
                        for energy in range(count):
                            other = energy + sign * energy_step
                            if other < 0 or other >= count:
                                continue
                            at = (other * 2 + q) * 2
                            b_re, b_im = low_ref[at, rows], low_ref[at + 1, rows]
                            t_re = w_re * b_re - w_im * b_im
                            t_im = w_re * b_im + w_im * b_re
                            re[energy] = t_re if re[energy] is None else re[energy] + t_re
                            im[energy] = t_im if im[energy] is None else im[energy] + t_im
            for energy in range(count):
                sum_ref[2 * energy, rows] = re[energy]
                sum_ref[2 * energy + 1, rows] = im[energy]
            return carry

        return step

    lax.fori_loop(0, plan.entries // 8, run(0), 0, unroll=2)
    lax.fori_loop(plan.entries // 8, plan.held // 8, run(4 * plan.classes), 0, unroll=5)
    lane = lax.broadcasted_iota(jnp.int32, (plan.rest_pad, LANES), 1)
    for partner in range(chips):
        first = plan.energies * (rank ^ partner)
        tail = jnp.zeros((plan.rest_pad, LANES), F32)
        for slab in range(plan.slabs):
            place = 2 * first + slab
            rows = slice(slab * plan.entries, (slab + 1) * plan.entries)
            outs[partner][rows] = sum_ref[place, : plan.entries].astype(BF16)
            piece = sum_ref[place, plan.entries :]
            if slab:
                piece = pltpu.roll(piece, slab * plan.rest, 1)
            mine = (lane >= slab * plan.rest) & (lane < (slab + 1) * plan.rest)
            tail = jnp.where(mine, piece, tail)
        if plan.tail > plan.rest_pad:
            blank = jnp.zeros((plan.tail - plan.rest_pad, LANES), F32)
            tail = jnp.concatenate([tail, blank], axis=0)
        outs[partner][plan.main_rows :] = tail.astype(BF16)


def gather_kernel(plan, rank_ref, *refs):
    chips = plan.n_energy
    out_ref, rest_ref, held_ref, sems = refs[chips:]
    rank = rank_ref[0]
    copies = []
    for slab in range(plan.slabs):
        place = (slab // 2, 0, slab % 2)
        for partner, message in enumerate(refs[:chips]):
            source = rank ^ partner
            lanes = pl.ds(pl.multiple_of(source * LANES, LANES), LANES)
            tail = message[plan.main_rows :].astype(F32)[: plan.rest_pad]
            rows = slice(slab * plan.entries, (slab + 1) * plan.entries)
            held_ref[slab // 2, 0, slab % 2, :, lanes] = message[rows]
            turned = tail if slab == 0 else pltpu.roll(tail, LANES - slab * plan.rest, 1)
            rest_ref[slab, source] = turned
        parts = [rest_ref[slab, source, : plan.rest_rows] for source in range(chips)]
        rest = jnp.concatenate(parts, axis=0)[:, : plan.rest]
        held_ref[slab // 2, 0, slab % 2, :, plan.tiles * LANES :] = rest.astype(BF16)
        copies.append(pltpu.make_async_copy(held_ref.at[place], out_ref.at[place], sems.at[slab]))
        copies[-1].start()
    for copy in copies:
        copy.wait()


def next_kernel(
    plan, polar_ref, ret_ref, near_ref, pair_ref, out_ref, v_ref, dense_ref, after_ref, sems
):
    bonds, atoms, order = plan.bonds, plan.atoms, plan.order
    padded = -(-bonds // 8) * 8
    lines = []
    for p in range(plan.n_phonon):
        rest = jnp.zeros((4, LANES), F32)
        for tile in range(plan.tiles):
            main = jnp.zeros((4, LANES), F32)
            for half in range(plan.n_momentum):
                block = polar_ref[(tile * plan.n_momentum + half) * plan.n_phonon + p]
                main = main + block[:4]
                rest = rest + block[4:]
            lines.append(main)
        lines.append(rest[:, : plan.rest])
    flat = jnp.concatenate(lines, axis=1)
    bond = lax.broadcasted_iota(jnp.int32, (padded, 1), 0)
    keep = bond == bond_of(plan, (1, plan.columns))
    tall = jnp.concatenate(
        [jnp.where(keep, flat[row : row + 1], 0.0) for row in range(2 * plan.modes)], axis=0
    )
    upper = tall.astype(BF16)
    lower = (tall - upper.astype(F32)).astype(BF16)
    contract = (((1,), (1,)), ((), ()))
    both = lax.dot_general(
        jnp.concatenate([upper, lower], axis=0), atom_table(plan), contract, preferred_element_type=F32
    )
    by_bond = both[: tall.shape[0]] + both[tall.shape[0] :]
    ways = [(i, j) for i in range(3) for j in range(i, 3)]
    near = near_ref[...]
    for row in range(2 * plan.modes):
        values = by_bond[row * padded : row * padded + bonds]
        values = [values * pair_ref[way] for way in range(len(ways))]
        sums = [jnp.zeros((bonds, atoms), F32) for _ in ways]
        for n in range(bonds):
            same = near == near[n : n + 1]
            for way in range(len(ways)):
                sums[way] = sums[way] + jnp.where(same, values[way][n : n + 1], 0.0)
        for way in range(len(ways)):
            v_ref[row * len(ways) + way, :bonds] = sums[way]

    near = near.astype(BF16)

    def build(m, first):
        number = (lax.broadcasted_iota(jnp.int32, (16, atoms), 0) + first).astype(BF16)
        for z in range(2):
            row = 2 * m + z
            blocks = [jnp.zeros((16, atoms), BF16) for _ in ways]
            for n in range(bonds):
                hit = number == near[n : n + 1]
                for way in range(len(ways)):
                    value = v_ref[row * len(ways) + way, n : n + 1].astype(BF16)
                    blocks[way] = jnp.where(hit, value, blocks[way])
            for way, (i, j) in enumerate(ways):
                block = blocks[way]
                other = block if z else -block
                for up, left in sorted({(j, i), (i, j)}):
                    place = pl.ds(pl.multiple_of(up * atoms + first, 16), 16)
                    dense_ref[m, place, pl.ds(z * order + left * atoms, atoms)] = block
                    place = pl.ds(pl.multiple_of(order + up * atoms + first, 16), 16)
                    dense_ref[m, place, pl.ds((1 - z) * order + left * atoms, atoms)] = other

    for m in range(plan.modes):
        for chunk in range(atoms // 16):
            build(m, chunk * 16)
    copies = []
    for m in range(plan.modes):
        ret = jnp.concatenate([ret_ref[m, 0], ret_ref[m, 1]], axis=1)
        half = jnp.dot(ret, dense_ref[m], preferred_element_type=F32).astype(BF16)
        half_re, half_im = half[:, :order], half[:, order:]
        for z, parts in enumerate(([half_re, -half_im], [half_im, half_re])):
            right = jnp.concatenate(parts, axis=1)
            after = lax.dot_general(ret, right, contract, preferred_element_type=F32)
            after_ref[m, z] = after.astype(BF16)
            copy = pltpu.make_async_copy(after_ref.at[m, z], out_ref.at[m, z], sems.at[m, z])
            copy.start()
            copies.append(copy)
    for copy in copies:
        copy.wait()


def swap(block, axis, distance):
    return lax.ppermute(block, axis, [(i, i ^ distance) for i in range(lax.axis_size(axis))])


def to_chips(plan, blocks):
    return [blocks[0]] + [swap(blocks[k], "energy", k) for k in range(1, plan.n_energy)]


def dealt(
    plan, g_less, g_great, d_less, d_ret, neighbours, bond_dirs, energy_offset, momentum_offset, absorb
):
    rank = lax.axis_index("energy").astype(jnp.int32).reshape(1)
    chips, held, count = plan.n_energy, plan.held, plan.all_energies
    lines = 2 * plan.classes
    modes = plan.devices * plan.modes
    message = jax.ShapeDtypeStruct((plan.message, LANES), BF16)

    def deal(blocks):
        return call(
            functools.partial(deal_kernel, plan), [message] * chips, rank, blocks,
            scalars=1, scratch=[pltpu.VMEM((plan.entries + plan.tail, LANES), F32)],
            moved=4 * blocks.size,
        )

    low_blocks = deal(g_less)
    own, g_great = lax.optimization_barrier((low_blocks[0], g_great))
    low_blocks = [own] + list(low_blocks[1:])
    low = to_chips(plan, low_blocks)
    high_blocks = deal(g_great)
    own, d_less, bond_dirs = lax.optimization_barrier((high_blocks[0], d_less, bond_dirs))
    high = to_chips(plan, [own] + list(high_blocks[1:]))
    low[0], low[1] = lax.optimization_barrier((low[0], low[1]))
    low_beside = [swap(block, "momentum", 1) for block in low]
    small = jax.ShapeDtypeStruct((plan.devices, 8, LANES), F32)
    coupling, table, pairs = call(
        functools.partial(couple_kernel, plan),
        [
            small,
            jax.ShapeDtypeStruct((4 * lines, plan.devices * 8), F32),
            jax.ShapeDtypeStruct((6, plan.bonds, plan.atoms), F32),
        ],
        d_less.transpose(0, 2, 3, 1, 4), bond_dirs.transpose(1, 0, 2),
        energy_offset.reshape(1, modes), momentum_offset.reshape(1, modes), absorb.reshape(1, modes),
        scratch=[pltpu.VMEM((-(-2 * plan.bonds * plan.modes // 16) * 16, plan.atoms), F32)],
        moved=4 * d_less.size,
    )
    coupling = lax.all_to_all(coupling, EVERY, 0, 0, tiled=True)
    low_scratch = pltpu.VMEM((4 * count, held, LANES), F32)
    half_scratch = pltpu.VMEM((2 * count, held, LANES), F32)
    polar = call(
        functools.partial(polar_kernel, plan), small, rank, table, *low, *low_beside, *high,
        scalars=1, scratch=[low_scratch, half_scratch], moved=8 * 2**20,
    )
    polar = lax.all_to_all(polar, EVERY, 0, 0, tiled=True)
    sums = call(
        functools.partial(energy_kernel, plan), [message] * chips,
        rank, table, coupling, *low, *low_beside,
        scalars=1, scratch=[low_scratch, half_scratch, pltpu.VMEM((4 * lines, LANES), F32)],
        moved=8 * 2**20,
    )
    sums = to_chips(plan, sums)
    padded = -(-plan.bonds // 8) * 8
    d_next = call(
        functools.partial(next_kernel, plan), jax.ShapeDtypeStruct(d_ret.shape, BF16),
        polar, d_ret, neighbours, pairs,
        out_space=pltpu.HBM,
        scratch=[
            pltpu.VMEM((12 * plan.modes, padded, plan.atoms), F32),
            pltpu.VMEM((plan.modes, 2 * plan.order, 2 * plan.order), BF16),
            pltpu.VMEM(d_ret.shape, BF16),
            pltpu.SemaphoreType.DMA((plan.modes, 2)),
        ],
        moved=20 * 2**20,
    )
    d_next, own = lax.optimization_barrier((d_next, sums[0]))
    self_energy = call(
        functools.partial(gather_kernel, plan), jax.ShapeDtypeStruct(g_less.shape, BF16), rank,
        own, *sums[1:],
        scalars=1, out_space=pltpu.HBM, moved=4 * 2**20,
        scratch=[
            pltpu.VMEM((plan.slabs, chips, plan.rest_pad, LANES), F32),
            pltpu.VMEM(g_less.shape, BF16),
            pltpu.SemaphoreType.DMA((plan.slabs,)),
        ],
    )
    return self_energy, d_next


def local(*arrays):
    plan = Plan(
        arrays[0].shape, arrays[2].shape, arrays[3].shape,
        lax.axis_size("energy"), lax.axis_size("momentum"), lax.axis_size("phonon"),
    )
    return dealt(plan, *arrays) if plan.fits() else general(*arrays)


def solution(mesh):
    in_specs = (
        P("energy", "momentum", None, None, "phonon"),
        P("energy", "momentum", None, None, "phonon"),
        P(("energy", "momentum", "phonon"), None, None, None, None),
        P(("energy", "momentum", "phonon"), None, None, None),
        P(),
        P(),
        P(),
        P(),
        P(),
    )
    out_specs = (
        P("energy", "momentum", None, None, "phonon"),
        P(("energy", "momentum", "phonon"), None, None, None),
    )
    return jax.shard_map(local, mesh=mesh, in_specs=in_specs, out_specs=out_specs, check_vma=False)
```

```python
import functools

import jax
import jax.numpy as jnp
from jax import lax
from jax.experimental import pallas as pl
from jax.experimental.pallas import tpu as pltpu
from jax.sharding import PartitionSpec as P

ORB = 12
REACH = 4
LANES = 128


HIGH = lax.Precision.HIGHEST


def shifted_2(block, axis, distance):
    devices = range(lax.axis_size(axis))
    route = [(i - distance, i) for i in devices if i - distance in devices]
    return lax.ppermute(block, axis, route)


def scaled_blocks(weights, blocks):
    real_w = weights[None, :, :, 0, None, :]
    imag_w = weights[None, :, :, 1, None, :]
    real_b = blocks[:, None, :, 0].astype(jnp.float32)
    imag_b = blocks[:, None, :, 1].astype(jnp.float32)
    real_part = jnp.sum(real_w * real_b - imag_w * imag_b, axis=2)
    imag_part = jnp.sum(real_w * imag_b + imag_w * real_b, axis=2)
    return jnp.stack([real_part, imag_part], axis=2)


def inner_sums(local_blocks, shifted):
    local_real = local_blocks[:, :, 0].astype(jnp.float32)[:, :, None]
    local_imag = local_blocks[:, :, 1].astype(jnp.float32)[:, :, None]
    other_real = shifted[:, :, 0].astype(jnp.float32)[:, None]
    other_imag = shifted[:, :, 1].astype(jnp.float32)[:, None]
    real_sum = jnp.sum(local_real * other_real + local_imag * other_imag, axis=(0, 3))
    imag_sum = jnp.sum(local_imag * other_real - local_real * other_imag, axis=(0, 3))
    return jnp.stack([real_sum, imag_sum], axis=2)


def times_adjoint(left, right):
    return jnp.einsum("mab,mcb->mac", left, right, preferred_element_type=jnp.float32)


def times_plain(left, right):
    return jnp.einsum("mab,mbc->mac", left, right, preferred_element_type=jnp.float32)


def general(
    g_less, g_great, d_less, d_ret, neighbours, bond_dirs, energy_offset, momentum_offset, absorb
):
    energies = g_less.shape[0]
    momenta_here = g_less.shape[1]
    local_width = g_less.shape[4]
    bonds = d_less.shape[3]
    whole_atoms = d_less.shape[4]
    atom_share = local_width // bonds
    all_momenta = momenta_here * lax.axis_size("momentum")
    all_energies = energies * lax.axis_size("energy")
    modes_here = d_less.shape[0]
    order = d_ret.shape[2]
    classes = REACH * all_momenta
    energy_rank = lax.axis_index("energy")
    momentum_rank = lax.axis_index("momentum")
    phonon_rank = lax.axis_index("phonon")
    span = -(-REACH // energies)
    lower_steps = list(range(span, 0, -1))
    both_steps = lower_steps + list(range(-1, -span - 1, -1))
    label = (energy_offset - 1) * all_momenta + momentum_offset
    table = (label[:, None] == jnp.arange(classes, dtype=jnp.int32)[None, :]).astype(jnp.float32)
    soaked = table * absorb[:, None]
    pair_cube = bond_dirs[:, None] * bond_dirs[None, :]
    pair = pair_cube.reshape((9,) + bond_dirs.shape[1:])
    coupling = jnp.sum(d_less * pair[None, None], axis=2)
    first_mode = (
        (energy_rank * lax.axis_size("momentum") + momentum_rank) * lax.axis_size("phonon")
        + phonon_rank
    ) * modes_here
    own_table = lax.dynamic_slice_in_dim(table, first_mode, modes_here, 0)
    spread = lax.all_to_all(
        coupling.astype(jnp.bfloat16), "phonon", split_axis=3, concat_axis=0, tiled=True
    ).astype(coupling.dtype)
    blank = jnp.zeros((classes, 2 * bonds * atom_share), jnp.float32)
    piece = lax.all_gather(
        spread.astype(jnp.bfloat16), ("energy", "momentum"), axis=0, tiled=True
    ).astype(jnp.float32)
    rows = piece.shape[0]
    flat_piece = piece.reshape(rows, -1)
    emitted = blank + jnp.einsum("mc,mx->cx", table, flat_piece, precision=HIGH)
    absorbed = blank + jnp.einsum("mc,mx->cx", soaked, flat_piece, precision=HIGH)
    emitted = emitted.reshape(classes, 2, bonds, atom_share)
    absorbed = absorbed.reshape(classes, 2, bonds, atom_share)
    emit_table = emitted.transpose(0, 1, 3, 2).reshape(REACH, all_momenta, 2, local_width)
    soak_table = absorbed.transpose(0, 1, 3, 2).reshape(REACH, all_momenta, 2, local_width)
    moved = [shifted_2(g_less, "energy", step) for step in both_steps]
    lower = jnp.concatenate(moved[:span], axis=0)
    upper = jnp.concatenate(moved[span:], axis=0)
    lesser_rimmed = jnp.concatenate([lower, g_less, upper], axis=0)
    greater_moved = [shifted_2(g_great, "energy", step) for step in lower_steps]
    greater_rim = jnp.concatenate(greater_moved, axis=0)
    greater_rimmed = jnp.concatenate([greater_rim, g_great], axis=0)
    lesser_wide, greater_wide = (
        lax.all_gather(lesser_rimmed, "momentum", axis=1, tiled=True),
        lax.all_gather(greater_rimmed, "momentum", axis=1, tiled=True),
    )
    here_moment = momentum_rank * momenta_here + jnp.arange(momenta_here, dtype=jnp.int32)
    every_moment = jnp.arange(all_momenta, dtype=jnp.int32)
    behind = (here_moment[:, None] - every_moment[None, :]) % all_momenta
    ahead = (every_moment[None, :] - here_moment[:, None]) % all_momenta
    pick_behind = (behind[:, :, None] == every_moment[None, None, :]).astype(jnp.float32)
    pick_ahead = (ahead[:, :, None] == every_moment[None, None, :]).astype(jnp.float32)
    total = jnp.zeros(g_less.shape, jnp.float32)
    polar_parts = []
    for energy_step in range(1, REACH + 1):
        below = lesser_wide[REACH - energy_step : REACH - energy_step + energies]
        above = lesser_wide[REACH + energy_step : REACH + energy_step + energies]
        weight_below = jnp.einsum(
            "lkq,qzx->lkzx", pick_behind, emit_table[energy_step - 1], precision=HIGH
        )
        weight_above = jnp.einsum(
            "lkq,qzx->lkzx", pick_ahead, soak_table[energy_step - 1], precision=HIGH
        )
        total = total + scaled_blocks(weight_below, below) + scaled_blocks(weight_above, above)
        earlier = greater_wide[REACH - energy_step : REACH - energy_step + energies]
        pairs = inner_sums(g_less, earlier)
        polar_parts.append(jnp.einsum("lkq,lkzx->qzx", pick_behind, pairs, precision=HIGH))
    self_energy = total.astype(jnp.bfloat16)
    scale = float(all_energies * all_momenta * ORB * ORB) ** (-0.5)
    polar_local = jnp.stack(polar_parts).reshape(classes, 2, local_width) * scale
    polar_summed = lax.psum(polar_local, ("energy", "momentum"))
    polar_full = lax.all_gather(polar_summed, "phonon", axis=2, tiled=True)
    own_polar = jnp.einsum("mc,czx->mzx", own_table, polar_full, precision=HIGH)
    own_polar = own_polar.reshape(modes_here, 2, whole_atoms, bonds).transpose(0, 1, 3, 2)
    link = (
        neighbours[:, :, None] == jnp.arange(whole_atoms, dtype=jnp.int32)[None, None, :]
    ).astype(jnp.float32)
    weighted = pair_cube[None, None] * own_polar[:, :, None, None]
    dense = jnp.einsum("mzijna,nab->mziajb", weighted, link, precision=HIGH)
    dense = dense.reshape(modes_here, 2, order, order).astype(jnp.bfloat16)
    dense_re, dense_im = (dense[:, 0], dense[:, 1])
    ret_re, ret_im = (d_ret[:, 0], d_ret[:, 1])
    half_re = (times_adjoint(dense_re, ret_re) + times_adjoint(dense_im, ret_im)).astype(
        jnp.bfloat16
    )
    half_im = (times_adjoint(dense_im, ret_re) - times_adjoint(dense_re, ret_im)).astype(
        jnp.bfloat16
    )
    next_re = times_plain(ret_re, half_re) - times_plain(ret_im, half_im)
    next_im = times_plain(ret_re, half_im) + times_plain(ret_im, half_re)
    d_next = jnp.stack([next_re, next_im], axis=1).astype(jnp.bfloat16)
    return (self_energy, d_next)


EVERY = ("energy", "momentum", "phonon")
F32 = jnp.float32
BF16 = jnp.bfloat16


class Plan:
    def __init__(self, g_shape, d_shape, ret_shape, n_energy, n_momentum, n_phonon):
        self.energies, self.momenta, _, self.entries, self.width = g_shape
        self.modes, _, _, self.bonds, self.atoms = d_shape
        self.order = ret_shape[2]
        self.n_energy = n_energy
        self.n_momentum = n_momentum
        self.n_phonon = n_phonon
        self.devices = n_energy * n_momentum * n_phonon
        self.all_energies = self.energies * n_energy
        self.all_momenta = self.momenta * n_momentum
        self.classes = REACH * self.all_momenta
        self.slabs = 2 * self.energies
        self.tiles = self.width // LANES
        self.rest = self.width % LANES
        self.rest_rows = self.entries // n_energy
        self.main_rows = self.slabs * self.entries
        self.rest_pad = -(-self.rest_rows // 8) * 8
        self.message = -(-(self.main_rows + self.rest_pad) // 16) * 16
        self.tail = self.message - self.main_rows
        self.held = self.entries + self.rest_pad
        self.columns = self.width * n_phonon

    def fits(self):
        return (
            self.momenta == 1
            and self.all_momenta == 2
            and self.n_energy == self.tiles
            and self.n_energy & (self.n_energy - 1) == 0
            and self.entries % 16 == 0
            and self.entries % self.n_energy == 0
            and self.rest > 0
            and self.slabs * self.rest == LANES
            and self.modes <= 2
            and self.atoms == LANES
            and self.order == 3 * self.atoms
            and self.all_energies <= 8
        )


def call(kernel, out_shape, *operands, scratch=(), scalars=0, flops=0, moved=0, out_space=pltpu.VMEM):
    smem = pl.BlockSpec(memory_space=pltpu.SMEM)
    vmem = pl.BlockSpec(memory_space=pltpu.VMEM)
    specs = [smem] * scalars + [vmem] * (len(operands) - scalars)
    many = isinstance(out_shape, (list, tuple))
    return pl.pallas_call(
        kernel,
        out_shape=out_shape,
        in_specs=specs,
        out_specs=[vmem] * len(out_shape) if many else pl.BlockSpec(memory_space=out_space),
        scratch_shapes=list(scratch),
        compiler_params=pltpu.CompilerParams(vmem_limit_bytes=48 * 2**20),
        cost_estimate=pl.CostEstimate(flops=flops, bytes_accessed=moved, transcendentals=0),
    )(*operands)


def deal_kernel(plan, rank_ref, source_ref, *refs):
    outs, rest_ref = refs[: plan.n_energy], refs[plan.n_energy]
    rank = rank_ref[0]
    slabs = [(e, z) for e in range(plan.energies) for z in range(2)]
    pieces = [source_ref[e, 0, z, :, plan.tiles * LANES :].astype(F32) for e, z in slabs]
    rest_ref[: plan.entries] = jnp.concatenate(pieces, axis=1)
    rest_ref[plan.entries :] = jnp.zeros((plan.tail, LANES), F32)
    for partner in range(plan.n_energy):
        target = rank ^ partner
        lanes = pl.ds(pl.multiple_of(target * LANES, LANES), LANES)
        for slab, (e, z) in enumerate(slabs):
            rows = slice(slab * plan.entries, (slab + 1) * plan.entries)
            outs[partner][rows] = source_ref[e, 0, z, :, lanes]
        rest = rest_ref[pl.ds(target * plan.rest_rows, plan.tail), :]
        outs[partner][plan.main_rows :] = rest.astype(BF16)


def bond_of(plan, shape):
    column = lax.broadcasted_iota(jnp.int32, shape, len(shape) - 1)
    atom = jnp.floor((column.astype(F32) + 0.5) * (1.0 / plan.bonds)).astype(jnp.int32)
    return column - atom * plan.bonds


def atom_table(plan):
    atom = lax.broadcasted_iota(jnp.int32, (plan.atoms, plan.columns), 0)
    column = lax.broadcasted_iota(jnp.int32, (plan.atoms, plan.columns), 1)
    inside = column - atom * plan.bonds
    return jnp.where((inside >= 0) & (inside < plan.bonds), 1.0, 0.0).astype(BF16)


def mode_table(plan, energy_ref, momentum_ref, absorb_ref):
    width = plan.devices * 8
    modes = plan.devices * plan.modes
    label = (energy_ref[...] - 1) * plan.all_momenta + momentum_ref[...]
    stacked = jnp.concatenate(
        [label.astype(F32), absorb_ref[...], jnp.zeros((6, modes), F32)], axis=0
    )
    mode = lax.broadcasted_iota(jnp.int32, (modes, width), 0)
    column = lax.broadcasted_iota(jnp.int32, (modes, width), 1)
    inner = (column & 3) >> 1
    chosen = (mode == (column >> 3) * plan.modes + inner) & (inner < plan.modes)
    spread = jnp.dot(
        stacked, jnp.where(chosen, 1.0, 0.0), precision=HIGH, preferred_element_type=F32
    )
    label = (spread[:1] + 0.5).astype(jnp.int32)
    column = lax.broadcasted_iota(jnp.int32, (2 * plan.classes, width), 1)
    row = lax.broadcasted_iota(jnp.int32, (2 * plan.classes, width), 0)
    hit = (label == (row >> 1)) & ((column & 1) == (row & 1))
    hit = hit & (((column & 3) >> 1) < plan.modes)
    blocks = []
    for kind in range(2):
        here = hit & (((column >> 2) & 1) == kind)
        blocks.append(jnp.where(here, 1.0, 0.0))
        blocks.append(jnp.where(here, spread[1:2], 0.0))
    return jnp.concatenate(blocks, axis=0)


def couple_kernel(
    plan, less_ref, dirs_ref, energy_ref, momentum_ref, absorb_ref,
    out_ref, table_ref, pair_ref, held_ref,
):
    bonds, width = plan.bonds, plan.width
    held_ref[...] = jnp.zeros(held_ref.shape, F32)
    for n in range(bonds):
        pairs = [dirs_ref[n, i : i + 1] * dirs_ref[n, j : j + 1] for i in range(3) for j in range(3)]
        for way, (i, j) in enumerate((i, j) for i in range(3) for j in range(i, 3)):
            pair_ref[way, n : n + 1] = pairs[3 * i + j]
        for m in range(plan.modes):
            total = less_ref[m, 0, n] * pairs[0]
            for t in range(1, 9):
                total = total + less_ref[m, t, n] * pairs[t]
            row = (m * bonds + n) * 2
            held_ref[row : row + 2] = total
    rows = held_ref.shape[0]
    spread = jnp.dot(held_ref[...].astype(BF16), atom_table(plan), preferred_element_type=F32)
    row = lax.broadcasted_iota(jnp.int32, (rows, 1), 0)
    bond = (row >> 1) - jnp.where(row >= 2 * bonds, bonds, 0)
    keep = bond == bond_of(plan, (1, plan.columns))
    kept = jnp.where(keep, spread, 0.0).astype(BF16)
    line = lax.broadcasted_iota(jnp.int32, (8, rows), 0)
    row = lax.broadcasted_iota(jnp.int32, (8, rows), 1)
    owner = jnp.where(row >= 2 * bonds, 2, 0) + (row & 1)
    gather = jnp.where((line == owner) & (row < 2 * bonds * plan.modes), 1.0, 0.0).astype(BF16)
    flat = jnp.dot(gather, kept, preferred_element_type=F32)[:4]
    for p in range(plan.n_phonon):
        start = p * width
        rest = flat[:, start + plan.tiles * LANES : start + width]
        rest = jnp.concatenate([rest, jnp.zeros((4, LANES - plan.rest), F32)], axis=1)
        for tile in range(plan.tiles):
            main = flat[:, start + tile * LANES : start + (tile + 1) * LANES]
            block = jnp.concatenate([main, rest], axis=0)
            for half in range(plan.n_momentum):
                out_ref[(tile * plan.n_momentum + half) * plan.n_phonon + p] = block
    table_ref[...] = mode_table(plan, energy_ref, momentum_ref, absorb_ref)


def stage_blocks(plan, rank, messages, held_ref, stride, offset):
    row = lax.broadcasted_iota(jnp.int32, (plan.rest_pad, LANES), 0)
    for partner, message in enumerate(messages):
        first = plan.energies * (rank ^ partner)
        tail = message[plan.main_rows :].astype(F32)[: plan.rest_pad]
        tail = jnp.where(row < plan.rest_rows, tail, 0.0)
        for e in range(plan.energies):
            for z in range(2):
                slab = 2 * e + z
                place = ((first + e) * stride + offset) * 2 + z
                rows = slice(slab * plan.entries, (slab + 1) * plan.entries)
                held_ref[place, : plan.entries] = message[rows].astype(F32)
                turned = tail if slab == 0 else pltpu.roll(tail, LANES - slab * plan.rest, 1)
                held_ref[place, plan.entries :] = turned


def polar_kernel(plan, rank_ref, table_ref, *refs):
    chips = plan.n_energy
    out_ref, low_ref, high_ref = refs[3 * chips :]
    rank = rank_ref[0]
    stage_blocks(plan, rank, refs[:chips], low_ref, 2, 0)
    stage_blocks(plan, rank, refs[chips : 2 * chips], low_ref, 2, 1)
    stage_blocks(plan, rank, refs[2 * chips : 3 * chips], high_ref, 1, 0)
    count = plan.all_energies

    def step(chunk, sums):
        rows = pl.ds(pl.multiple_of(chunk * 8, 8), 8)
        sums = list(sums)
        for energy in range(count):
            high_re, high_im = high_ref[2 * energy, rows], high_ref[2 * energy + 1, rows]
            for energy_step in range(1, REACH + 1):
                if energy + energy_step >= count:
                    continue
                for q in range(2):
                    index = ((energy_step - 1) * 2 + q) * 2
                    low = ((energy + energy_step) * 2 + q) * 2
                    low_re, low_im = low_ref[low, rows], low_ref[low + 1, rows]
                    sums[index] = sums[index] + (low_re * high_re + low_im * high_im)
                    sums[index + 1] = sums[index + 1] + (low_im * high_re - low_re * high_im)
        return tuple(sums)

    none = tuple(jnp.zeros((8, LANES), F32) for _ in range(2 * plan.classes))
    main = lax.fori_loop(0, plan.entries // 8, step, none, unroll=3)
    rest = lax.fori_loop(plan.entries // 8, plan.held // 8, step, none, unroll=5)
    scale = float(count * 2 * plan.entries) ** (-0.5)
    lines = [jnp.sum(part, axis=0, keepdims=True) * scale for part in main + rest]
    sums = jnp.concatenate(lines, axis=0)
    lines = 2 * plan.classes
    picks = jnp.concatenate([table_ref[:lines], table_ref[2 * lines : 3 * lines]], axis=0)
    picked = lax.dot_general(
        picks, sums, (((0,), (0,)), ((), ())), precision=HIGH, preferred_element_type=F32
    )
    out_ref[...] = picked.reshape(out_ref.shape)


def energy_kernel(plan, rank_ref, table_ref, coupling_ref, *refs):
    chips = plan.n_energy
    outs = refs[2 * chips : 3 * chips]
    low_ref, sum_ref, weight_ref, mixed_ref = refs[3 * chips :]
    rank = rank_ref[0]
    flat = coupling_ref[...].reshape(plan.devices * 8, LANES)
    weights = jnp.dot(table_ref[...], flat, precision=HIGH, preferred_element_type=F32)
    following = pltpu.roll(weights, weights.shape[0] - 1, 0)
    weight_ref[...] = weights
    mixed_ref[0] = weights + following
    mixed_ref[1] = following - weights
    stage_blocks(plan, rank, refs[:chips], low_ref, 2, 0)
    stage_blocks(plan, rank, refs[chips : 2 * chips], low_ref, 2, 1)
    count = plan.all_energies

    def run(base):
        def step(chunk, carry):
            rows = pl.ds(pl.multiple_of(chunk * 8, 8), 8)
            both = [low_ref[2 * at, rows] + low_ref[2 * at + 1, rows] for at in range(2 * count)]
            parts = [[None] * count for _ in range(3)]
            for energy_step in range(1, REACH + 1):
                for q in range(2):
                    index = base + ((energy_step - 1) * 2 + q) * 2
                    for kind, sign in ((0, -1), (1, 1)):
                        at = index + kind * 2 * plan.classes
                        w_re = jnp.broadcast_to(weight_ref[at : at + 1], (8, LANES))
                        w_sum = jnp.broadcast_to(mixed_ref[0, at : at + 1], (8, LANES))
                        w_dif = jnp.broadcast_to(mixed_ref[1, at : at + 1], (8, LANES))
                        for energy in range(count):
                            other = energy + sign * energy_step
                            if other < 0 or other >= count:
                                continue
                            at = other * 2 + q
                            terms = (
                                w_re * both[at],
                                w_sum * low_ref[2 * at + 1, rows],
                                w_dif * low_ref[2 * at, rows],
                            )
                            for part, term in zip(parts, terms):
                                part[energy] = term if part[energy] is None else part[energy] + term
            for energy in range(count):
                sum_ref[2 * energy, rows] = parts[0][energy] - parts[1][energy]
                sum_ref[2 * energy + 1, rows] = parts[0][energy] + parts[2][energy]
            return carry

        return step

    lax.fori_loop(0, plan.entries // 8, run(0), 0, unroll=2)
    lax.fori_loop(plan.entries // 8, plan.held // 8, run(4 * plan.classes), 0, unroll=5)
    lane = lax.broadcasted_iota(jnp.int32, (plan.rest_pad, LANES), 1)
    for partner in range(chips):
        first = plan.energies * (rank ^ partner)
        tail = jnp.zeros((plan.rest_pad, LANES), F32)
        for slab in range(plan.slabs):
            place = 2 * first + slab
            rows = slice(slab * plan.entries, (slab + 1) * plan.entries)
            outs[partner][rows] = sum_ref[place, : plan.entries].astype(BF16)
            piece = sum_ref[place, plan.entries :]
            if slab:
                piece = pltpu.roll(piece, slab * plan.rest, 1)
            mine = (lane >= slab * plan.rest) & (lane < (slab + 1) * plan.rest)
            tail = jnp.where(mine, piece, tail)
        if plan.tail > plan.rest_pad:
            blank = jnp.zeros((plan.tail - plan.rest_pad, LANES), F32)
            tail = jnp.concatenate([tail, blank], axis=0)
        outs[partner][plan.main_rows :] = tail.astype(BF16)


def gather_kernel(plan, rank_ref, *refs):
    chips = plan.n_energy
    out_ref, rest_ref, held_ref, sems = refs[chips:]
    rank = rank_ref[0]
    copies = []
    for slab in range(plan.slabs):
        place = (slab // 2, 0, slab % 2)
        for partner, message in enumerate(refs[:chips]):
            source = rank ^ partner
            lanes = pl.ds(pl.multiple_of(source * LANES, LANES), LANES)
            tail = message[plan.main_rows :].astype(F32)[: plan.rest_pad]
            rows = slice(slab * plan.entries, (slab + 1) * plan.entries)
            held_ref[slab // 2, 0, slab % 2, :, lanes] = message[rows]
            turned = tail if slab == 0 else pltpu.roll(tail, LANES - slab * plan.rest, 1)
            rest_ref[slab, source] = turned
        parts = [rest_ref[slab, source, : plan.rest_rows] for source in range(chips)]
        rest = jnp.concatenate(parts, axis=0)[:, : plan.rest]
        held_ref[slab // 2, 0, slab % 2, :, plan.tiles * LANES :] = rest.astype(BF16)
        copies.append(pltpu.make_async_copy(held_ref.at[place], out_ref.at[place], sems.at[slab]))
        copies[-1].start()
    for copy in copies:
        copy.wait()


def next_kernel(
    plan, polar_ref, ret_ref, near_ref, pair_ref, out_ref, v_ref, dense_ref, after_ref, sems
):
    bonds, atoms, order = plan.bonds, plan.atoms, plan.order
    padded = -(-bonds // 8) * 8
    lines = []
    for p in range(plan.n_phonon):
        rest = jnp.zeros((4, LANES), F32)
        for tile in range(plan.tiles):
            main = jnp.zeros((4, LANES), F32)
            for half in range(plan.n_momentum):
                block = polar_ref[(tile * plan.n_momentum + half) * plan.n_phonon + p]
                main = main + block[:4]
                rest = rest + block[4:]
            lines.append(main)
        lines.append(rest[:, : plan.rest])
    flat = jnp.concatenate(lines, axis=1)
    bond = lax.broadcasted_iota(jnp.int32, (padded, 1), 0)
    keep = bond == bond_of(plan, (1, plan.columns))
    tall = jnp.concatenate(
        [jnp.where(keep, flat[row : row + 1], 0.0) for row in range(2 * plan.modes)], axis=0
    )
    upper = tall.astype(BF16)
    lower = (tall - upper.astype(F32)).astype(BF16)
    contract = (((1,), (1,)), ((), ()))
    both = lax.dot_general(
        jnp.concatenate([upper, lower], axis=0), atom_table(plan), contract, preferred_element_type=F32
    )
    by_bond = both[: tall.shape[0]] + both[tall.shape[0] :]
    ways = [(i, j) for i in range(3) for j in range(i, 3)]
    near = near_ref[...]
    for row in range(2 * plan.modes):
        values = by_bond[row * padded : row * padded + bonds]
        values = [values * pair_ref[way] for way in range(len(ways))]
        sums = [jnp.zeros((bonds, atoms), F32) for _ in ways]
        for n in range(bonds):
            same = near == near[n : n + 1]
            for way in range(len(ways)):
                sums[way] = sums[way] + jnp.where(same, values[way][n : n + 1], 0.0)
        for way in range(len(ways)):
            v_ref[row * len(ways) + way, :bonds] = sums[way]

    near = near.astype(BF16)

    def build(m, first):
        number = (lax.broadcasted_iota(jnp.int32, (16, atoms), 0) + first).astype(BF16)
        for z in range(2):
            row = 2 * m + z
            blocks = [jnp.zeros((16, atoms), BF16) for _ in ways]
            for n in range(bonds):
                hit = number == near[n : n + 1]
                for way in range(len(ways)):
                    value = v_ref[row * len(ways) + way, n : n + 1].astype(BF16)
                    blocks[way] = jnp.where(hit, value, blocks[way])
            for way, (i, j) in enumerate(ways):
                block = blocks[way]
                other = block if z else -block
                for up, left in sorted({(j, i), (i, j)}):
                    place = pl.ds(pl.multiple_of(up * atoms + first, 16), 16)
                    dense_ref[m, place, pl.ds(z * order + left * atoms, atoms)] = block
                    place = pl.ds(pl.multiple_of(order + up * atoms + first, 16), 16)
                    dense_ref[m, place, pl.ds((1 - z) * order + left * atoms, atoms)] = other

    for m in range(plan.modes):
        for chunk in range(atoms // 16):
            build(m, chunk * 16)
    copies = []
    for m in range(plan.modes):
        ret = jnp.concatenate([ret_ref[m, 0], ret_ref[m, 1]], axis=1)
        half = jnp.dot(ret, dense_ref[m], preferred_element_type=F32).astype(BF16)
        half_re, half_im = half[:, :order], half[:, order:]
        for z, parts in enumerate(([half_re, -half_im], [half_im, half_re])):
            right = jnp.concatenate(parts, axis=1)
            after = lax.dot_general(ret, right, contract, preferred_element_type=F32)
            after_ref[m, z] = after.astype(BF16)
            copy = pltpu.make_async_copy(after_ref.at[m, z], out_ref.at[m, z], sems.at[m, z])
            copy.start()
            copies.append(copy)
    for copy in copies:
        copy.wait()


def swap(block, axis, distance):
    return lax.ppermute(block, axis, [(i, i ^ distance) for i in range(lax.axis_size(axis))])


def to_chips(plan, blocks):
    return [blocks[0]] + [swap(blocks[k], "energy", k) for k in range(1, plan.n_energy)]


def dealt(
    plan, g_less, g_great, d_less, d_ret, neighbours, bond_dirs, energy_offset, momentum_offset, absorb
):
    rank = lax.axis_index("energy").astype(jnp.int32).reshape(1)
    chips, held, count = plan.n_energy, plan.held, plan.all_energies
    lines = 2 * plan.classes
    modes = plan.devices * plan.modes
    message = jax.ShapeDtypeStruct((plan.message, LANES), BF16)

    def deal(blocks):
        return call(
            functools.partial(deal_kernel, plan), [message] * chips, rank, blocks,
            scalars=1, scratch=[pltpu.VMEM((plan.entries + plan.tail, LANES), F32)],
            moved=4 * blocks.size,
        )

    low_blocks = deal(g_less)
    own, g_great = lax.optimization_barrier((low_blocks[0], g_great))
    low_blocks = [own] + list(low_blocks[1:])
    low = to_chips(plan, low_blocks)
    high_blocks = deal(g_great)
    own, d_less, bond_dirs = lax.optimization_barrier((high_blocks[0], d_less, bond_dirs))
    high = to_chips(plan, [own] + list(high_blocks[1:]))
    low[0], low[1] = lax.optimization_barrier((low[0], low[1]))
    low_beside = [swap(block, "momentum", 1) for block in low]
    small = jax.ShapeDtypeStruct((plan.devices, 8, LANES), F32)
    coupling, table, pairs = call(
        functools.partial(couple_kernel, plan),
        [
            small,
            jax.ShapeDtypeStruct((4 * lines, plan.devices * 8), F32),
            jax.ShapeDtypeStruct((6, plan.bonds, plan.atoms), F32),
        ],
        d_less.transpose(0, 2, 3, 1, 4), bond_dirs.transpose(1, 0, 2),
        energy_offset.reshape(1, modes), momentum_offset.reshape(1, modes), absorb.reshape(1, modes),
        scratch=[pltpu.VMEM((-(-2 * plan.bonds * plan.modes // 16) * 16, plan.atoms), F32)],
        moved=4 * d_less.size,
    )
    coupling = lax.all_to_all(coupling, EVERY, 0, 0, tiled=True)
    low_scratch = pltpu.VMEM((4 * count, held, LANES), F32)
    half_scratch = pltpu.VMEM((2 * count, held, LANES), F32)
    polar = call(
        functools.partial(polar_kernel, plan), small, rank, table, *low, *low_beside, *high,
        scalars=1, scratch=[low_scratch, half_scratch], moved=8 * 2**20,
    )
    polar = lax.all_to_all(polar, EVERY, 0, 0, tiled=True)
    sums = call(
        functools.partial(energy_kernel, plan), [message] * chips,
        rank, table, coupling, *low, *low_beside,
        scalars=1, scratch=[
            low_scratch,
            half_scratch,
            pltpu.VMEM((4 * lines, LANES), F32),
            pltpu.VMEM((2, 4 * lines, LANES), F32),
        ],
        moved=8 * 2**20,
    )
    sums = to_chips(plan, sums)
    padded = -(-plan.bonds // 8) * 8
    d_next = call(
        functools.partial(next_kernel, plan), jax.ShapeDtypeStruct(d_ret.shape, BF16),
        polar, d_ret, neighbours, pairs,
        out_space=pltpu.HBM,
        scratch=[
            pltpu.VMEM((12 * plan.modes, padded, plan.atoms), F32),
            pltpu.VMEM((plan.modes, 2 * plan.order, 2 * plan.order), BF16),
            pltpu.VMEM(d_ret.shape, BF16),
            pltpu.SemaphoreType.DMA((plan.modes, 2)),
        ],
        moved=20 * 2**20,
    )
    d_next, own = lax.optimization_barrier((d_next, sums[0]))
    self_energy = call(
        functools.partial(gather_kernel, plan), jax.ShapeDtypeStruct(g_less.shape, BF16), rank,
        own, *sums[1:],
        scalars=1, out_space=pltpu.HBM, moved=4 * 2**20,
        scratch=[
            pltpu.VMEM((plan.slabs, chips, plan.rest_pad, LANES), F32),
            pltpu.VMEM(g_less.shape, BF16),
            pltpu.SemaphoreType.DMA((plan.slabs,)),
        ],
    )
    return self_energy, d_next


def local(*arrays):
    plan = Plan(
        arrays[0].shape, arrays[2].shape, arrays[3].shape,
        lax.axis_size("energy"), lax.axis_size("momentum"), lax.axis_size("phonon"),
    )
    return dealt(plan, *arrays) if plan.fits() else general(*arrays)


def solution(mesh):
    in_specs = (
        P("energy", "momentum", None, None, "phonon"),
        P("energy", "momentum", None, None, "phonon"),
        P(("energy", "momentum", "phonon"), None, None, None, None),
        P(("energy", "momentum", "phonon"), None, None, None),
        P(),
        P(),
        P(),
        P(),
        P(),
    )
    out_specs = (
        P("energy", "momentum", None, None, "phonon"),
        P(("energy", "momentum", "phonon"), None, None, None),
    )
    return jax.shard_map(local, mesh=mesh, in_specs=in_specs, out_specs=out_specs, check_vma=False)
```

```python
import functools

import jax
import jax.numpy as jnp
from jax import lax
from jax.experimental import pallas as pl
from jax.experimental.pallas import tpu as pltpu
from jax.sharding import PartitionSpec as P

ORB = 12
REACH = 4
LANES = 128


HIGH = lax.Precision.HIGHEST


def shifted_2(block, axis, distance):
    devices = range(lax.axis_size(axis))
    route = [(i - distance, i) for i in devices if i - distance in devices]
    return lax.ppermute(block, axis, route)


def scaled_blocks(weights, blocks):
    real_w = weights[None, :, :, 0, None, :]
    imag_w = weights[None, :, :, 1, None, :]
    real_b = blocks[:, None, :, 0].astype(jnp.float32)
    imag_b = blocks[:, None, :, 1].astype(jnp.float32)
    real_part = jnp.sum(real_w * real_b - imag_w * imag_b, axis=2)
    imag_part = jnp.sum(real_w * imag_b + imag_w * real_b, axis=2)
    return jnp.stack([real_part, imag_part], axis=2)


def inner_sums(local_blocks, shifted):
    local_real = local_blocks[:, :, 0].astype(jnp.float32)[:, :, None]
    local_imag = local_blocks[:, :, 1].astype(jnp.float32)[:, :, None]
    other_real = shifted[:, :, 0].astype(jnp.float32)[:, None]
    other_imag = shifted[:, :, 1].astype(jnp.float32)[:, None]
    real_sum = jnp.sum(local_real * other_real + local_imag * other_imag, axis=(0, 3))
    imag_sum = jnp.sum(local_imag * other_real - local_real * other_imag, axis=(0, 3))
    return jnp.stack([real_sum, imag_sum], axis=2)


def times_adjoint(left, right):
    return jnp.einsum("mab,mcb->mac", left, right, preferred_element_type=jnp.float32)


def times_plain(left, right):
    return jnp.einsum("mab,mbc->mac", left, right, preferred_element_type=jnp.float32)


def general(
    g_less, g_great, d_less, d_ret, neighbours, bond_dirs, energy_offset, momentum_offset, absorb
):
    energies = g_less.shape[0]
    momenta_here = g_less.shape[1]
    local_width = g_less.shape[4]
    bonds = d_less.shape[3]
    whole_atoms = d_less.shape[4]
    atom_share = local_width // bonds
    all_momenta = momenta_here * lax.axis_size("momentum")
    all_energies = energies * lax.axis_size("energy")
    modes_here = d_less.shape[0]
    order = d_ret.shape[2]
    classes = REACH * all_momenta
    energy_rank = lax.axis_index("energy")
    momentum_rank = lax.axis_index("momentum")
    phonon_rank = lax.axis_index("phonon")
    span = -(-REACH // energies)
    lower_steps = list(range(span, 0, -1))
    both_steps = lower_steps + list(range(-1, -span - 1, -1))
    label = (energy_offset - 1) * all_momenta + momentum_offset
    table = (label[:, None] == jnp.arange(classes, dtype=jnp.int32)[None, :]).astype(jnp.float32)
    soaked = table * absorb[:, None]
    pair_cube = bond_dirs[:, None] * bond_dirs[None, :]
    pair = pair_cube.reshape((9,) + bond_dirs.shape[1:])
    coupling = jnp.sum(d_less * pair[None, None], axis=2)
    first_mode = (
        (energy_rank * lax.axis_size("momentum") + momentum_rank) * lax.axis_size("phonon")
        + phonon_rank
    ) * modes_here
    own_table = lax.dynamic_slice_in_dim(table, first_mode, modes_here, 0)
    spread = lax.all_to_all(
        coupling.astype(jnp.bfloat16), "phonon", split_axis=3, concat_axis=0, tiled=True
    ).astype(coupling.dtype)
    blank = jnp.zeros((classes, 2 * bonds * atom_share), jnp.float32)
    piece = lax.all_gather(
        spread.astype(jnp.bfloat16), ("energy", "momentum"), axis=0, tiled=True
    ).astype(jnp.float32)
    rows = piece.shape[0]
    flat_piece = piece.reshape(rows, -1)
    emitted = blank + jnp.einsum("mc,mx->cx", table, flat_piece, precision=HIGH)
    absorbed = blank + jnp.einsum("mc,mx->cx", soaked, flat_piece, precision=HIGH)
    emitted = emitted.reshape(classes, 2, bonds, atom_share)
    absorbed = absorbed.reshape(classes, 2, bonds, atom_share)
    emit_table = emitted.transpose(0, 1, 3, 2).reshape(REACH, all_momenta, 2, local_width)
    soak_table = absorbed.transpose(0, 1, 3, 2).reshape(REACH, all_momenta, 2, local_width)
    moved = [shifted_2(g_less, "energy", step) for step in both_steps]
    lower = jnp.concatenate(moved[:span], axis=0)
    upper = jnp.concatenate(moved[span:], axis=0)
    lesser_rimmed = jnp.concatenate([lower, g_less, upper], axis=0)
    greater_moved = [shifted_2(g_great, "energy", step) for step in lower_steps]
    greater_rim = jnp.concatenate(greater_moved, axis=0)
    greater_rimmed = jnp.concatenate([greater_rim, g_great], axis=0)
    lesser_wide, greater_wide = (
        lax.all_gather(lesser_rimmed, "momentum", axis=1, tiled=True),
        lax.all_gather(greater_rimmed, "momentum", axis=1, tiled=True),
    )
    here_moment = momentum_rank * momenta_here + jnp.arange(momenta_here, dtype=jnp.int32)
    every_moment = jnp.arange(all_momenta, dtype=jnp.int32)
    behind = (here_moment[:, None] - every_moment[None, :]) % all_momenta
    ahead = (every_moment[None, :] - here_moment[:, None]) % all_momenta
    pick_behind = (behind[:, :, None] == every_moment[None, None, :]).astype(jnp.float32)
    pick_ahead = (ahead[:, :, None] == every_moment[None, None, :]).astype(jnp.float32)
    total = jnp.zeros(g_less.shape, jnp.float32)
    polar_parts = []
    for energy_step in range(1, REACH + 1):
        below = lesser_wide[REACH - energy_step : REACH - energy_step + energies]
        above = lesser_wide[REACH + energy_step : REACH + energy_step + energies]
        weight_below = jnp.einsum(
            "lkq,qzx->lkzx", pick_behind, emit_table[energy_step - 1], precision=HIGH
        )
        weight_above = jnp.einsum(
            "lkq,qzx->lkzx", pick_ahead, soak_table[energy_step - 1], precision=HIGH
        )
        total = total + scaled_blocks(weight_below, below) + scaled_blocks(weight_above, above)
        earlier = greater_wide[REACH - energy_step : REACH - energy_step + energies]
        pairs = inner_sums(g_less, earlier)
        polar_parts.append(jnp.einsum("lkq,lkzx->qzx", pick_behind, pairs, precision=HIGH))
    self_energy = total.astype(jnp.bfloat16)
    scale = float(all_energies * all_momenta * ORB * ORB) ** (-0.5)
    polar_local = jnp.stack(polar_parts).reshape(classes, 2, local_width) * scale
    polar_summed = lax.psum(polar_local, ("energy", "momentum"))
    polar_full = lax.all_gather(polar_summed, "phonon", axis=2, tiled=True)
    own_polar = jnp.einsum("mc,czx->mzx", own_table, polar_full, precision=HIGH)
    own_polar = own_polar.reshape(modes_here, 2, whole_atoms, bonds).transpose(0, 1, 3, 2)
    link = (
        neighbours[:, :, None] == jnp.arange(whole_atoms, dtype=jnp.int32)[None, None, :]
    ).astype(jnp.float32)
    weighted = pair_cube[None, None] * own_polar[:, :, None, None]
    dense = jnp.einsum("mzijna,nab->mziajb", weighted, link, precision=HIGH)
    dense = dense.reshape(modes_here, 2, order, order).astype(jnp.bfloat16)
    dense_re, dense_im = (dense[:, 0], dense[:, 1])
    ret_re, ret_im = (d_ret[:, 0], d_ret[:, 1])
    half_re = (times_adjoint(dense_re, ret_re) + times_adjoint(dense_im, ret_im)).astype(
        jnp.bfloat16
    )
    half_im = (times_adjoint(dense_im, ret_re) - times_adjoint(dense_re, ret_im)).astype(
        jnp.bfloat16
    )
    next_re = times_plain(ret_re, half_re) - times_plain(ret_im, half_im)
    next_im = times_plain(ret_re, half_im) + times_plain(ret_im, half_re)
    d_next = jnp.stack([next_re, next_im], axis=1).astype(jnp.bfloat16)
    return (self_energy, d_next)


EVERY = ("energy", "momentum", "phonon")
F32 = jnp.float32
BF16 = jnp.bfloat16


class Plan:
    def __init__(self, g_shape, d_shape, ret_shape, n_energy, n_momentum, n_phonon):
        self.energies, self.momenta, _, self.entries, self.width = g_shape
        self.modes, _, _, self.bonds, self.atoms = d_shape
        self.order = ret_shape[2]
        self.n_energy = n_energy
        self.n_momentum = n_momentum
        self.n_phonon = n_phonon
        self.devices = n_energy * n_momentum * n_phonon
        self.all_energies = self.energies * n_energy
        self.all_momenta = self.momenta * n_momentum
        self.classes = REACH * self.all_momenta
        self.slabs = 2 * self.energies
        self.tiles = self.width // LANES
        self.rest = self.width % LANES
        self.rest_rows = self.entries // n_energy
        self.main_rows = self.slabs * self.entries
        self.rest_pad = -(-self.rest_rows // 8) * 8
        self.message = -(-(self.main_rows + self.rest_pad) // 16) * 16
        self.tail = self.message - self.main_rows
        self.held = self.entries + self.rest_pad
        self.columns = self.width * n_phonon

    def fits(self):
        return (
            self.momenta == 1
            and self.all_momenta == 2
            and self.n_energy == self.tiles
            and self.n_energy & (self.n_energy - 1) == 0
            and self.entries % 16 == 0
            and self.entries % self.n_energy == 0
            and self.rest > 0
            and self.slabs * self.rest == LANES
            and self.modes <= 2
            and self.atoms == LANES
            and self.order == 3 * self.atoms
            and self.all_energies <= 8
        )


def call(kernel, out_shape, *operands, scratch=(), scalars=0, flops=0, moved=0, out_space=pltpu.VMEM):
    smem = pl.BlockSpec(memory_space=pltpu.SMEM)
    vmem = pl.BlockSpec(memory_space=pltpu.VMEM)
    specs = [smem] * scalars + [vmem] * (len(operands) - scalars)
    many = isinstance(out_shape, (list, tuple))
    return pl.pallas_call(
        kernel,
        out_shape=out_shape,
        in_specs=specs,
        out_specs=[vmem] * len(out_shape) if many else pl.BlockSpec(memory_space=out_space),
        scratch_shapes=list(scratch),
        compiler_params=pltpu.CompilerParams(vmem_limit_bytes=48 * 2**20),
        cost_estimate=pl.CostEstimate(flops=flops, bytes_accessed=moved, transcendentals=0),
    )(*operands)


def deal_kernel(plan, rank_ref, source_ref, *refs):
    outs, rest_ref = refs[: plan.n_energy], refs[plan.n_energy]
    rank = rank_ref[0]
    slabs = [(e, z) for e in range(plan.energies) for z in range(2)]
    pieces = [source_ref[e, 0, z, :, plan.tiles * LANES :].astype(F32) for e, z in slabs]
    rest_ref[: plan.entries] = jnp.concatenate(pieces, axis=1)
    rest_ref[plan.entries :] = jnp.zeros((plan.tail, LANES), F32)
    for partner in range(plan.n_energy):
        target = rank ^ partner
        lanes = pl.ds(pl.multiple_of(target * LANES, LANES), LANES)
        for slab, (e, z) in enumerate(slabs):
            rows = slice(slab * plan.entries, (slab + 1) * plan.entries)
            outs[partner][rows] = source_ref[e, 0, z, :, lanes]
        rest = rest_ref[pl.ds(target * plan.rest_rows, plan.tail), :]
        outs[partner][plan.main_rows :] = rest.astype(BF16)


def bond_of(plan, shape):
    column = lax.broadcasted_iota(jnp.int32, shape, len(shape) - 1)
    atom = jnp.floor((column.astype(F32) + 0.5) * (1.0 / plan.bonds)).astype(jnp.int32)
    return column - atom * plan.bonds


def atom_table(plan):
    atom = lax.broadcasted_iota(jnp.int32, (plan.atoms, plan.columns), 0)
    column = lax.broadcasted_iota(jnp.int32, (plan.atoms, plan.columns), 1)
    inside = column - atom * plan.bonds
    return jnp.where((inside >= 0) & (inside < plan.bonds), 1.0, 0.0).astype(BF16)


def mode_table(plan, energy_ref, momentum_ref, absorb_ref):
    width = plan.devices * 8
    modes = plan.devices * plan.modes
    label = (energy_ref[...] - 1) * plan.all_momenta + momentum_ref[...]
    stacked = jnp.concatenate(
        [label.astype(F32), absorb_ref[...], jnp.zeros((6, modes), F32)], axis=0
    )
    mode = lax.broadcasted_iota(jnp.int32, (modes, width), 0)
    column = lax.broadcasted_iota(jnp.int32, (modes, width), 1)
    inner = (column & 3) >> 1
    chosen = (mode == (column >> 3) * plan.modes + inner) & (inner < plan.modes)
    spread = jnp.dot(
        stacked, jnp.where(chosen, 1.0, 0.0), precision=HIGH, preferred_element_type=F32
    )
    label = (spread[:1] + 0.5).astype(jnp.int32)
    column = lax.broadcasted_iota(jnp.int32, (2 * plan.classes, width), 1)
    row = lax.broadcasted_iota(jnp.int32, (2 * plan.classes, width), 0)
    hit = (label == (row >> 1)) & ((column & 1) == (row & 1))
    hit = hit & (((column & 3) >> 1) < plan.modes)
    blocks = []
    for kind in range(2):
        here = hit & (((column >> 2) & 1) == kind)
        blocks.append(jnp.where(here, 1.0, 0.0))
        blocks.append(jnp.where(here, spread[1:2], 0.0))
    return jnp.concatenate(blocks, axis=0)


def couple_kernel(
    plan, less_ref, dirs_ref, energy_ref, momentum_ref, absorb_ref,
    out_ref, table_ref, pair_ref, held_ref,
):
    bonds, width = plan.bonds, plan.width
    held_ref[...] = jnp.zeros(held_ref.shape, F32)
    for n in range(bonds):
        pairs = [dirs_ref[n, i : i + 1] * dirs_ref[n, j : j + 1] for i in range(3) for j in range(3)]
        for way, (i, j) in enumerate((i, j) for i in range(3) for j in range(i, 3)):
            pair_ref[way, n : n + 1] = pairs[3 * i + j]
        for m in range(plan.modes):
            total = less_ref[m, 0, n] * pairs[0]
            for t in range(1, 9):
                total = total + less_ref[m, t, n] * pairs[t]
            row = (m * bonds + n) * 2
            held_ref[row : row + 2] = total
    rows = held_ref.shape[0]
    spread = jnp.dot(held_ref[...].astype(BF16), atom_table(plan), preferred_element_type=F32)
    row = lax.broadcasted_iota(jnp.int32, (rows, 1), 0)
    bond = (row >> 1) - jnp.where(row >= 2 * bonds, bonds, 0)
    keep = bond == bond_of(plan, (1, plan.columns))
    kept = jnp.where(keep, spread, 0.0).astype(BF16)
    line = lax.broadcasted_iota(jnp.int32, (8, rows), 0)
    row = lax.broadcasted_iota(jnp.int32, (8, rows), 1)
    owner = jnp.where(row >= 2 * bonds, 2, 0) + (row & 1)
    gather = jnp.where((line == owner) & (row < 2 * bonds * plan.modes), 1.0, 0.0).astype(BF16)
    flat = jnp.dot(gather, kept, preferred_element_type=F32)[:4]
    for p in range(plan.n_phonon):
        start = p * width
        rest = flat[:, start + plan.tiles * LANES : start + width]
        rest = jnp.concatenate([rest, jnp.zeros((4, LANES - plan.rest), F32)], axis=1)
        for tile in range(plan.tiles):
            main = flat[:, start + tile * LANES : start + (tile + 1) * LANES]
            block = jnp.concatenate([main, rest], axis=0)
            for half in range(plan.n_momentum):
                out_ref[(tile * plan.n_momentum + half) * plan.n_phonon + p] = block
    table_ref[...] = mode_table(plan, energy_ref, momentum_ref, absorb_ref)


def stage_blocks(plan, rank, messages, held_ref, stride, offset):
    row = lax.broadcasted_iota(jnp.int32, (plan.rest_pad, LANES), 0)
    for partner, message in enumerate(messages):
        first = plan.energies * (rank ^ partner)
        tail = message[plan.main_rows :].astype(F32)[: plan.rest_pad]
        tail = jnp.where(row < plan.rest_rows, tail, 0.0)
        for e in range(plan.energies):
            for z in range(2):
                slab = 2 * e + z
                place = ((first + e) * stride + offset) * 2 + z
                rows = slice(slab * plan.entries, (slab + 1) * plan.entries)
                held_ref[place, : plan.entries] = message[rows].astype(F32)
                turned = tail if slab == 0 else pltpu.roll(tail, LANES - slab * plan.rest, 1)
                held_ref[place, plan.entries :] = turned


def polar_kernel(plan, rank_ref, table_ref, *refs):
    chips = plan.n_energy
    out_ref, low_ref, high_ref = refs[3 * chips :]
    rank = rank_ref[0]
    stage_blocks(plan, rank, refs[:chips], low_ref, 2, 0)
    stage_blocks(plan, rank, refs[chips : 2 * chips], low_ref, 2, 1)
    stage_blocks(plan, rank, refs[2 * chips : 3 * chips], high_ref, 1, 0)
    count = plan.all_energies

    def step(chunk, sums):
        rows = pl.ds(pl.multiple_of(chunk * 8, 8), 8)
        sums = list(sums)
        both = [low_ref[2 * at, rows] + low_ref[2 * at + 1, rows] for at in range(2 * count)]
        for energy in range(count - 1):
            high_re, high_im = high_ref[2 * energy, rows], high_ref[2 * energy + 1, rows]
            high_sum, high_dif = high_re + high_im, high_re - high_im
            for energy_step in range(1, min(REACH, count - 1 - energy) + 1):
                for q in range(2):
                    index = ((energy_step - 1) * 2 + q) * 3
                    at = (energy + energy_step) * 2 + q
                    sums[index] = sums[index] + both[at] * high_re
                    sums[index + 1] = sums[index + 1] + low_ref[2 * at + 1, rows] * high_dif
                    sums[index + 2] = sums[index + 2] + low_ref[2 * at, rows] * high_sum
        return tuple(sums)

    none = tuple(jnp.zeros((8, LANES), F32) for _ in range(3 * plan.classes))

    def joined(sums):
        parts = []
        for index in range(0, 3 * plan.classes, 3):
            parts += [sums[index] - sums[index + 1], sums[index] - sums[index + 2]]
        return parts

    main = joined(lax.fori_loop(0, plan.entries // 8, step, none, unroll=3))
    rest = joined(lax.fori_loop(plan.entries // 8, plan.held // 8, step, none, unroll=5))
    scale = float(count * 2 * plan.entries) ** (-0.5)
    lines = [jnp.sum(part, axis=0, keepdims=True) * scale for part in main + rest]
    sums = jnp.concatenate(lines, axis=0)
    lines = 2 * plan.classes
    picks = jnp.concatenate([table_ref[:lines], table_ref[2 * lines : 3 * lines]], axis=0)
    picked = lax.dot_general(
        picks, sums, (((0,), (0,)), ((), ())), precision=HIGH, preferred_element_type=F32
    )
    out_ref[...] = picked.reshape(out_ref.shape)


def energy_kernel(plan, rank_ref, table_ref, coupling_ref, *refs):
    chips = plan.n_energy
    outs = refs[2 * chips : 3 * chips]
    low_ref, sum_ref, weight_ref, mixed_ref = refs[3 * chips :]
    rank = rank_ref[0]
    flat = coupling_ref[...].reshape(plan.devices * 8, LANES)
    weights = jnp.dot(table_ref[...], flat, precision=HIGH, preferred_element_type=F32)
    following = pltpu.roll(weights, weights.shape[0] - 1, 0)
    weight_ref[...] = weights
    mixed_ref[0] = weights + following
    mixed_ref[1] = following - weights
    stage_blocks(plan, rank, refs[:chips], low_ref, 2, 0)
    stage_blocks(plan, rank, refs[chips : 2 * chips], low_ref, 2, 1)
    count = plan.all_energies

    def run(base):
        def step(chunk, carry):
            rows = pl.ds(pl.multiple_of(chunk * 8, 8), 8)
            both = [low_ref[2 * at, rows] + low_ref[2 * at + 1, rows] for at in range(2 * count)]
            parts = [[None] * count for _ in range(3)]
            for energy_step in range(1, REACH + 1):
                for q in range(2):
                    index = base + ((energy_step - 1) * 2 + q) * 2
                    for kind, sign in ((0, -1), (1, 1)):
                        at = index + kind * 2 * plan.classes
                        w_re = jnp.broadcast_to(weight_ref[at : at + 1], (8, LANES))
                        w_sum = jnp.broadcast_to(mixed_ref[0, at : at + 1], (8, LANES))
                        w_dif = jnp.broadcast_to(mixed_ref[1, at : at + 1], (8, LANES))
                        for energy in range(count):
                            other = energy + sign * energy_step
                            if other < 0 or other >= count:
                                continue
                            at = other * 2 + q
                            terms = (
                                w_re * both[at],
                                w_sum * low_ref[2 * at + 1, rows],
                                w_dif * low_ref[2 * at, rows],
                            )
                            for part, term in zip(parts, terms):
                                part[energy] = term if part[energy] is None else part[energy] + term
            for energy in range(count):
                sum_ref[2 * energy, rows] = parts[0][energy] - parts[1][energy]
                sum_ref[2 * energy + 1, rows] = parts[0][energy] + parts[2][energy]
            return carry

        return step

    lax.fori_loop(0, plan.entries // 8, run(0), 0, unroll=2)
    lax.fori_loop(plan.entries // 8, plan.held // 8, run(4 * plan.classes), 0, unroll=5)
    lane = lax.broadcasted_iota(jnp.int32, (plan.rest_pad, LANES), 1)
    for partner in range(chips):
        first = plan.energies * (rank ^ partner)
        tail = jnp.zeros((plan.rest_pad, LANES), F32)
        for slab in range(plan.slabs):
            place = 2 * first + slab
            rows = slice(slab * plan.entries, (slab + 1) * plan.entries)
            outs[partner][rows] = sum_ref[place, : plan.entries].astype(BF16)
            piece = sum_ref[place, plan.entries :]
            if slab:
                piece = pltpu.roll(piece, slab * plan.rest, 1)
            mine = (lane >= slab * plan.rest) & (lane < (slab + 1) * plan.rest)
            tail = jnp.where(mine, piece, tail)
        if plan.tail > plan.rest_pad:
            blank = jnp.zeros((plan.tail - plan.rest_pad, LANES), F32)
            tail = jnp.concatenate([tail, blank], axis=0)
        outs[partner][plan.main_rows :] = tail.astype(BF16)


def gather_kernel(plan, rank_ref, *refs):
    chips = plan.n_energy
    out_ref, rest_ref, held_ref, sems = refs[chips:]
    rank = rank_ref[0]
    copies = []
    for slab in range(plan.slabs):
        place = (slab // 2, 0, slab % 2)
        for partner, message in enumerate(refs[:chips]):
            source = rank ^ partner
            lanes = pl.ds(pl.multiple_of(source * LANES, LANES), LANES)
            tail = message[plan.main_rows :].astype(F32)[: plan.rest_pad]
            rows = slice(slab * plan.entries, (slab + 1) * plan.entries)
            held_ref[slab // 2, 0, slab % 2, :, lanes] = message[rows]
            turned = tail if slab == 0 else pltpu.roll(tail, LANES - slab * plan.rest, 1)
            rest_ref[slab, source] = turned
        parts = [rest_ref[slab, source, : plan.rest_rows] for source in range(chips)]
        rest = jnp.concatenate(parts, axis=0)[:, : plan.rest]
        held_ref[slab // 2, 0, slab % 2, :, plan.tiles * LANES :] = rest.astype(BF16)
        copies.append(pltpu.make_async_copy(held_ref.at[place], out_ref.at[place], sems.at[slab]))
        copies[-1].start()
    for copy in copies:
        copy.wait()


def next_kernel(
    plan, polar_ref, ret_ref, near_ref, pair_ref, out_ref, v_ref, dense_ref, after_ref, sems
):
    bonds, atoms, order = plan.bonds, plan.atoms, plan.order
    padded = -(-bonds // 8) * 8
    lines = []
    for p in range(plan.n_phonon):
        rest = jnp.zeros((4, LANES), F32)
        for tile in range(plan.tiles):
            main = jnp.zeros((4, LANES), F32)
            for half in range(plan.n_momentum):
                block = polar_ref[(tile * plan.n_momentum + half) * plan.n_phonon + p]
                main = main + block[:4]
                rest = rest + block[4:]
            lines.append(main)
        lines.append(rest[:, : plan.rest])
    flat = jnp.concatenate(lines, axis=1)
    bond = lax.broadcasted_iota(jnp.int32, (padded, 1), 0)
    keep = bond == bond_of(plan, (1, plan.columns))
    tall = jnp.concatenate(
        [jnp.where(keep, flat[row : row + 1], 0.0) for row in range(2 * plan.modes)], axis=0
    )
    upper = tall.astype(BF16)
    lower = (tall - upper.astype(F32)).astype(BF16)
    contract = (((1,), (1,)), ((), ()))
    both = lax.dot_general(
        jnp.concatenate([upper, lower], axis=0), atom_table(plan), contract, preferred_element_type=F32
    )
    by_bond = both[: tall.shape[0]] + both[tall.shape[0] :]
    ways = [(i, j) for i in range(3) for j in range(i, 3)]
    near = near_ref[...]
    for row in range(2 * plan.modes):
        values = by_bond[row * padded : row * padded + bonds]
        values = [values * pair_ref[way] for way in range(len(ways))]
        sums = [jnp.zeros((bonds, atoms), F32) for _ in ways]
        for n in range(bonds):
            same = near == near[n : n + 1]
            for way in range(len(ways)):
                sums[way] = sums[way] + jnp.where(same, values[way][n : n + 1], 0.0)
        for way in range(len(ways)):
            v_ref[row * len(ways) + way, :bonds] = sums[way]

    near = near.astype(BF16)

    def build(m, first):
        number = (lax.broadcasted_iota(jnp.int32, (16, atoms), 0) + first).astype(BF16)
        for z in range(2):
            row = 2 * m + z
            blocks = [jnp.zeros((16, atoms), BF16) for _ in ways]
            for n in range(bonds):
                hit = number == near[n : n + 1]
                for way in range(len(ways)):
                    value = v_ref[row * len(ways) + way, n : n + 1].astype(BF16)
                    blocks[way] = jnp.where(hit, value, blocks[way])
            for way, (i, j) in enumerate(ways):
                block = blocks[way]
                other = block if z else -block
                for up, left in sorted({(j, i), (i, j)}):
                    place = pl.ds(pl.multiple_of(up * atoms + first, 16), 16)
                    dense_ref[m, place, pl.ds(z * order + left * atoms, atoms)] = block
                    place = pl.ds(pl.multiple_of(order + up * atoms + first, 16), 16)
                    dense_ref[m, place, pl.ds((1 - z) * order + left * atoms, atoms)] = other

    for m in range(plan.modes):
        for chunk in range(atoms // 16):
            build(m, chunk * 16)
    copies = []
    for m in range(plan.modes):
        ret = jnp.concatenate([ret_ref[m, 0], ret_ref[m, 1]], axis=1)
        half = jnp.dot(ret, dense_ref[m], preferred_element_type=F32).astype(BF16)
        half_re, half_im = half[:, :order], half[:, order:]
        for z, parts in enumerate(([half_re, -half_im], [half_im, half_re])):
            right = jnp.concatenate(parts, axis=1)
            after = lax.dot_general(ret, right, contract, preferred_element_type=F32)
            after_ref[m, z] = after.astype(BF16)
            copy = pltpu.make_async_copy(after_ref.at[m, z], out_ref.at[m, z], sems.at[m, z])
            copy.start()
            copies.append(copy)
    for copy in copies:
        copy.wait()


def swap(block, axis, distance):
    return lax.ppermute(block, axis, [(i, i ^ distance) for i in range(lax.axis_size(axis))])


def to_chips(plan, blocks):
    return [blocks[0]] + [swap(blocks[k], "energy", k) for k in range(1, plan.n_energy)]


def dealt(
    plan, g_less, g_great, d_less, d_ret, neighbours, bond_dirs, energy_offset, momentum_offset, absorb
):
    rank = lax.axis_index("energy").astype(jnp.int32).reshape(1)
    chips, held, count = plan.n_energy, plan.held, plan.all_energies
    lines = 2 * plan.classes
    modes = plan.devices * plan.modes
    message = jax.ShapeDtypeStruct((plan.message, LANES), BF16)

    def deal(blocks):
        return call(
            functools.partial(deal_kernel, plan), [message] * chips, rank, blocks,
            scalars=1, scratch=[pltpu.VMEM((plan.entries + plan.tail, LANES), F32)],
            moved=4 * blocks.size,
        )

    low_blocks = deal(g_less)
    own, g_great = lax.optimization_barrier((low_blocks[0], g_great))
    low_blocks = [own] + list(low_blocks[1:])
    low = to_chips(plan, low_blocks)
    high_blocks = deal(g_great)
    own, d_less, bond_dirs = lax.optimization_barrier((high_blocks[0], d_less, bond_dirs))
    high = to_chips(plan, [own] + list(high_blocks[1:]))
    low[0], low[1] = lax.optimization_barrier((low[0], low[1]))
    low_beside = [swap(block, "momentum", 1) for block in low]
    small = jax.ShapeDtypeStruct((plan.devices, 8, LANES), F32)
    coupling, table, pairs = call(
        functools.partial(couple_kernel, plan),
        [
            small,
            jax.ShapeDtypeStruct((4 * lines, plan.devices * 8), F32),
            jax.ShapeDtypeStruct((6, plan.bonds, plan.atoms), F32),
        ],
        d_less.transpose(0, 2, 3, 1, 4), bond_dirs.transpose(1, 0, 2),
        energy_offset.reshape(1, modes), momentum_offset.reshape(1, modes), absorb.reshape(1, modes),
        scratch=[pltpu.VMEM((-(-2 * plan.bonds * plan.modes // 16) * 16, plan.atoms), F32)],
        moved=4 * d_less.size,
    )
    coupling = lax.all_to_all(coupling, EVERY, 0, 0, tiled=True)
    low_scratch = pltpu.VMEM((4 * count, held, LANES), F32)
    half_scratch = pltpu.VMEM((2 * count, held, LANES), F32)
    polar = call(
        functools.partial(polar_kernel, plan), small, rank, table, *low, *low_beside, *high,
        scalars=1, scratch=[low_scratch, half_scratch], moved=8 * 2**20,
    )
    polar = lax.all_to_all(polar, EVERY, 0, 0, tiled=True)
    sums = call(
        functools.partial(energy_kernel, plan), [message] * chips,
        rank, table, coupling, *low, *low_beside,
        scalars=1, scratch=[
            low_scratch,
            half_scratch,
            pltpu.VMEM((4 * lines, LANES), F32),
            pltpu.VMEM((2, 4 * lines, LANES), F32),
        ],
        moved=8 * 2**20,
    )
    sums = to_chips(plan, sums)
    padded = -(-plan.bonds // 8) * 8
    d_next = call(
        functools.partial(next_kernel, plan), jax.ShapeDtypeStruct(d_ret.shape, BF16),
        polar, d_ret, neighbours, pairs,
        out_space=pltpu.HBM,
        scratch=[
            pltpu.VMEM((12 * plan.modes, padded, plan.atoms), F32),
            pltpu.VMEM((plan.modes, 2 * plan.order, 2 * plan.order), BF16),
            pltpu.VMEM(d_ret.shape, BF16),
            pltpu.SemaphoreType.DMA((plan.modes, 2)),
        ],
        moved=20 * 2**20,
    )
    d_next, own = lax.optimization_barrier((d_next, sums[0]))
    self_energy = call(
        functools.partial(gather_kernel, plan), jax.ShapeDtypeStruct(g_less.shape, BF16), rank,
        own, *sums[1:],
        scalars=1, out_space=pltpu.HBM, moved=4 * 2**20,
        scratch=[
            pltpu.VMEM((plan.slabs, chips, plan.rest_pad, LANES), F32),
            pltpu.VMEM(g_less.shape, BF16),
            pltpu.SemaphoreType.DMA((plan.slabs,)),
        ],
    )
    return self_energy, d_next


def local(*arrays):
    plan = Plan(
        arrays[0].shape, arrays[2].shape, arrays[3].shape,
        lax.axis_size("energy"), lax.axis_size("momentum"), lax.axis_size("phonon"),
    )
    return dealt(plan, *arrays) if plan.fits() else general(*arrays)


def solution(mesh):
    in_specs = (
        P("energy", "momentum", None, None, "phonon"),
        P("energy", "momentum", None, None, "phonon"),
        P(("energy", "momentum", "phonon"), None, None, None, None),
        P(("energy", "momentum", "phonon"), None, None, None),
        P(),
        P(),
        P(),
        P(),
        P(),
    )
    out_specs = (
        P("energy", "momentum", None, None, "phonon"),
        P(("energy", "momentum", "phonon"), None, None, None),
    )
    return jax.shard_map(local, mesh=mesh, in_specs=in_specs, out_specs=out_specs, check_vma=False)
```
